32 devices in a mesh: clip: 8 (over y, x, core), head: 4 (over z).
Axes of the slice: x: 2, y: 2, z: 4, core: 2. Of those that a mesh axis runs over, the one named last changes fastest.
Arguments:
- latents: bfloat16 [8, 24, 64, 1280], P('clip', 'head'), may hold values from -6 to 6
- cotangent: bfloat16 [8, 24, 64, 1280], P('clip', 'head'), may hold values from -6 to 6
- frames: int32 [8], P('clip'), may hold values from 8 to 24, as said below
- timesteps: int32 [8], P('clip'), may hold values from 0 to 999
- text: bfloat16 [8, 77, 768], P('clip'), may hold values from -6 to 6
- conv_weight: bfloat16 [2, 9, 1280, 1280], P(None, None, 'head'), may hold values from -0.0546875 to 0.0546875
- time_weight: bfloat16 [1280, 1280], P('head'), may hold values from -0.15625 to 0.15625
- frozen_params: float32 [20, 1280], replicated, may hold values from 0.1 to 1.9
- spatial_square: bfloat16 [8, 1280, 1280], P(None, 'head'), as said below
- cross_kv: bfloat16 [2, 1280, 768], P(None, 'head'), may hold values from -0.21875 to 0.21875
- spatial_ffn: bfloat16 [3, 5120, 1280], P(None, 'head'), may hold values from -0.15625 to 0.15625
- geglu_bias: float32 [2, 5120], P(None, 'head'), may hold values from -1.75 to 1.75
- projections: float32 [10, 1280, 1280], P(None, 'head', 'clip'), as said below
- feedforward: float32 [2, 5120, 1280], P(None, 'head', 'clip'), may hold values from -0.15625 to 0.15625
- up_bias: float32 [40, 128], P('head', 'clip'), may hold values from -1.75 to 1.75
- vectors: float32 [13, 1280], P(None, 'clip'), may hold values from 0.1 to 1.9
- projections_moment: float32 [10, 1280, 1280], P(None, 'head', 'clip'), may hold values from -512 to 512
- feedforward_moment: float32 [2, 5120, 1280], P(None, 'head', 'clip'), may hold values from -512 to 512
- up_bias_moment: float32 [40, 128], P('head', 'clip'), may hold values from -512 to 512
- vectors_moment: float32 [13, 1280], P(None, 'clip'), may hold values from -512 to 512
- projections_average: float32 [10, 1280, 1280], P(None, 'head', 'clip'), may hold values from -0.15625 to 0.15625
- feedforward_average: float32 [2, 5120, 1280], P(None, 'head', 'clip'), may hold values from -0.15625 to 0.15625
- up_bias_average: float32 [40, 128], P('head', 'clip'), may hold values from -1.75 to 1.75
- vectors_average: float32 [13, 1280], P(None, 'clip'), may hold values from 0.1 to 1.9
Outputs:
- output: bfloat16 [8, 24, 64, 1280], P('clip', 'head')
- input_gradient: bfloat16 [8, 24, 64, 1280], P('clip', 'head')
- projections_moment_new: float32 [10, 1280, 1280], P(None, 'head', 'clip')
- projections_average_new: float32 [10, 1280, 1280], P(None, 'head', 'clip')
- projections_new: float32 [10, 1280, 1280], P(None, 'head', 'clip')
- feedforward_moment_new: float32 [2, 5120, 1280], P(None, 'head', 'clip')
- feedforward_average_new: float32 [2, 5120, 1280], P(None, 'head', 'clip')
- feedforward_new: float32 [2, 5120, 1280], P(None, 'head', 'clip')
- up_bias_moment_new: float32 [40, 128], P('head', 'clip')
- up_bias_average_new: float32 [40, 128], P('head', 'clip')
- up_bias_new: float32 [40, 128], P('head', 'clip')
- vectors_moment_new: float32 [13, 1280], P(None, 'clip')
- vectors_average_new: float32 [13, 1280], P(None, 'clip')
- vectors_new: float32 [13, 1280], P(None, 'clip')
The draws below stay inside these ranges and needn't reach their ends.
Inputs may be any that keep to these rules, and one draw needn't show every extreme that they name: Each clip has 8 to 24 frames; in every draw one clip has exactly 24 and one exactly 8. `projections`: entries are independent. `spatial_square`: entries are independent.
All inputs are finite; a program needn't handle non-finite values.
Results may differ from the reference program's by a relative error of at most 0.025.
Values may be sent and summed in bfloat16 or wider, within the bound.
A program may use at most 384 MiB of HBM per device.

```python
import math
import jax
import jax.numpy as jnp
from jax import lax

C = 1280
HD = 160
FF = 5120
GROUPS = 32
TEXT_DIM = 768
TEXT_LEN = 77
FMAX = 24
FMIN = 8
SIDE = 8
NV = 13
PIX = 64
TOTAL_CLIPS = 8


def draw_frames(key, part):
    key = jax.random.fold_in(key, 11)
    counts = jax.random.randint(jax.random.fold_in(key, 1), (TOTAL_CLIPS,), FMIN, FMAX + 1, jnp.int32)
    shuffled = jax.random.permutation(jax.random.fold_in(key, 2), TOTAL_CLIPS)
    counts = counts.at[shuffled[0]].set(FMAX)
    counts = counts.at[shuffled[1]].set(FMIN)
    return counts.astype(jnp.int32)


def draw_projections(key, part):
    key = jax.random.fold_in(key, 23)
    entries = jax.random.normal(key, (10, C, C), jnp.float32)
    scaling = jnp.array([1.0, 4.0, 1.0, 1.0, 1.0, 1.0, 4.0, 1.0, 1.0, 1.0], jnp.float32) * C ** (-0.5)
    return entries * scaling[:, None, None]


def draw_spatial_square(key, part):
    key = jax.random.fold_in(key, 37)
    entries = jax.random.normal(key, (8, C, C), jnp.float32)
    scaling = jnp.array([1.0, 1.0, 1.0, 1.0, 4.0, 1.0, 4.0, 1.0], jnp.float32) * C ** (-0.5)
    return (entries * scaling[:, None, None]).astype(jnp.bfloat16)


def place_ends(values, key, least, high):
    longest = values.shape.index(max(values.shape))
    spots = []
    for shift in (0, 1):
        where = [jax.random.randint(jax.random.fold_in(key, axis), (), 0, length) for axis, length in enumerate(values.shape)]
        where[longest] = (where[longest] + shift) % values.shape[longest]
        spots.append(tuple(where))
    return values.at[spots[0]].set(least).at[spots[1]].set(high)


def level_of(rng, dims, shards, least, high):
    loudness = 1.0
    for dim, parts in shards:
        steps = jax.random.uniform(jax.random.fold_in(jax.random.fold_in(rng, 6), dim), (parts,), jnp.float32, least / len(shards), high / len(shards))
        loudness = loudness * jnp.repeat(jnp.exp(steps), dims[dim] // parts).reshape((-1,) + (1,) * (len(dims) - 1 - dim))
    return loudness


def gaussian(key, shape, scale, limit, split=(), held_as=jnp.bfloat16):
    gain = level_of(key, shape, split, -0.22, 0.18) if split else 1.0
    values = jax.random.normal(key, shape, jnp.float32) * scale * gain
    return jnp.minimum(jnp.maximum(values, -limit), limit).astype(held_as)


def setup_inputs(seed: int = 0) -> dict:
    keys = jax.random.split(jax.random.key(seed), 25)
    latents = gaussian(keys[0], (TOTAL_CLIPS, FMAX, PIX, C), 1.0, 6.0, ((0, 8), (1, 4)))
    cotangent = gaussian(keys[1], (TOTAL_CLIPS, FMAX, PIX, C), 1.0, 6.0, ((0, 8), (1, 4)))
    frames = draw_frames(jax.random.fold_in(keys[24], 71), 0)
    timesteps = place_ends(jax.random.randint(keys[3], (TOTAL_CLIPS,), 0, 1000), jax.random.fold_in(keys[3], 1), 0, 999).astype(jnp.int32)
    text = gaussian(keys[4], (TOTAL_CLIPS, TEXT_LEN, TEXT_DIM), 1.0, 6.0, ((0, 8),))
    conv_weight = gaussian(keys[5], (2, 9, C, C), (9 * C) ** -0.5, 0.0546875, ((2, 4),))
    time_weight = gaussian(keys[6], (C, C), C ** -0.5, 0.15625, ((0, 4),))
    frozen_params = jnp.clip(1.0 + 0.18 * jax.random.normal(keys[7], (20, C), jnp.float32), 0.1, 1.9)
    spatial_square = draw_spatial_square(jax.random.fold_in(keys[24], 71), 0)
    cross_kv = gaussian(keys[9], (2, C, TEXT_DIM), TEXT_DIM ** -0.5, 0.21875, ((1, 4),))
    spatial_ffn = gaussian(keys[10], (3, FF, C), C ** -0.5, 0.15625, ((1, 4),))
    geglu_bias = gaussian(keys[11], (2, FF), 0.3, 1.75, ((1, 4),), jnp.float32)
    projections = draw_projections(jax.random.fold_in(keys[24], 71), 0)
    feedforward = gaussian(keys[13], (2, FF, C), C ** -0.5, 0.15625, ((1, 4), (2, 8)), jnp.float32)
    up_bias = gaussian(keys[14], (FF // 128, 128), 0.3, 1.75, ((0, 4), (1, 8)), jnp.float32)
    vectors = jnp.clip(1.0 + 0.18 * jax.random.normal(keys[15], (NV, C), jnp.float32), 0.1, 1.9)
    projections_moment = gaussian(keys[16], (10, C, C), ((TOTAL_CLIPS * (FMIN + FMAX) * PIX // 2) ** 0.5), 512.0, ((1, 4), (2, 8)), jnp.float32)
    feedforward_moment = gaussian(keys[17], (2, FF, C), ((TOTAL_CLIPS * (FMIN + FMAX) * PIX // 2) ** 0.5), 512.0, ((1, 4), (2, 8)), jnp.float32)
    up_bias_moment = gaussian(keys[18], (FF // 128, 128), ((TOTAL_CLIPS * (FMIN + FMAX) * PIX // 2) ** 0.5), 512.0, ((0, 4), (1, 8)), jnp.float32)
    vectors_moment = gaussian(keys[19], (NV, C), ((TOTAL_CLIPS * (FMIN + FMAX) * PIX // 2) ** 0.5), 512.0, ((1, 8),), jnp.float32)
    projections_average = gaussian(keys[20], (10, C, C), C ** -0.5, 0.15625, ((1, 4), (2, 8)), jnp.float32)
    feedforward_average = gaussian(keys[21], (2, FF, C), C ** -0.5, 0.15625, ((1, 4), (2, 8)), jnp.float32)
    up_bias_average = gaussian(keys[22], (FF // 128, 128), 0.3, 1.75, ((0, 4), (1, 8)), jnp.float32)
    vectors_average = jnp.clip(1.0 + 0.18 * jax.random.normal(keys[23], (NV, C), jnp.float32), 0.1, 1.9)
    return dict(latents=latents, cotangent=cotangent, frames=frames, timesteps=timesteps, text=text, conv_weight=conv_weight, time_weight=time_weight, frozen_params=frozen_params, spatial_square=spatial_square, cross_kv=cross_kv, spatial_ffn=spatial_ffn, geglu_bias=geglu_bias, projections=projections, feedforward=feedforward, up_bias=up_bias, vectors=vectors, projections_moment=projections_moment, feedforward_moment=feedforward_moment, up_bias_moment=up_bias_moment, vectors_moment=vectors_moment, projections_average=projections_average, feedforward_average=feedforward_average, up_bias_average=up_bias_average, vectors_average=vectors_average)


MOMENTUM = 0.9
RATE_MATRIX = 0.0002
RATE_VECTOR = 0.002
AVERAGE_DECAY = 0.7
GROUP_EPS = 1e-06
LAYER_EPS = 1e-05
MASK_FILL = -1e+30
HIGHEST = lax.Precision.HIGHEST

@jax.custom_vjp
def low(v):
    return lax.optimization_barrier(v.astype(jnp.bfloat16)).astype(jnp.float32)

@jax.custom_vjp
def low_back(v):
    return v

def low_keep(v):
    return (low(v), None)

def low_pass(kept, grad):
    return (grad,)

def back_keep(v):
    return (v, None)

def back_low(kept, grad):
    return (low(grad),)
low.defvjp(low_keep, low_pass)
low_back.defvjp(back_keep, back_low)

def group_norm(values, norm_gain, norm_shift):
    group_width = C // GROUPS
    in_shape = values.shape
    grouped = values.reshape(in_shape[:-1] + (in_shape[-1] // group_width, group_width))
    center = lax.optimization_barrier(jnp.mean(grouped, axis=(-3, -1), keepdims=True))
    centered = grouped - center
    variance = lax.optimization_barrier(jnp.mean(centered * centered, axis=(-3, -1), keepdims=True))
    scaled = (centered * lax.rsqrt(variance + GROUP_EPS)).reshape(in_shape)
    return scaled * norm_gain + norm_shift

def layer_norm(values, norm_gain, norm_shift):
    center = lax.optimization_barrier(jnp.mean(values, axis=-1, keepdims=True))
    centered = values - center
    variance = lax.optimization_barrier(jnp.mean(centered * centered, axis=-1, keepdims=True))
    return centered * lax.rsqrt(variance + LAYER_EPS) * norm_gain + norm_shift

def frame_table():
    frame_pos = jnp.arange(FMAX, dtype=jnp.float32)[:, None]
    channel = jnp.arange(C)
    frequency = jnp.exp((channel - channel % 2).astype(jnp.float32) * (-math.log(10000.0) / C))
    angles = frame_pos * frequency[None, :]
    return jnp.where(channel[None, :] % 2 == 0, jnp.sin(angles), jnp.cos(angles))

def time_table(timesteps):
    half_width = C // 2
    frequency = jnp.exp(jnp.arange(half_width, dtype=jnp.float32) * (-math.log(10000.0) / half_width))
    angles = timesteps.astype(jnp.float32)[:, None] * frequency[None, :]
    return jnp.concatenate([jnp.cos(angles), jnp.sin(angles)], axis=1)

def split_heads(values):
    return values.reshape(values.shape[:-1] + (values.shape[-1] // HD, HD))

def softmax_rows(scores):
    row_max = lax.optimization_barrier(jnp.max(scores, axis=-1, keepdims=True))
    weights = jnp.exp(scores - row_max)
    return weights / lax.optimization_barrier(jnp.sum(weights, axis=-1, keepdims=True))

def temporal_core(queries, keys_all, contents, present):
    in_shape = queries.shape
    scores = jnp.einsum('bfphd,bgphd->bphfg', split_heads(queries), split_heads(keys_all), precision=HIGHEST) * HD ** (-0.5)
    scores = jnp.where(present[:, None, None, None, :], scores, MASK_FILL)
    attention = jnp.einsum('bphfg,bgphd->bfphd', softmax_rows(scores), split_heads(contents), precision=HIGHEST)
    return attention.reshape(in_shape)

def spatial_core(queries, keys_all, contents):
    in_shape = queries.shape
    scores = jnp.einsum('bfphd,bfqhd->bfhpq', split_heads(queries), split_heads(keys_all), precision=HIGHEST) * HD ** (-0.5)
    attention = jnp.einsum('bfhpq,bfqhd->bfphd', softmax_rows(scores), split_heads(contents), precision=HIGHEST)
    return attention.reshape(in_shape)

def cross_core(queries, keys_all, contents):
    in_shape = queries.shape
    scores = jnp.einsum('bfphd,blhd->bfhpl', split_heads(queries), split_heads(keys_all), precision=HIGHEST) * HD ** (-0.5)
    attention = jnp.einsum('bfhpl,blhd->bfphd', softmax_rows(scores), split_heads(contents), precision=HIGHEST)
    return attention.reshape(in_shape)

def conv_grid(inputs, weight):
    leading = inputs.shape[:2]
    channels = inputs.shape[-1]
    as_grid = inputs.reshape(leading + (SIDE, SIDE, channels))
    padded = jnp.pad(as_grid, ((0, 0), (0, 0), (1, 1), (1, 1), (0, 0)))
    summed = jnp.zeros(leading + (SIDE, SIDE, weight.shape[-1]), jnp.float32)
    for offset in range(9):
        vertical = offset // 3
        horizontal = offset % 3
        window = padded[:, :, vertical:vertical + SIDE, horizontal:horizontal + SIDE, :]
        summed = summed + jnp.einsum('bfyxc,cd->bfyxd', window, weight[offset], precision=HIGHEST)
    return summed.reshape(leading + (PIX, weight.shape[-1]))

def project(values, weight):
    return jnp.einsum('bfpc,cd->bfpd', values, weight, precision=HIGHEST)

def project_back(values, weight):
    return jnp.einsum('bfpc,dc->bfpd', values, weight, precision=HIGHEST)

def gelu_tanh(values):
    return jax.nn.gelu(values, approximate=True)

def gelu_exact(values):
    return jax.nn.gelu(values, approximate=False)

def update(weight, moment, average, gradient, step_rate):
    moment_new = MOMENTUM * moment + gradient
    weight_new = weight - step_rate * (gradient + MOMENTUM * moment_new)
    average_new = AVERAGE_DECAY * average + (1.0 - AVERAGE_DECAY) * weight_new
    return (moment_new, average_new, weight_new)

def reference(latents, cotangent, frames, timesteps, text, conv_weight, time_weight, frozen_params, spatial_square, cross_kv, spatial_ffn, geglu_bias, projections, feedforward, up_bias, vectors, projections_moment, feedforward_moment, up_bias_moment, vectors_moment, projections_average, feedforward_average, up_bias_average, vectors_average):
    present = jnp.arange(FMAX)[None, :] < frames[:, None]
    conv_full = conv_weight.astype(jnp.float32)
    square_full = spatial_square.astype(jnp.float32)
    cross_full = cross_kv.astype(jnp.float32)
    sffn_full = spatial_ffn.astype(jnp.float32)
    frozen = frozen_params
    time_in = low(jax.nn.silu(time_table(timesteps)))
    time_bias = jnp.dot(time_in, time_weight.astype(jnp.float32), precision=HIGHEST)
    text_full = text.astype(jnp.float32)
    frame_codes = frame_table()[None, :, None, :]

    def clip_forward(weights, clip_in, clip_time, clip_text, clip_present):
        square_w, ffn_w, bias_w, vector_w = weights
        inputs = clip_in[None]
        alive = clip_present[None]
        mask = alive.astype(jnp.float32)[:, :, None, None]
        act1 = low(jax.nn.silu(group_norm(inputs, frozen[0], frozen[1])))
        hid1 = low_back(conv_grid(act1, conv_full[0]) + clip_time + frozen[2] + frozen[3])
        act2 = low(jax.nn.silu(group_norm(hid1, frozen[4], frozen[5])))
        hid2 = low_back(conv_grid(act2, conv_full[1]) + frozen[6])
        first_res = inputs + hid2
        spatial_gn = low(group_norm(first_res, frozen[7], frozen[8]))
        state0 = low_back(project(spatial_gn, square_full[0]) + frozen[9])
        norm1 = low(layer_norm(state0, frozen[10], frozen[11]))
        self_q = low_back(project_back(norm1, square_full[1]))
        self_k = low_back(project_back(norm1, square_full[2]))
        self_v = low_back(project_back(norm1, square_full[3]))
        self_att = low(spatial_core(self_q, self_k, self_v))
        state1 = state0 + low_back(project(self_att, square_full[4]) + frozen[12])
        norm2 = low(layer_norm(state1, frozen[13], frozen[14]))
        cross_q = low_back(project_back(norm2, square_full[5]))
        text_k = jnp.einsum('lt,ct->lc', clip_text, cross_full[0], precision=HIGHEST)[None]
        text_v = jnp.einsum('lt,ct->lc', clip_text, cross_full[1], precision=HIGHEST)[None]
        cross_att = low(cross_core(cross_q, text_k, text_v))
        state2 = state1 + low_back(project(cross_att, square_full[6]) + frozen[15])
        norm3 = low(layer_norm(state2, frozen[16], frozen[17]))
        value_in = low_back(project_back(norm3, sffn_full[0]) + geglu_bias[0])
        gate_in = low_back(project_back(norm3, sffn_full[1]) + geglu_bias[1])
        mixed = low(value_in * gelu_exact(gate_in))
        state3 = low(state2 + low_back(project(mixed, sffn_full[2]) + frozen[18]))
        second_res = first_res + low_back(project(state3, square_full[7]) + frozen[19])
        normed = low(group_norm(second_res, vector_w[0], vector_w[1]))
        entered = low_back(project(normed, square_w[0]) + vector_w[2])
        tnorm1 = low(layer_norm(entered, vector_w[3], vector_w[4]) + frame_codes)
        query1 = low_back(project_back(tnorm1, square_w[3]))
        key1 = low_back(project_back(tnorm1, square_w[4]))
        value1 = low_back(project_back(tnorm1, square_w[5]))
        attend1 = low(temporal_core(query1, key1, value1, alive))
        block1 = entered + low_back(project(attend1, square_w[1]) + vector_w[5])
        tnorm2 = low(layer_norm(block1, vector_w[6], vector_w[7]) + frame_codes)
        query2 = low_back(project_back(tnorm2, square_w[7]))
        key2 = low_back(project_back(tnorm2, square_w[8]))
        value2 = low_back(project_back(tnorm2, square_w[9]))
        attend2 = low(temporal_core(query2, key2, value2, alive))
        block2 = block1 + low_back(project(attend2, square_w[6]) + vector_w[8])
        tnorm3 = low(layer_norm(block2, vector_w[9], vector_w[10]))
        inner_act = low_back(project_back(tnorm3, ffn_w[0]) + bias_w.reshape(FF))
        spread = low(gelu_tanh(inner_act))
        stream = low(block2 + low_back(project(spread, ffn_w[1]) + vector_w[11]))
        result = second_res + project(stream, square_w[2]) + vector_w[12]
        return (mask * result)[0]
    step = jax.checkpoint(clip_forward)

    def forward(inputs, square_w, ffn_w, bias_w, vector_w):
        weights = (low(square_w), low(ffn_w), low(bias_w), low(vector_w))
        return lax.map(lambda item: step(weights, item[0], item[1], item[2], item[3]), (inputs, time_bias, text_full, present))
    inputs = latents.astype(jnp.float32)
    result, pullback = jax.vjp(forward, inputs, projections, feedforward, up_bias, vectors)
    grad_in, grad_square, grad_ffn, grad_bias, grad_vector = pullback(cotangent.astype(jnp.float32))
    square_parts = update(projections, projections_moment, projections_average, grad_square, RATE_MATRIX)
    ffn_parts = update(feedforward, feedforward_moment, feedforward_average, grad_ffn, RATE_MATRIX)
    bias_parts = update(up_bias, up_bias_moment, up_bias_average, grad_bias, RATE_VECTOR)
    vector_parts = update(vectors, vectors_moment, vectors_average, grad_vector, RATE_VECTOR)
    return (result.astype(jnp.bfloat16), grad_in.astype(jnp.bfloat16), square_parts[0], square_parts[1], square_parts[2], ffn_parts[0], ffn_parts[1], ffn_parts[2], bias_parts[0], bias_parts[1], bias_parts[2], vector_parts[0], vector_parts[1], vector_parts[2])
```

```python
import functools
import math

import jax
import jax.numpy as jnp
from jax import lax
from jax.experimental import pallas as pl
from jax.experimental.pallas import tpu as pltpu
from jax.sharding import PartitionSpec as P

C = 1280
HD = 160
HEADS = C // HD
GROUPS = 32
FMAX = 24
SIDE = 8
PIX = 64
BF = jnp.bfloat16
F32 = jnp.float32
MESH = pl.DeviceIdType.MESH

MOMENTUM = 0.9
RATE_MATRIX = 0.0002
RATE_VECTOR = 0.002
AVERAGE_DECAY = 0.7
GROUP_EPS = 1e-06
LAYER_EPS = 1e-05
MASK_FILL = -1e30


def place():
    c = lax.axis_index("clip")
    h = lax.axis_index("head")
    core, gx, gy = c % 2, (c // 2) % 2, c // 4
    partners = {
        "x": (c + 2 - 4 * gx, h),
        "y": (c + 4 - 8 * gy, h),
        "core": (c + 1 - 2 * core, h),
    }
    heads = [h, h + 1 - 2 * (h % 2), h + 2 - 4 * (h // 2), 3 - h]
    return c, h, core, gx, gy, partners, heads


def greet(devices):
    barrier = pltpu.get_barrier_semaphore()
    for device in devices:
        pl.semaphore_signal(barrier, inc=1, device_id=device, device_id_type=MESH)
    pl.semaphore_wait(barrier, len(devices))


def gather_kernel(jobs, n_in, n_out, *refs):
    ins, outs = refs[:n_in], refs[n_in : n_in + n_out]
    send, recv, load_sem, store_sem, hold = refs[n_in + n_out :]
    c, h, core, gx, gy, partners, heads = place()
    xp, yp, cp = partners["x"], partners["y"], partners["core"]
    greet([xp, yp, cp] + [(c, heads[j]) for j in (1, 2, 3)])
    slots = hold.shape[0]

    def copy(a, j, kind, src, dst, device):
        return pltpu.make_async_remote_copy(
            src_ref=src,
            dst_ref=dst,
            send_sem=send.at[a, j, kind],
            recv_sem=recv.at[a, j, kind],
            device_id=device,
            device_id_type=MESH,
        )

    def view(job):
        kind, i_ref, o_ref, lo, at, n = job[0], ins[job[1]], outs[job[2]], job[3], job[4], job[5]
        rows = o_ref.shape[-2]
        part, into = pl.ds(lo, n), pl.ds(at, n)
        if kind == "frozen":
            half = o_ref.shape[-1] // 2
            lanes = pl.ds(pl.multiple_of(core * half, 128), half)
            src = i_ref.at[part, gy, gx, :, lanes]

            def slot(z, y, x, n0=0, nn=n, r0=0, rr=rows):
                return o_ref.at[pl.ds(at + n0, nn), z, y, x, pl.ds(r0, rr), lanes]

            def bundle(z):
                return o_ref.at[into, z, :, :, :, lanes]

            local = (i_ref.at[part], o_ref.at[into, h])
        else:
            src = i_ref.at[part]

            def slot(z, y, x, n0=0, nn=n, r0=0, rr=rows):
                return o_ref.at[pl.ds(at + n0, nn), y, z, x, core, pl.ds(r0, rr)]

            def bundle(z):
                return o_ref.at[into, :, z, :, core]

            local = (src, slot(h, gy, gx))
        if n >= 4 or n == 2:
            first = dict(n0=0, nn=(n + 1) // 2)
            second = dict(n0=(n + 1) // 2, nn=n - (n + 1) // 2)
        else:
            top = (rows // 2 + 15) // 16 * 16
            first, second = dict(r0=0, rr=top), dict(r0=top, rr=rows - top)
        return kind, src, slot, bundle, local, first, second

    views = [view(job) for job in jobs]

    def local_copies(a):
        kind, src, slot, bundle, local, first, second = views[a]
        buf = hold.at[a % slots]
        if kind == "frozen":
            n, ny, nx, rows, cols = local[0].shape
            pairs = []
            for i in range(n):
                for y in range(ny):
                    for x in range(nx):
                        at = ((i * ny + y) * nx + x) * rows
                        pairs.append(
                            (
                                local[0].at[i, y, x],
                                buf.at[pl.ds(at, rows), pl.ds(0, cols)],
                                local[1].at[i, y, x],
                            )
                        )
            return pairs
        n, rows, cols = local[0].shape
        return [
            (
                local[0].at[i],
                buf.at[pl.ds(i * rows, rows), pl.ds(0, cols)],
                local[1].at[i],
            )
            for i in range(n)
        ]

    def numbers(a):
        return (1, 2, 3) if views[a][0] == "frozen" else (0, 1, 2, 3)

    def fetch(a):
        src, slot = views[a][1:3]
        for j in (1, 2, 3):
            copy(a, j, 0, src, slot(h, gy, gx), (c, heads[j])).start()
        for k, (inp, mid, out) in enumerate(local_copies(a)):
            pltpu.make_async_copy(inp, mid, load_sem.at[a, k]).start()

    def trade(a):
        src, slot = views[a][1:3]
        for j in numbers(a):
            here = slot(heads[j], gy, gx)
            if j:
                copy(a, j, 0, src, here, (c, heads[j])).wait_recv()
            give = here if j else src
            copy(a, j, 1, give, here, xp).start()
            copy(a, j, 2, give, here, yp).start()
        for k, (inp, mid, out) in enumerate(local_copies(a)):
            pltpu.make_async_copy(inp, mid, load_sem.at[a, k]).wait()
            pltpu.make_async_copy(mid, out, store_sem.at[a, k]).start()

    def forward(a):
        kind, src, slot, bundle, local, first, second = views[a]
        for j in numbers(a):
            from_x, from_y = slot(heads[j], gy, 1 - gx), slot(heads[j], 1 - gy, gx)
            copy(a, j, 1, from_x, from_x, xp).wait_recv()
            piece = slot(heads[j], gy, 1 - gx, **first)
            copy(a, j, 3, piece, piece, yp).start()
            copy(a, j, 2, from_y, from_y, yp).wait_recv()
            piece = slot(heads[j], 1 - gy, gx, **second)
            copy(a, j, 4, piece, piece, xp).start()
        for k, (inp, mid, out) in enumerate(local_copies(a)):
            pltpu.make_async_copy(mid, out, store_sem.at[a, k]).wait()

    def share(a):
        kind, src, slot, bundle, local, first, second = views[a]
        for j in numbers(a):
            piece = slot(heads[j], 1 - gy, 1 - gx, **first)
            copy(a, j, 3, piece, piece, yp).wait_recv()
            piece = slot(heads[j], 1 - gy, 1 - gx, **second)
            copy(a, j, 4, piece, piece, xp).wait_recv()
            whole = bundle(heads[j])
            copy(a, j, 5, whole, whole, cp).start()

    def finish(a):
        kind, src, slot, bundle, local, first, second = views[a]
        for j in numbers(a):
            whole = bundle(heads[j])
            copy(a, j, 5, whole, whole, cp).wait()
            here = slot(heads[j], gy, gx)
            give = here if j else src
            if j:
                copy(a, j, 0, src, here, (c, heads[j])).wait_send()
            copy(a, j, 1, give, here, xp).wait_send()
            copy(a, j, 2, give, here, yp).wait_send()
            piece = slot(heads[j], gy, 1 - gx, **first)
            copy(a, j, 3, piece, piece, yp).wait_send()
            piece = slot(heads[j], 1 - gy, gx, **second)
            copy(a, j, 4, piece, piece, xp).wait_send()

    count = len(jobs)
    ahead = min(2, count)
    for a in range(ahead):
        fetch(a)
    for step in range(count + 3):
        if step < count:
            trade(step)
        if step + ahead < count:
            fetch(step + ahead)
        if 0 <= step - 1 < count:
            forward(step - 1)
        if 0 <= step - 2 < count:
            share(step - 2)
        if 0 <= step - 3 < count:
            finish(step - 3)


def gather_call(ins, out_shapes, jobs, collective_id):
    count = len(jobs)
    most = max(
        job[5] * (4 if job[0] == "frozen" else 1) * out_shapes[job[2]][-2] for job in jobs
    )
    return pl.pallas_call(
        functools.partial(gather_kernel, jobs, len(ins), len(out_shapes)),
        out_shape=tuple(jax.ShapeDtypeStruct(shape, BF) for shape in out_shapes),
        in_specs=[pl.BlockSpec(memory_space=pl.ANY)] * len(ins),
        out_specs=tuple(pl.BlockSpec(memory_space=pl.ANY) for _ in out_shapes),
        scratch_shapes=[
            pltpu.SemaphoreType.DMA((count, 4, 6)),
            pltpu.SemaphoreType.DMA((count, 4, 6)),
            pltpu.SemaphoreType.DMA((count, 16)),
            pltpu.SemaphoreType.DMA((count, 16)),
            pltpu.VMEM((4, most, C), BF),
        ],
        compiler_params=pltpu.CompilerParams(
            collective_id=collective_id, has_side_effects=True, vmem_limit_bytes=40 << 20
        ),
    )(*ins)


def gather_frozen(sizes, conv_weight, time_weight, spatial_square, cross_kv, spatial_ffn, small):
    arrays = (
        time_weight[None],
        conv_weight.reshape((18,) + conv_weight.shape[2:]),
        spatial_square,
        cross_kv,
        spatial_ffn,
    )
    pieces = [(0, 0, 1), (1, 0, 9), (1, 9, 9), (2, 0, 1), (2, 1, 3)]
    pieces += [(2, i, 1) for i in (4, 5, 6, 7)] + [(3, 0, 2)] + [(4, i, 1) for i in range(3)]
    if sizes != (8, 4):
        small = lax.all_gather(lax.all_gather(small, "head", axis=0), "clip", axis=0)
        return [
            lax.all_gather(arrays[i][lo : lo + n], "head", axis=1, tiled=True)
            for i, lo, n in pieces
        ] + [small]
    ins, shapes, jobs = [], [], []
    for a in arrays:
        n, rows, cols = a.shape
        ins.append(a.reshape(n, 2, 2, rows // 4, cols))
    for o, (i, lo, n) in enumerate(pieces):
        block = ins[i].shape[1:]
        shapes.append((n, 4) + block)
        step = 3 if n == 9 else n
        jobs += [("frozen", i, o, lo + at, at, step) for at in range(0, n, step)]
    ins.append(small[None])
    shapes.append((1, 2, 4, 2, 2) + small.shape)
    jobs.insert(0, ("own", len(ins) - 1, len(shapes) - 1, 0, 0, 1))
    outs = gather_call(ins, shapes, jobs, 1)
    whole = [o.reshape(o.shape[0], -1, o.shape[-1]) for o in outs[:-1]]
    order = outs[-1][0].transpose(0, 2, 3, 1, 4, 5)
    return whole + [order.reshape((8, 4) + small.shape)]


def gather_trained(sizes, projections, feedforward):
    square, wide = projections.astype(BF), feedforward.astype(BF)
    if sizes != (8, 4):
        return [
            lax.all_gather(
                lax.all_gather(a, "clip", axis=2, tiled=True), "head", axis=1, tiled=True
            )
            for a in (square, wide)
        ]
    square = lax.all_to_all(square.reshape(5, 8, 80, 160), "clip", 1, 3, tiled=True)
    wide = lax.all_to_all(wide.reshape(8, 320, 160), "clip", 0, 2, tiled=True)
    ins = [square.reshape(5, 80, C), wide.reshape(1, 320, C)]
    shapes = [(5, 2, 4, 2, 2, 80, C), (1, 2, 4, 2, 2, 320, C)]
    jobs = [("own", 0, 0, 0, 0, 2), ("own", 0, 0, 2, 2, 3), ("own", 1, 1, 0, 0, 1)]
    outs = gather_call(ins, shapes, jobs, 2)
    return [outs[0].reshape(10, C, C), outs[1].reshape(2, 4 * C, C)]


def pack_small(sizes, vectors, up_bias, geglu_bias):
    share = geglu_bias.shape[1] // sizes[0]
    start = lax.axis_index("clip") * share
    gate = lax.dynamic_slice_in_dim(geglu_bias, start, share, 1)
    high = gate.astype(BF)
    low = (gate - high.astype(F32)).astype(BF)
    flat = [vectors.astype(BF), up_bias.astype(BF), high, low]
    flat = jnp.concatenate([a.reshape(-1) for a in flat])
    return jnp.pad(flat, (0, 32 * C - flat.shape[0])).reshape(32, C)


def unpack_small(sizes, packed, vectors, up_bias, geglu_bias):
    n_clip, n_head = sizes
    packed = packed.reshape(n_clip, n_head, -1).astype(F32)
    sizes_of = [vectors.size, up_bias.size, geglu_bias.size // n_clip, geglu_bias.size // n_clip]
    parts, at = [], 0
    for size in sizes_of:
        parts.append(packed[:, :, at : at + size])
        at += size
    vector = parts[0][:, 0].reshape((n_clip,) + vectors.shape).transpose(1, 0, 2)
    bias = parts[1].reshape((n_clip, n_head) + up_bias.shape).transpose(1, 2, 0, 3)
    gate = (parts[2] + parts[3]).reshape(n_clip, n_head, 2, -1).transpose(2, 1, 0, 3)
    return vector.reshape(vectors.shape[0], C), bias.reshape(1, -1), gate.reshape(2, -1)


CHUNKS = 9


def sum_kernel(*refs):
    grads = refs[:12]
    out, landed = refs[12:14]
    total, own, got_x, got_y, got2, got3, send, recv, load_sem = refs[14:]
    c, h, core, gx, gy, partners, heads = place()
    xp, yp, cp = partners["x"], partners["y"], partners["core"]
    greet([xp, yp, cp] + [(c, heads[j]) for j in (1, 2, 3)])
    slots, loads = total.shape[0], own.shape[0]

    def block(k, y):
        if k < 5:
            return grads[2 * k + y]
        return grads[10 + y].at[:, :, :, k - 5]

    def copy(k, kind, src, dst, device):
        return pltpu.make_async_remote_copy(
            src_ref=src,
            dst_ref=dst,
            send_sem=send.at[k, kind],
            recv_sem=recv.at[k, kind],
            device_id=device,
            device_id_type=MESH,
        )

    def core_copies(k):
        return [copy(k, y, block(k, y).at[:, :, 1 - core], landed.at[k, y], cp) for y in (0, 1)]

    def load_copies(k):
        copies = [(landed.at[k], total.at[k % slots], 0)]
        for y in (0, 1):
            copies.append((block(k, y).at[:, :, core], own.at[k % loads, y], 1 + y))
        return [pltpu.make_async_copy(src, dst, load_sem.at[k, i]) for src, dst, i in copies]

    def first_copy(k):
        held = total.at[k % slots]
        if k % 2 == 0:
            return copy(k, 2, held.at[:, :, 1 - gx], got_x.at[k // 2], xp)
        return copy(k, 2, held.at[1 - gy], got_y.at[k // 2], yp)

    def second_copy(k):
        if k % 2 == 0:
            return copy(k, 3, got_x.at[k // 2, 1 - gy], got2.at[k], yp)
        return copy(k, 3, got_y.at[k // 2, :, 1 - gx], got2.at[k], xp)

    def last_copies(k):
        return [
            copy(k, 3 + j, got2.at[k, heads[j]], got3.at[k, j - 1], (c, heads[j]))
            for j in (1, 2, 3)
        ]

    def exchange(k):
        for item in core_copies(k):
            item.start()

    def load(k):
        for item in core_copies(k):
            item.wait_recv()
        if k >= slots:
            first_copy(k - slots).wait_send()
        for item in load_copies(k):
            item.start()

    def add_core(k):
        for item in load_copies(k):
            item.wait()
        slot, near = k % slots, k % loads

        def body(i, carry):
            y, z, x = i // 8, i // 2 % 4, i % 2
            total[slot, y, z, x] = total[slot, y, z, x] + own[near, y, z, x]
            return carry

        lax.fori_loop(0, 16, body, 0)
        first_copy(k).start()

    def add_first(k):
        first_copy(k).wait_recv()
        slot, at = k % slots, k // 2

        def body(i, carry):
            if k % 2 == 0:
                y, z = i // 4, i % 4
                got_x[at, y, z] = got_x[at, y, z] + total[slot, y, z, gx]
            else:
                z, x = i // 2, i % 2
                got_y[at, z, x] = got_y[at, z, x] + total[slot, gy, z, x]
            return carry

        lax.fori_loop(0, 8, body, 0)
        second_copy(k).start()

    def add_second(k):
        second_copy(k).wait_recv()
        at = k // 2

        def body(z, carry):
            if k % 2 == 0:
                got2[k, z] = got2[k, z] + got_x[at, gy, z]
            else:
                got2[k, z] = got2[k, z] + got_y[at, z, gx]
            return carry

        lax.fori_loop(0, 4, body, 0)
        for item in last_copies(k):
            item.start()

    def add_last(k):
        for item in last_copies(k):
            item.wait()
        rest = got3[k, 0].astype(F32) + got3[k, 1].astype(F32) + got3[k, 2].astype(F32)
        out[k] = got2[k, h].astype(F32) + rest

    for k in range(CHUNKS):
        exchange(k)
    load(0)
    for step in range(CHUNKS + 4):
        if step + 1 < CHUNKS:
            load(step + 1)
        if step < CHUNKS:
            add_core(step)
        if 0 <= step - 2 < CHUNKS:
            add_first(step - 2)
        if 0 <= step - 3 < CHUNKS:
            add_second(step - 3)
        if 0 <= step - 4 < CHUNKS:
            add_last(step - 4)
    for k in range(CHUNKS):
        for item in core_copies(k):
            item.wait_send()
        if k >= CHUNKS - slots:
            first_copy(k).wait_send()
        second_copy(k).wait_send()


def sum_square(sizes, parts, wide_parts):
    if sizes != (8, 4):
        return [
            jnp.stack(
                [
                    lax.psum_scatter(
                        lax.psum_scatter(g, "head", scatter_dimension=0, tiled=True),
                        "clip",
                        scatter_dimension=1,
                        tiled=True,
                    ).astype(F32)
                    for g in a
                ]
            )
            for a in (parts, wide_parts)
        ]
    ins = [g.reshape(4, 2, 2, 80, C) for g in parts]
    ins += [g.reshape(4, 2, 2, 4, 80, C) for g in wide_parts]
    own, _ = pl.pallas_call(
        sum_kernel,
        out_shape=(
            jax.ShapeDtypeStruct((CHUNKS, 80, C), F32),
            jax.ShapeDtypeStruct((CHUNKS, 2, 4, 2, 80, C), BF),
        ),
        in_specs=[pl.BlockSpec(memory_space=pl.ANY)] * 12,
        out_specs=(pl.BlockSpec(memory_space=pltpu.VMEM), pl.BlockSpec(memory_space=pl.ANY)),
        scratch_shapes=[
            pltpu.VMEM((4, 2, 4, 2, 80, C), BF),
            pltpu.VMEM((2, 2, 4, 2, 80, C), BF),
            pltpu.VMEM((5, 2, 4, 80, C), BF),
            pltpu.VMEM((4, 4, 2, 80, C), BF),
            pltpu.VMEM((CHUNKS, 4, 80, C), BF),
            pltpu.VMEM((CHUNKS, 3, 80, C), BF),
            pltpu.SemaphoreType.DMA((CHUNKS, 7)),
            pltpu.SemaphoreType.DMA((CHUNKS, 7)),
            pltpu.SemaphoreType.DMA((CHUNKS, 3)),
        ],
        compiler_params=pltpu.CompilerParams(
            collective_id=3, has_side_effects=True, vmem_limit_bytes=56 << 20
        ),
    )(*ins)
    own = own.astype(BF)
    square = lax.all_to_all(own[None, :5], "clip", 3, 0, tiled=True)
    wide = lax.all_to_all(own[5:].reshape(1, 320, C), "clip", 2, 0, tiled=True)
    square = square.transpose(1, 0, 2, 3).reshape(10, 320, 160).astype(F32)
    return square, wide.reshape(2, C, 160).astype(F32)


def head_window(head):
    start = head * HD // 128 * 128
    return start, head * HD - start


def lane_mask(shape, low):
    lane = lax.broadcasted_iota(jnp.int32, shape, 1)
    return (lane >= low) & (lane < low + HD)


def dot_f32(a, b, dims):
    return lax.dot_general(a, b, (dims, ((), ())), preferred_element_type=F32)


def head_probs(q, k, bias):
    scores = dot_f32(q, k, ((1,), (1,))) * HD ** (-0.5) + bias
    top = jnp.max(scores, axis=1, keepdims=True)
    weights = jnp.exp(scores - top)
    return weights / jnp.sum(weights, axis=1, keepdims=True)


def attend_kernel(q_ref, k_ref, v_ref, bias_ref, o_ref, acc):
    acc[...] = jnp.zeros_like(acc)
    for head in range(HEADS):
        start, low = head_window(head)
        win = pl.ds(start, 256)
        q = q_ref[:, win]
        mask = lane_mask(q.shape, low)
        q = jnp.where(mask, q, jnp.zeros_like(q))
        probs = head_probs(q, k_ref[:, win], bias_ref[...])
        out = dot_f32(probs.astype(BF), v_ref[:, win], ((1,), (0,)))
        acc[:, win] += jnp.where(mask, out, 0.0)
    o_ref[...] = acc[...].astype(BF)


def attend(q, k, v, bias):
    return pl.pallas_call(
        attend_kernel,
        out_shape=jax.ShapeDtypeStruct(q.shape, BF),
        scratch_shapes=[pltpu.VMEM(q.shape, F32)],
        compiler_params=pltpu.CompilerParams(vmem_limit_bytes=40 << 20),
    )(q, k, v, bias)


def attend_back_kernel(with_keys, q_ref, k_ref, v_ref, bias_ref, g_ref, *refs):
    if with_keys:
        dq_ref, dk_ref, dv_ref, dq, dk, dv = refs
        dk[...] = jnp.zeros_like(dk)
        dv[...] = jnp.zeros_like(dv)
    else:
        dq_ref, dq = refs
    dq[...] = jnp.zeros_like(dq)
    for head in range(HEADS):
        start, low = head_window(head)
        win = pl.ds(start, 256)
        q, k, v, g = q_ref[:, win], k_ref[:, win], v_ref[:, win], g_ref[:, win]
        mask = lane_mask(q.shape, low)
        q = jnp.where(mask, q, jnp.zeros_like(q))
        g = jnp.where(mask, g, jnp.zeros_like(g))
        probs = head_probs(q, k, bias_ref[...])
        dp = dot_f32(g, v, ((1,), (1,)))
        ds = probs * (dp - jnp.sum(dp * probs, axis=1, keepdims=True)) * HD ** (-0.5)
        ds = ds.astype(BF)
        dq[:, win] += jnp.where(mask, dot_f32(ds, k, ((1,), (0,))), 0.0)
        if with_keys:
            dk[:, win] += dot_f32(ds, q, ((0,), (0,)))
            dv[:, win] += dot_f32(probs.astype(BF), g, ((0,), (0,)))
    dq_ref[...] = dq[...].astype(BF)
    if with_keys:
        dk_ref[...] = dk[...].astype(BF)
        dv_ref[...] = dv[...].astype(BF)


def attend_back(q, k, v, bias, g, with_keys=True):
    count = 3 if with_keys else 1
    return pl.pallas_call(
        functools.partial(attend_back_kernel, with_keys),
        out_shape=(jax.ShapeDtypeStruct(q.shape, BF),) * count,
        scratch_shapes=[pltpu.VMEM(q.shape, F32)] * count,
        compiler_params=pltpu.CompilerParams(vmem_limit_bytes=48 << 20),
    )(q, k, v, bias, g)


def group_mean(per_channel):
    width = C // GROUPS
    means = jnp.mean(per_channel.reshape(-1, GROUPS, width), axis=-1) / PIX
    return jnp.repeat(means, width, axis=1)[:, None, :]


def gn_stats(x):
    center = group_mean(jnp.sum(x, axis=1))
    centered = x - center
    variance = group_mean(jnp.sum(centered * centered, axis=1))
    return center, lax.rsqrt(variance + GROUP_EPS)


def gn(x, stats, gain, shift):
    return (x - stats[0]) * stats[1] * gain + shift


def gn_back(dy, x, stats, gain):
    z = (x - stats[0]) * stats[1]
    gd = dy * gain
    mean_gd = group_mean(jnp.sum(gd, axis=1))
    mean_gz = group_mean(jnp.sum(gd * z, axis=1))
    return (gd - mean_gd - z * mean_gz) * stats[1]


def ln_stats(x):
    center = jnp.mean(x, axis=-1, keepdims=True)
    centered = x - center
    variance = jnp.mean(centered * centered, axis=-1, keepdims=True)
    return center, lax.rsqrt(variance + LAYER_EPS)


def ln(x, stats, gain, shift):
    return (x - stats[0]) * stats[1] * gain + shift


def ln_back(dy, x, stats, gain):
    z = (x - stats[0]) * stats[1]
    gd = dy * gain
    mean_gd = jnp.mean(gd, axis=-1, keepdims=True)
    mean_gz = jnp.mean(gd * z, axis=-1, keepdims=True)
    return (gd - mean_gd - z * mean_gz) * stats[1]


def ln_param_grads(dy, x, stats):
    z = (x - stats[0]) * stats[1]
    return jnp.sum(dy * z, axis=0), jnp.sum(dy, axis=0)


def silu_back(dy, v):
    gate = jax.nn.sigmoid(v)
    return dy * gate * (1.0 + v * (1.0 - gate))


def gelu_exact(v):
    return jax.nn.gelu(v, approximate=False)


def gelu_exact_slope(v):
    density = jnp.exp(-0.5 * v * v) * (1.0 / math.sqrt(2.0 * math.pi))
    return 0.5 * (1.0 + lax.erf(v * math.sqrt(0.5))) + v * density


def gelu_tanh(v):
    return jax.nn.gelu(v, approximate=True)


def gelu_tanh_slope(v):
    k = math.sqrt(2.0 / math.pi)
    t = jnp.tanh(k * (v + 0.044715 * v * v * v))
    return 0.5 * (1.0 + t) + 0.5 * v * (1.0 - t * t) * k * (1.0 + 3.0 * 0.044715 * v * v)


def frame_table():
    frame_pos = jnp.arange(FMAX, dtype=F32)[:, None]
    channel = jnp.arange(C)
    frequency = jnp.exp((channel - channel % 2).astype(F32) * (-math.log(10000.0) / C))
    angles = frame_pos * frequency[None, :]
    return jnp.where(channel[None, :] % 2 == 0, jnp.sin(angles), jnp.cos(angles))


def time_table(timesteps):
    half_width = C // 2
    frequency = jnp.exp(jnp.arange(half_width, dtype=F32) * (-math.log(10000.0) / half_width))
    angles = timesteps.astype(F32)[:, None] * frequency[None, :]
    return jnp.concatenate([jnp.cos(angles), jnp.sin(angles)], axis=1)


def through(x, w):
    return dot_f32(x, w, ((1,), (0,)))


def against(x, w):
    return dot_f32(x, w, ((1,), (1,)))


def outer(a, b):
    return dot_f32(a, b, ((0,), (0,))).astype(BF)


def windows(x, flipped):
    frames = x.shape[0]
    padded = jnp.pad(x.reshape(frames, SIDE, SIDE, C), ((0, 0), (1, 1), (1, 1), (0, 0)))
    pieces = []
    for tap in range(9):
        dy, dx = tap // 3, tap % 3
        if flipped:
            dy, dx = 2 - dy, 2 - dx
        pieces.append(padded[:, dy : dy + SIDE, dx : dx + SIDE].reshape(frames * PIX, C))
    return pieces


def conv(x, w):
    return through(jnp.concatenate(windows(x, False), axis=1), w.reshape(9 * C, C))


def conv_back(g, w):
    stacked = jnp.stack(windows(g, True), axis=1)
    return lax.dot_general(
        stacked, w, (((1, 2), (0, 2)), ((), ())), preferred_element_type=F32
    )


def update(weight, moment, average, gradient, step_rate):
    moment_new = MOMENTUM * moment + gradient
    weight_new = weight - step_rate * (gradient + MOMENTUM * moment_new)
    average_new = AVERAGE_DECAY * average + (1.0 - AVERAGE_DECAY) * weight_new
    return (moment_new, average_new, weight_new)


def per_device(
    sizes,
    latents,
    cotangent,
    frames,
    timesteps,
    text,
    conv_weight,
    time_weight,
    frozen_params,
    spatial_square,
    cross_kv,
    spatial_ffn,
    geglu_bias,
    projections,
    feedforward,
    up_bias,
    vectors,
    projections_moment,
    feedforward_moment,
    up_bias_moment,
    vectors_moment,
    projections_average,
    feedforward_average,
    up_bias_average,
    vectors_average,
):
    Q = frozen_params
    n_head = sizes[1]
    head_index = lax.axis_index("head")
    clip_index = lax.axis_index("clip")
    own_frames = latents.shape[1]
    tokens = own_frames * PIX
    own_pixels = PIX // n_head
    columns = FMAX * own_pixels

    def framed(x):
        return x.reshape(own_frames, PIX, C)

    def flat(x):
        return x.reshape(tokens, C)

    def to_pixels(x):
        x = lax.all_to_all(framed(x), "head", 1, 0, tiled=True)
        return x.reshape(columns, C)

    def to_frames(x):
        x = lax.all_to_all(x.reshape(FMAX, own_pixels, C), "head", 0, 1, tiled=True)
        return x.reshape(tokens, C)

    frame_of = jnp.arange(tokens) // PIX
    spatial_bias = jnp.where(frame_of[:, None] == frame_of[None, :], 0.0, MASK_FILL).astype(F32)
    column = jnp.arange(columns)
    same_pixel = (column % own_pixels)[:, None] == (column % own_pixels)[None, :]
    key_there = (column // own_pixels)[None, :] < frames[0]
    temporal_bias = jnp.where(same_pixel & key_there, 0.0, MASK_FILL).astype(F32)
    text_len = text.shape[1]
    text_rows = 128
    cross_bias = jnp.broadcast_to(
        jnp.where(jnp.arange(text_rows)[None, :] < text_len, 0.0, MASK_FILL), (tokens, text_rows)
    ).astype(F32)
    codes = jnp.repeat(frame_table(), own_pixels, axis=0)
    own_frame = head_index * own_frames + jnp.arange(own_frames)
    frame_mask = (own_frame < frames[0]).astype(F32)[:, None, None]

    small = pack_small(sizes, vectors, up_bias, geglu_bias)
    gathered = gather_frozen(
        sizes, conv_weight, time_weight, spatial_square, cross_kv, spatial_ffn, small
    )
    time_w, conv1_w, conv2_w, in_w, self_w, self_o, cross_qw, cross_o, out_w = gathered[:9]
    cross_w, ffn_value, ffn_gate, ffn_down, small = gathered[9:]
    vector_f, bias_f, geglu_f = unpack_small(sizes, small, vectors, up_bias, geglu_bias)
    square_w, ffn_w = gather_trained(sizes, projections, feedforward)

    x0 = latents[0].astype(F32)
    grad_out = frame_mask * cotangent[0].astype(F32)

    stats0 = gn_stats(x0)
    act1 = jax.nn.silu(gn(x0, stats0, Q[0], Q[1])).astype(BF)
    time_in = jax.nn.silu(time_table(timesteps)).astype(BF)
    hid1 = framed(conv(act1, conv1_w) + through(time_in, time_w[0]) + Q[2] + Q[3])
    stats1 = gn_stats(hid1)
    act2 = jax.nn.silu(gn(hid1, stats1, Q[4], Q[5])).astype(BF)
    first = x0 + framed(conv(act2, conv2_w) + Q[6])

    stats2 = gn_stats(first)
    spatial_in = flat(gn(first, stats2, Q[7], Q[8]).astype(BF))
    state0 = through(spatial_in, in_w[0]) + Q[9]
    sl1 = ln_stats(state0)
    norm1 = ln(state0, sl1, Q[10], Q[11]).astype(BF)
    self_q, self_k, self_v = (against(norm1, self_w[i - 1]).astype(BF) for i in (1, 2, 3))
    self_att = attend(self_q, self_k, self_v, spatial_bias)
    state1 = state0 + through(self_att, self_o[0]) + Q[12]
    sl2 = ln_stats(state1)
    norm2 = ln(state1, sl2, Q[13], Q[14]).astype(BF)
    cross_q = against(norm2, cross_qw[0]).astype(BF)
    text_pad = jnp.pad(text[0], ((0, text_rows - text_len), (0, 0)))
    text_k, text_v = (against(text_pad, cross_w[i]).astype(BF) for i in (0, 1))
    cross_att = attend(cross_q, text_k, text_v, cross_bias)
    state2 = state1 + through(cross_att, cross_o[0]) + Q[15]
    sl3 = ln_stats(state2)
    norm3 = ln(state2, sl3, Q[16], Q[17]).astype(BF)
    value_in = against(norm3, ffn_value[0]) + geglu_f[0]
    gate_in = against(norm3, ffn_gate[0]) + geglu_f[1]
    mixed = (value_in * gelu_exact(gate_in)).astype(BF)
    state3 = (state2 + through(mixed, ffn_down[0]) + Q[18]).astype(BF)
    second = first + framed(through(state3, out_w[0]) + Q[19])

    stats3 = gn_stats(second)
    normed = to_pixels(gn(second, stats3, vector_f[0], vector_f[1]).astype(BF))
    entered = through(normed, square_w[0]) + vector_f[2]

    def temporal_in(x, gain_row, wq):
        stats = ln_stats(x)
        t = (ln(x, stats, vector_f[gain_row], vector_f[gain_row + 1]) + codes).astype(BF)
        qkv = [against(t, square_w[wq + i]).astype(BF) for i in range(3)]
        return stats, t, qkv

    tl1, t1, qkv1 = temporal_in(entered, 3, 3)
    att1 = attend(*qkv1, temporal_bias)
    block1 = entered + through(att1, square_w[1]) + vector_f[5]
    tl2, t2, qkv2 = temporal_in(block1, 6, 7)
    att2 = attend(*qkv2, temporal_bias)
    block2 = block1 + through(att2, square_w[6]) + vector_f[8]
    tl3 = ln_stats(block2)
    t3 = ln(block2, tl3, vector_f[9], vector_f[10]).astype(BF)
    inner = against(t3, ffn_w[0]) + bias_f
    spread = gelu_tanh(inner).astype(BF)
    stream = (block2 + through(spread, ffn_w[1]) + vector_f[11]).astype(BF)
    moved = to_frames(through(stream, square_w[2]).astype(BF)).astype(F32)
    output = (frame_mask * (second + framed(moved) + vector_f[12])).astype(BF)[None]

    g_out = to_pixels(grad_out.astype(BF))
    col = lambda v: jnp.sum(v.astype(F32), axis=0)
    G = {}
    G[2] = outer(stream, g_out)
    grad_stream = against(g_out, square_w[2])
    g_ffn = grad_stream.astype(BF)
    grad_down = outer(spread, g_ffn)
    g_inner = (gelu_tanh_slope(inner) * against(g_ffn, ffn_w[1])).astype(BF)
    grad_up = outer(g_inner, t3)
    grad_t3 = through(g_inner, ffn_w[0])
    grad_b2 = grad_stream + ln_back(grad_t3, block2, tl3, vector_f[9])
    dgain3, dshift3 = ln_param_grads(grad_t3, block2, tl3)

    def temporal_back(grad, x, stats, t, qkv, att, gain_row, wo, wq):
        low = grad.astype(BF)
        G[wo] = outer(att, low)
        dqkv = attend_back(*qkv, temporal_bias, against(low, square_w[wo]).astype(BF))
        for i in range(3):
            G[wq + i] = outer(dqkv[i], t)
        grad_t = sum(through(dqkv[i], square_w[wq + i]) for i in range(3))
        grad_x = grad + ln_back(grad_t, x, stats, vector_f[gain_row])
        return grad_x, ln_param_grads(grad_t, x, stats), col(low)

    grad_b1, (dgain2, dshift2), dbias2 = temporal_back(
        grad_b2, block1, tl2, t2, qkv2, att2, 6, 6, 7
    )
    grad_e, (dgain1, dshift1), dbias1 = temporal_back(
        grad_b1, entered, tl1, t1, qkv1, att1, 3, 1, 3
    )
    g_entry = grad_e.astype(BF)
    G[0] = outer(normed, g_entry)
    grad_normed = framed(to_frames(against(g_entry, square_w[0]).astype(BF)).astype(F32))
    z = (second - stats3[0]) * stats3[1]
    dgain0 = jnp.sum(grad_normed * z, axis=(0, 1))
    dshift0 = jnp.sum(grad_normed, axis=(0, 1))
    grad_second = grad_out + gn_back(grad_normed, second, stats3, vector_f[0])

    grad_vector = jnp.stack(
        [
            dgain0,
            dshift0,
            col(g_entry),
            dgain1,
            dshift1,
            dbias1,
            dgain2,
            dshift2,
            dbias2,
            dgain3,
            dshift3,
            col(g_ffn),
            col(g_out),
        ]
    )
    small = jnp.concatenate([grad_vector.reshape(-1), col(g_inner)])
    small = lax.psum(small, ("clip", "head"))
    total_vector = small[: 13 * C].reshape(13, C)
    total_bias = small[13 * C :].reshape(-1, 128)
    own_vector = lax.dynamic_slice_in_dim(
        total_vector, clip_index * vectors.shape[1], vectors.shape[1], 1
    )
    own_bias = lax.dynamic_slice(
        total_bias,
        (head_index * up_bias.shape[0], clip_index * up_bias.shape[1]),
        up_bias.shape,
    )
    own_square, own_wide = sum_square(sizes, [G[i] for i in range(10)], [grad_up, grad_down])

    g_po = flat(grad_second).astype(BF)
    grad_s3 = against(g_po, out_w[0])
    g_fb = grad_s3.astype(BF)
    grad_mixed = against(g_fb, ffn_down[0])
    g_value = (gelu_exact(gate_in) * grad_mixed).astype(BF)
    g_gate = (value_in * gelu_exact_slope(gate_in) * grad_mixed).astype(BF)
    grad_n3 = through(g_value, ffn_value[0]) + through(g_gate, ffn_gate[0])
    grad_s2 = grad_s3 + ln_back(grad_n3, state2, sl3, Q[16])
    g_cb = grad_s2.astype(BF)
    (g_cq,) = attend_back(
        cross_q, text_k, text_v, cross_bias, against(g_cb, cross_o[0]).astype(BF), False
    )
    grad_s1 = grad_s2 + ln_back(through(g_cq, cross_qw[0]), state1, sl2, Q[13])
    g_sb = grad_s1.astype(BF)
    dself = attend_back(
        self_q, self_k, self_v, spatial_bias, against(g_sb, self_o[0]).astype(BF)
    )
    grad_n1 = sum(through(dself[i], self_w[i]) for i in range(3))
    grad_s0 = grad_s1 + ln_back(grad_n1, state0, sl1, Q[10])
    g_pi = grad_s0.astype(BF)
    grad_gn = framed(against(g_pi, in_w[0]))
    grad_first = grad_second + gn_back(grad_gn, first, stats2, Q[7])

    grad_act2 = framed(conv_back(grad_first.astype(BF), conv2_w))
    grad_n = silu_back(grad_act2, gn(hid1, stats1, Q[4], Q[5]))
    grad_hid1 = gn_back(grad_n, hid1, stats1, Q[4])
    grad_act1 = framed(conv_back(grad_hid1.astype(BF), conv1_w))
    grad_n = silu_back(grad_act1, gn(x0, stats0, Q[0], Q[1]))
    input_gradient = (grad_first + gn_back(grad_n, x0, stats0, Q[0])).astype(BF)[None]

    square_parts = update(
        projections, projections_moment, projections_average, own_square, RATE_MATRIX
    )
    ffn_parts = update(feedforward, feedforward_moment, feedforward_average, own_wide, RATE_MATRIX)
    bias_parts = update(up_bias, up_bias_moment, up_bias_average, own_bias, RATE_VECTOR)
    vector_parts = update(vectors, vectors_moment, vectors_average, own_vector, RATE_VECTOR)
    return (output, input_gradient) + square_parts + ffn_parts + bias_parts + vector_parts


def solution(mesh):
    sizes = (mesh.shape["clip"], mesh.shape["head"])
    return jax.shard_map(
        functools.partial(per_device, sizes),
        mesh=mesh,
        in_specs=(
            P("clip", "head", None, None),
            P("clip", "head", None, None),
            P("clip"),
            P("clip"),
            P("clip", None, None),
            P(None, None, "head", None),
            P("head", None),
            P(),
            P(None, "head", None),
            P(None, "head", None),
            P(None, "head", None),
            P(None, "head"),
            P(None, "head", "clip"),
            P(None, "head", "clip"),
            P("head", "clip"),
            P(None, "clip"),
            P(None, "head", "clip"),
            P(None, "head", "clip"),
            P("head", "clip"),
            P(None, "clip"),
            P(None, "head", "clip"),
            P(None, "head", "clip"),
            P("head", "clip"),
            P(None, "clip"),
        ),
        out_specs=(
            P("clip", "head", None, None),
            P("clip", "head", None, None),
            P(None, "head", "clip"),
            P(None, "head", "clip"),
            P(None, "head", "clip"),
            P(None, "head", "clip"),
            P(None, "head", "clip"),
            P(None, "head", "clip"),
            P("head", "clip"),
            P("head", "clip"),
            P("head", "clip"),
            P(None, "clip"),
            P(None, "clip"),
            P(None, "clip"),
        ),
        check_vma=False,
    )
```

```python
import functools
import math

import jax
import jax.numpy as jnp
from jax import lax
from jax.experimental import pallas as pl
from jax.experimental.pallas import tpu as pltpu
from jax.sharding import PartitionSpec as P

C = 1280
HD = 160
HEADS = C // HD
GROUPS = 32
FMAX = 24
SIDE = 8
PIX = 64
BF = jnp.bfloat16
F32 = jnp.float32
MESH = pl.DeviceIdType.MESH

MOMENTUM = 0.9
RATE_MATRIX = 0.0002
RATE_VECTOR = 0.002
AVERAGE_DECAY = 0.7
GROUP_EPS = 1e-06
LAYER_EPS = 1e-05
MASK_FILL = -1e30


def place():
    c = lax.axis_index("clip")
    h = lax.axis_index("head")
    core, gx, gy = c % 2, (c // 2) % 2, c // 4
    partners = {
        "x": (c + 2 - 4 * gx, h),
        "y": (c + 4 - 8 * gy, h),
        "core": (c + 1 - 2 * core, h),
    }
    heads = [h, h + 1 - 2 * (h % 2), h + 2 - 4 * (h // 2), 3 - h]
    return c, h, core, gx, gy, partners, heads


def greet(devices):
    barrier = pltpu.get_barrier_semaphore()
    for device in devices:
        pl.semaphore_signal(barrier, inc=1, device_id=device, device_id_type=MESH)
    pl.semaphore_wait(barrier, len(devices))


class Gather:

    def __init__(self, jobs, ins, outs, send, recv, load_sem, store_sem, hold):
        self.jobs = jobs
        self.sems = (send, recv, load_sem, store_sem)
        self.hold = hold
        c, h, core, gx, gy, partners, heads = place()
        self.c, self.h, self.core, self.gx, self.gy = c, h, core, gx, gy
        self.xp, self.yp, self.cp = partners["x"], partners["y"], partners["core"]
        self.heads = heads
        self.views = [self.view(job, ins, outs) for job in jobs]

    def peers(self):
        return [self.xp, self.yp, self.cp] + [(self.c, self.heads[j]) for j in (1, 2, 3)]

    def copy(self, a, j, kind, src, dst, device):
        return pltpu.make_async_remote_copy(
            src_ref=src,
            dst_ref=dst,
            send_sem=self.sems[0].at[a, j, kind],
            recv_sem=self.sems[1].at[a, j, kind],
            device_id=device,
            device_id_type=MESH,
        )

    def view(self, job, ins, outs):
        kind, i_ref, o_ref, lo, at, n = job[0], ins[job[1]], outs[job[2]], job[3], job[4], job[5]
        core, gx, gy, h = self.core, self.gx, self.gy, self.h
        part, into = pl.ds(lo, n), pl.ds(at, n)
        if kind == "frozen":
            shard = i_ref.shape[-2]
            rows = shard // 4
            half = o_ref.shape[-1] // 2
            lanes = pl.ds(pl.multiple_of(core * half, 128), half)
            src = i_ref.at[part, pl.ds(pl.multiple_of((gy * 2 + gx) * rows, 16), rows), lanes]

            def slot(z, y, x, n0=0, nn=n, r0=0, rr=rows):
                first = pl.multiple_of(z * shard + (y * 2 + x) * rows + r0, 16)
                return o_ref.at[pl.ds(at + n0, nn), pl.ds(first, rr), lanes]

            def bundle(z):
                return o_ref.at[into, pl.ds(pl.multiple_of(z * shard, 16), shard), lanes]

            own = pl.ds(pl.multiple_of(h * shard, 16), shard)
            local = [(i_ref.at[lo + i], o_ref.at[at + i, own]) for i in range(n)]
        else:
            rows = i_ref.shape[-2]
            src = i_ref.at[part]

            def slot(z, y, x, n0=0, nn=n, r0=0, rr=rows):
                first = pl.multiple_of(((z * 2 + core) * 2 + x) * rows + r0, 16)
                return o_ref.at[pl.ds(at + n0, nn), y, pl.ds(first, rr)]

            def bundle(z):
                first = pl.multiple_of((z * 2 + core) * 2 * rows, 16)
                return o_ref.at[into, :, pl.ds(first, 2 * rows)]

            here = pl.ds(pl.multiple_of(((h * 2 + core) * 2 + gx) * rows, 16), rows)
            local = [(i_ref.at[lo + i], o_ref.at[at + i, gy, here]) for i in range(n)]
        if n >= 4 or n == 2:
            first = dict(n0=0, nn=(n + 1) // 2)
            second = dict(n0=(n + 1) // 2, nn=n - (n + 1) // 2)
        else:
            top = (rows // 2 + 15) // 16 * 16
            first, second = dict(r0=0, rr=top), dict(r0=top, rr=rows - top)
        return kind, src, slot, bundle, local, first, second

    def local_copies(self, a):
        buf = self.hold.at[a % self.hold.shape[0]]
        triples = []
        for i, (src, dst) in enumerate(self.views[a][4]):
            rows, cols = src.shape
            triples.append((src, buf.at[pl.ds(i * rows, rows), pl.ds(0, cols)], dst))
        return triples

    def numbers(self, a):
        return (1, 2, 3) if self.views[a][0] == "frozen" else (0, 1, 2, 3)

    def fetch(self, a):
        src, slot = self.views[a][1:3]
        for j in (1, 2, 3):
            there = (self.c, self.heads[j])
            self.copy(a, j, 0, src, slot(self.h, self.gy, self.gx), there).start()

    def trade(self, a):
        src, slot = self.views[a][1:3]
        locals_ = self.local_copies(a)
        for k, (inp, mid, out) in enumerate(locals_):
            pltpu.make_async_copy(inp, mid, self.sems[2].at[a, k]).start()
        for j in self.numbers(a):
            here = slot(self.heads[j], self.gy, self.gx)
            if j:
                self.copy(a, j, 0, src, here, (self.c, self.heads[j])).wait_recv()
            give = here if j else src
            self.copy(a, j, 1, give, here, self.xp).start()
            self.copy(a, j, 2, give, here, self.yp).start()
        for k, (inp, mid, out) in enumerate(locals_):
            pltpu.make_async_copy(inp, mid, self.sems[2].at[a, k]).wait()
            pltpu.make_async_copy(mid, out, self.sems[3].at[a, k]).start()

    def forward(self, a):
        kind, src, slot, bundle, local, first, second = self.views[a]
        gx, gy, xp, yp = self.gx, self.gy, self.xp, self.yp
        for j in self.numbers(a):
            z = self.heads[j]
            from_x, from_y = slot(z, gy, 1 - gx), slot(z, 1 - gy, gx)
            self.copy(a, j, 1, from_x, from_x, xp).wait_recv()
            piece = slot(z, gy, 1 - gx, **first)
            self.copy(a, j, 3, piece, piece, yp).start()
            self.copy(a, j, 2, from_y, from_y, yp).wait_recv()
            piece = slot(z, 1 - gy, gx, **second)
            self.copy(a, j, 4, piece, piece, xp).start()
        for k, (inp, mid, out) in enumerate(self.local_copies(a)):
            pltpu.make_async_copy(mid, out, self.sems[3].at[a, k]).wait()

    def share(self, a):
        kind, src, slot, bundle, local, first, second = self.views[a]
        gx, gy, xp, yp = self.gx, self.gy, self.xp, self.yp
        for j in self.numbers(a):
            z = self.heads[j]
            piece = slot(z, 1 - gy, 1 - gx, **first)
            self.copy(a, j, 3, piece, piece, yp).wait_recv()
            piece = slot(z, 1 - gy, 1 - gx, **second)
            self.copy(a, j, 4, piece, piece, xp).wait_recv()
            whole = bundle(z)
            self.copy(a, j, 5, whole, whole, self.cp).start()

    def finish(self, a):
        kind, src, slot, bundle, local, first, second = self.views[a]
        gx, gy, xp, yp = self.gx, self.gy, self.xp, self.yp
        for j in self.numbers(a):
            z = self.heads[j]
            whole = bundle(z)
            self.copy(a, j, 5, whole, whole, self.cp).wait()
            here = slot(z, gy, gx)
            give = here if j else src
            if j:
                self.copy(a, j, 0, src, here, (self.c, z)).wait_send()
            self.copy(a, j, 1, give, here, xp).wait_send()
            self.copy(a, j, 2, give, here, yp).wait_send()
            piece = slot(z, gy, 1 - gx, **first)
            self.copy(a, j, 3, piece, piece, yp).wait_send()
            piece = slot(z, 1 - gy, gx, **second)
            self.copy(a, j, 4, piece, piece, xp).wait_send()

    def run(self, units, ahead=2):
        count = len(self.jobs)
        done, at = 0, 0

        def work(most):
            nonlocal at
            while at < len(units) and units[at][0] <= done and most > 0:
                units[at][1]()
                at += 1
                most -= 1

        for a in range(min(ahead, count)):
            self.fetch(a)
        work(2)
        for step in range(count + 3):
            if step < count:
                self.trade(step)
                work(2)
            if step + ahead < count:
                self.fetch(step + ahead)
            if 0 <= step - 1 < count:
                self.forward(step - 1)
                work(2)
            if 0 <= step - 2 < count:
                self.share(step - 2)
                work(2)
            if 0 <= step - 3 < count:
                self.finish(step - 3)
                done = step - 2
                work(2)
        work(len(units))


FROZEN = [(0, 0, 1), (1, 0, 9), (1, 9, 9), (2, 0, 1), (2, 1, 3), (2, 4, 1), (2, 5, 1)]
FROZEN += [(3, 0, 2), (2, 6, 1), (4, 0, 1), (4, 1, 1), (4, 2, 1), (2, 7, 1)]


def frozen_arrays(conv_weight, time_weight, spatial_square, cross_kv, spatial_ffn):
    return [
        time_weight[None],
        conv_weight.reshape((18,) + conv_weight.shape[2:]),
        spatial_square,
        cross_kv,
        spatial_ffn,
    ]


def gather_plain(arrays, small, projections, feedforward):
    small = lax.all_gather(lax.all_gather(small, "head", axis=0), "clip", axis=0)
    frozen = [
        lax.all_gather(arrays[i][lo : lo + n], "head", axis=1, tiled=True) for i, lo, n in FROZEN
    ]
    trained = [
        lax.all_gather(
            lax.all_gather(a.astype(BF), "clip", axis=2, tiled=True), "head", axis=1, tiled=True
        )
        for a in (projections, feedforward)
    ]
    return frozen, trained, small


TILE = 256


def stream(count, tiles, body, sem, slots):
    def begin(i):
        for p, (src, dst) in enumerate(tiles(i, i % slots)):
            pltpu.make_async_copy(src, dst, sem.at[i % slots, p]).start()

    for i in range(min(slots - 1, count)):
        begin(i)

    def step(i, carry):
        @pl.when(i + slots - 1 < count)
        def _():
            begin(i + slots - 1)

        for p, (src, dst) in enumerate(tiles(i, i % slots)):
            pltpu.make_async_copy(src, dst, sem.at[i % slots, p]).wait()
        body(i, i % slots)
        return carry

    lax.fori_loop(0, count, step, 0)


def tile_at(i):
    return pl.ds(pl.multiple_of(i * TILE, TILE), TILE)


def through_tiles(x, w, buf, sem, sink):
    slots = buf.shape[0]

    def tiles(i, slot):
        return [(w.at[:, tile_at(i)], buf.at[slot])]

    def body(i, slot):
        sink(tile_at(i), dot_f32(x[...], buf[slot], ((1,), (0,))))

    stream(w.shape[1] // TILE, tiles, body, sem, slots)


def against_tiles(x, w, buf, sem, sink):
    slots, width = buf.shape[0], w.shape[1]
    lanes = pl.ds(0, width)

    def tiles(i, slot):
        return [(w.at[tile_at(i)], buf.at[slot, :, lanes])]

    def body(i, slot):
        sink(tile_at(i), dot_f32(x[...], buf[slot, :, lanes], ((1,), (1,))))

    stream(w.shape[0] // TILE, tiles, body, sem, slots)


def frame_rows(f):
    return pl.ds(pl.multiple_of(f * PIX, PIX), PIX)


def norm_rows(x, q, gain, out):
    def body(f, carry):
        rows = frame_rows(f)
        v = x[rows, :]
        v = v - jnp.mean(v, axis=1, keepdims=True)
        scale = lax.rsqrt(jnp.mean(v * v, axis=1, keepdims=True) + LAYER_EPS)
        out[rows, :] = (v * scale * q[gain : gain + 1] + q[gain + 1 : gain + 2]).astype(out.dtype)
        return carry

    lax.fori_loop(0, x.shape[0] // PIX, body, 0)


def dot_exact(a, b):
    return lax.dot_general(
        a, b, (((1,), (0,)), ((), ())), precision=lax.Precision.HIGHEST, preferred_element_type=F32
    )


def group_stats(x, fold, unfold, stat):
    frames = x.shape[0] // PIX
    stat[0] = jnp.zeros_like(stat[0])
    stat[1] = jnp.zeros_like(stat[1])
    for f in range(frames):
        block = x[f * PIX : (f + 1) * PIX, :].astype(F32)
        stat[0, f : f + 1] = jnp.sum(block, axis=0, keepdims=True)
    stat[0] = dot_exact(dot_exact(stat[0], fold[...]), unfold[...])
    for f in range(frames):
        block = x[f * PIX : (f + 1) * PIX, :].astype(F32) - stat[0, f : f + 1]
        stat[1, f : f + 1] = jnp.sum(block * block, axis=0, keepdims=True)
    variance = dot_exact(dot_exact(stat[1], fold[...]), unfold[...])
    stat[1] = lax.rsqrt(variance + GROUP_EPS)


def group_apply(x, stat, q, gain, out, act):
    for f in range(x.shape[0] // PIX):
        rows = slice(f * PIX, (f + 1) * PIX)
        v = (x[rows, :].astype(F32) - stat[0, f : f + 1]) * stat[1, f : f + 1]
        out[rows, :] = act(v * q[gain : gain + 1] + q[gain + 1 : gain + 2]).astype(out.dtype)


def group_matrices():
    group = jnp.arange(C) // (C // GROUPS)
    member = (group[:, None] == jnp.arange(128)[None, :]).astype(F32)
    return member / (C // GROUPS * PIX), member.T


def make_windows(x, win, flipped):
    tokens = x.shape[0]

    def body(j, carry):
        lanes = pl.ds(pl.multiple_of(j * 128, 128), 128)
        v = x[:, lanes]
        row = lax.broadcasted_iota(jnp.int32, v.shape, 0)
        py, px = row // SIDE % SIDE, row % SIDE
        for tap in range(9):
            dy, dx = tap // 3 - 1, tap % 3 - 1
            if flipped:
                dy, dx = -dy, -dx
            shift = (-(dy * SIDE + dx)) % tokens
            moved = pltpu.roll(v, shift, 0) if shift else v
            ok = (py + dy >= 0) & (py + dy < SIDE) & (px + dx >= 0) & (px + dx < SIDE)
            win[tap, :, lanes] = jnp.where(ok, moved, 0.0).astype(win.dtype)
        return carry

    lax.fori_loop(0, C // 128, body, 0)


def silu(v):
    return v / (1.0 + jnp.exp(-v))


def forward_kernel(jobs, needs, n_gather, n_out, *refs):
    ins, refs = refs[:n_gather], refs[n_gather:]
    lat, q, time_in, text, gate_bias, fold, unfold, sbias, cbias = refs[:9]
    outs, refs = refs[9 : 9 + n_out], refs[9 + n_out :]
    hid1, first, state0, state1, state2, second = refs[:6]
    self_q, self_k, self_v, cross_q, text_k, text_v, value_out, gate_out = refs[6:14]
    (
        send, recv, load_sem, store_sem, hold,
        bias_send, bias_recv, bias_all, col_sem, row_sem, save_sem,
        win, col_buf, row_buf, stage, acc, tmp, nrm, att, stat, extra,
    ) = refs[14:]
    (time_w, conv1, conv2, in_w, qkv_w, self_o, cross_w, text_w, cross_o, value_w, gate_w,
     down_w, out_w) = outs[:13]
    comm = Gather(jobs, ins, outs, send, recv, load_sem, store_sem, hold)
    greet(comm.peers())

    def bias_copy(j):
        return pltpu.make_async_remote_copy(
            src_ref=gate_bias,
            dst_ref=bias_all.at[comm.h],
            send_sem=bias_send.at[j],
            recv_sem=bias_recv.at[j],
            device_id=(comm.c, comm.heads[j]),
            device_id_type=MESH,
        )

    for j in (1, 2, 3):
        bias_copy(j).start()
    bias_all[comm.h] = gate_bias[...]

    def bias_in():
        for j in (1, 2, 3):
            bias_copy(j).wait()

    def time_unit():
        def sink(lanes, tile):
            extra[:, lanes] = tile + q[2:3, lanes] + q[3:4, lanes]

        through_tiles(time_in, time_w.at[0], col_buf, col_sem, sink)

    def act1_unit():
        group_stats(lat, fold, unfold, stat)
        group_apply(lat, stat, q, 0, tmp, silu)

    def windows_unit():
        make_windows(tmp, win, False)

    def conv_unit(w, tap):
        def sink(lanes, tile):
            if tap == 0:
                acc[:, lanes] = tile
            else:
                acc[:, lanes] += tile

        through_tiles(win.at[tap], w.at[tap], col_buf, col_sem, sink)

    def act2_unit():
        hid1[...] = acc[...] + extra[0:1]
        group_stats(hid1, fold, unfold, stat)
        group_apply(hid1, stat, q, 4, tmp, silu)

    def first_unit():
        first[...] = lat[...].astype(F32) + acc[...] + q[6:7]
        group_stats(first, fold, unfold, stat)
        group_apply(first, stat, q, 7, nrm, lambda v: v)

    def add_unit(x, w, base, bias, out, norm):
        def sink(lanes, tile):
            total = tile + q[bias : bias + 1, lanes]
            out[:, lanes] = total if base is None else total + base[:, lanes]

        through_tiles(x, w.at[0], col_buf, col_sem, sink)
        if norm is not None:
            norm_rows(out, q, norm, nrm)

    def project_unit(x, w, out):
        def sink(lanes, tile):
            out[:, lanes] = tile.astype(BF)

        against_tiles(x, w, row_buf, row_sem, sink)

    def attend_unit(qr, kr, vr, bias):
        attend_body(qr, kr, vr, bias, att, tmp)

    def save(i, k):
        dst = (value_out, gate_out)[k].at[:, tile_at(i)]
        return pltpu.make_async_copy(stage.at[i % 2, k], dst, save_sem.at[i % 2, k])

    def ffn_unit(part, parts):
        per = value_w.shape[1] // TILE // parts
        start = part * per

        def tiles(i, slot):
            rows = tile_at(start + i)
            return [
                (value_w.at[0, rows], row_buf.at[slot * 3]),
                (gate_w.at[0, rows], row_buf.at[slot * 3 + 1]),
                (down_w.at[0, rows], row_buf.at[slot * 3 + 2]),
            ]

        def body(i, slot):
            tile = start + i
            lanes = tile_at(tile % 5)
            z = tile // 5
            x = nrm[...]
            value = dot_f32(x, row_buf[slot * 3], ((1,), (1,))) + bias_all[z, 0:1, lanes]
            gate = dot_f32(x, row_buf[slot * 3 + 1], ((1,), (1,))) + bias_all[z, 1:2, lanes]
            mixed = (value * gelu_erf(gate)).astype(BF)

            @pl.when(tile >= 2)
            def _():
                save(tile - 2, 0).wait()
                save(tile - 2, 1).wait()

            stage[tile % 2, 0] = value.astype(BF)
            stage[tile % 2, 1] = gate.astype(BF)
            save(tile, 0).start()
            save(tile, 1).start()
            acc[...] += dot_f32(mixed, row_buf[slot * 3 + 2], ((1,), (0,)))

        if part == 0:
            acc[...] = state2[...] + q[18:19]
        stream(per, tiles, body, row_sem, 2)
        if part == parts - 1:
            for tile in (value_w.shape[1] // TILE - 2, value_w.shape[1] // TILE - 1):
                save(tile, 0).wait()
                save(tile, 1).wait()
            nrm[...] = acc[...].astype(BF)

    P_ = functools.partial
    units = [(0, act1_unit), (0, windows_unit), (needs["time"], time_unit)]
    units += [(needs["conv1", t], P_(conv_unit, conv1, t)) for t in range(9)]
    units += [(0, act2_unit), (0, windows_unit)]
    units += [(needs["conv2", t], P_(conv_unit, conv2, t)) for t in range(9)]
    units += [(0, first_unit)]
    units += [(needs["in"], P_(add_unit, nrm, in_w, None, 9, state0, 10))]
    units += [
        (needs["qkv"], P_(project_unit, nrm, qkv_w.at[i], o))
        for i, o in enumerate((self_q, self_k, self_v))
    ]
    units += [(0, P_(attend_unit, self_q, self_k, self_v, sbias))]
    units += [(needs["self_o"], P_(add_unit, att, self_o, state0, 12, state1, 13))]
    units += [(needs["cross"], P_(project_unit, nrm, cross_w.at[0], cross_q))]
    units += [(needs["text"], P_(project_unit, text, text_w.at[0], text_k))]
    units += [(needs["text"], P_(project_unit, text, text_w.at[1], text_v))]
    units += [(0, P_(attend_unit, cross_q, text_k, text_v, cbias))]
    units += [(needs["cross_o"], P_(add_unit, att, cross_o, state1, 15, state2, 16))]
    units += [(0, bias_in)]
    units += [(needs["ffn"], P_(ffn_unit, i, 5)) for i in range(5)]
    units += [(needs["out"], P_(add_unit, nrm, out_w, first, 19, second, None))]
    comm.run(units)


def forward_fused(arrays, small, projections, feedforward, lat, q, time_in, text, gate_bias, masks):
    tokens = lat.shape[0]
    square = projections.astype(BF).reshape(5, 2, 2, 2, 80, 160).transpose(0, 1, 3, 2, 4, 5)
    wide = feedforward.astype(BF).reshape(2, 2, 2, 320, 160).transpose(0, 2, 1, 3, 4)
    square = lax.all_to_all(square.reshape(5, 8, 80, 160), "clip", 1, 3, tiled=True)
    wide = lax.all_to_all(wide.reshape(8, 320, 160), "clip", 0, 2, tiled=True)
    ins = arrays + [square.reshape(5, 80, C), wide.reshape(1, 320, C), small[None]]
    shapes, jobs, needs = [], [], {}
    names = ["time", "conv1", "conv2", "in", "qkv", "self_o", "cross", "text", "cross_o"]
    names += ["value", "gate", "ffn", "out"]
    for o, (i, lo, n) in enumerate(FROZEN):
        rows, cols = ins[i].shape[1:]
        shapes.append((n, 4 * rows, cols))
        step = 3 if n == 9 else n
        for at in range(0, n, step):
            jobs.append(("frozen", i, o, lo + at, at, step))
            if n == 9:
                for t in range(at, at + step):
                    needs[names[o], t] = len(jobs)
        needs[names[o]] = len(jobs)
    shapes += [(5, 2, C, C), (1, 2, 4 * C, C), (1, 2, 16 * small.shape[0], C)]
    jobs += [("own", 7, 15, 0, 0, 1), ("own", 5, 13, 0, 0, 2), ("own", 5, 13, 2, 2, 3)]
    jobs += [("own", 6, 14, 0, 0, 1)]
    count = len(jobs)
    most = max(j[5] * ins[j[1]].shape[1] for j in jobs)
    any_spec, vmem = pl.BlockSpec(memory_space=pl.ANY), pl.BlockSpec(memory_space=pltpu.VMEM)
    wide_f32 = jax.ShapeDtypeStruct((tokens, C), F32)
    wide_bf = jax.ShapeDtypeStruct((tokens, C), BF)
    text_bf = jax.ShapeDtypeStruct((text.shape[0], C), BF)
    hidden = jax.ShapeDtypeStruct((tokens, 4 * C), BF)
    fold, unfold = group_matrices()
    dma = pltpu.SemaphoreType.DMA
    outs = pl.pallas_call(
        functools.partial(forward_kernel, jobs, needs, len(ins), len(shapes)),
        out_shape=tuple(jax.ShapeDtypeStruct(shape, BF) for shape in shapes)
        + (wide_f32,) * 6
        + (wide_bf,) * 4
        + (text_bf,) * 2
        + (hidden,) * 2,
        in_specs=[any_spec] * len(ins) + [vmem] * 9,
        out_specs=(any_spec,) * len(shapes) + (vmem,) * 12 + (any_spec,) * 2,
        scratch_shapes=[
            dma((count, 4, 6)),
            dma((count, 4, 6)),
            dma((count, 4)),
            dma((count, 4)),
            pltpu.VMEM((2, most, C), BF),
            dma((4,)),
            dma((4,)),
            pltpu.VMEM((4, 8, C), F32),
            dma((3, 1)),
            dma((6, 3)),
            dma((2, 2)),
            pltpu.VMEM((9, tokens, C), BF),
            pltpu.VMEM((3, C, TILE), BF),
            pltpu.VMEM((6, TILE, C), BF),
            pltpu.VMEM((2, 2, tokens, TILE), BF),
            pltpu.VMEM((tokens, C), F32),
            pltpu.VMEM((tokens, C), F32),
            pltpu.VMEM((tokens, C), BF),
            pltpu.VMEM((tokens, C), BF),
            pltpu.VMEM((2, 8, C), F32),
            pltpu.VMEM((16, C), F32),
        ],
        compiler_params=pltpu.CompilerParams(
            collective_id=1, has_side_effects=True, vmem_limit_bytes=60 << 20
        ),
    )(
        *ins,
        lat,
        jnp.pad(q, ((0, 4), (0, 0))),
        jnp.pad(time_in, ((0, 15), (0, 0))),
        text,
        jnp.pad(gate_bias, ((0, 6), (0, 0))),
        fold,
        unfold,
        *masks,
    )
    frozen, saved = outs[:13], outs[16:]
    packed = outs[15].reshape(2, 4, 2, 2, -1).transpose(0, 3, 2, 1, 4)
    trained = [outs[13].reshape(10, C, C), outs[14].reshape(2, 4 * C, C)]
    return frozen, trained, packed.reshape(8, 4, -1), saved


def pack_small(vectors, up_bias):
    flat = jnp.concatenate([a.astype(BF).reshape(-1) for a in (vectors, up_bias)])
    return jnp.pad(flat, (0, 32 * C - flat.shape[0])).reshape(32, C)


def unpack_small(sizes, packed, vectors, up_bias):
    packed = packed.reshape(sizes[0], sizes[1], -1).astype(F32)
    vector = packed[:, 0, : vectors.size].reshape((sizes[0],) + vectors.shape)
    bias = packed[:, :, vectors.size : vectors.size + up_bias.size]
    bias = bias.reshape(sizes + up_bias.shape).transpose(1, 2, 0, 3)
    return vector.transpose(1, 0, 2).reshape(vectors.shape[0], C), bias.reshape(1, -1)


CHUNKS = 9


def sum_kernel(*refs):
    grads = refs[:12]
    out, landed = refs[12:14]
    total, own, got_x, got_y, got2, got3, send, recv, load_sem = refs[14:]
    c, h, core, gx, gy, partners, heads = place()
    xp, yp, cp = partners["x"], partners["y"], partners["core"]
    greet([xp, yp, cp] + [(c, heads[j]) for j in (1, 2, 3)])
    slots, loads = total.shape[0], own.shape[0]

    def block(k, y):
        if k < 5:
            return grads[2 * k + y]
        return grads[10 + y].at[:, :, :, k - 5]

    def copy(k, kind, src, dst, device):
        return pltpu.make_async_remote_copy(
            src_ref=src,
            dst_ref=dst,
            send_sem=send.at[k, kind],
            recv_sem=recv.at[k, kind],
            device_id=device,
            device_id_type=MESH,
        )

    def core_copies(k):
        return [copy(k, y, block(k, y).at[:, 1 - core], landed.at[k, y], cp) for y in (0, 1)]

    def load_copies(k):
        copies = [(landed.at[k], total.at[k % slots], 0)]
        for y in (0, 1):
            copies.append((block(k, y).at[:, core], own.at[k % loads, y], 1 + y))
        return [pltpu.make_async_copy(src, dst, load_sem.at[k, i]) for src, dst, i in copies]

    def first_copy(k):
        held = total.at[k % slots]
        if k % 2 == 0:
            return copy(k, 2, held.at[:, :, 1 - gx], got_x.at[k // 2], xp)
        return copy(k, 2, held.at[1 - gy], got_y.at[k // 2], yp)

    def second_copy(k):
        if k % 2 == 0:
            return copy(k, 3, got_x.at[k // 2, 1 - gy], got2.at[k], yp)
        return copy(k, 3, got_y.at[k // 2, :, 1 - gx], got2.at[k], xp)

    def last_copies(k):
        return [
            copy(k, 3 + j, got2.at[k, heads[j]], got3.at[k, j - 1], (c, heads[j]))
            for j in (1, 2, 3)
        ]

    def exchange(k):
        for item in core_copies(k):
            item.start()

    def load(k):
        for item in core_copies(k):
            item.wait_recv()
        if k >= slots:
            first_copy(k - slots).wait_send()
        for item in load_copies(k):
            item.start()

    def add_core(k):
        for item in load_copies(k):
            item.wait()
        slot, near = k % slots, k % loads

        def body(i, carry):
            y, z, x = i // 8, i // 2 % 4, i % 2
            total[slot, y, z, x] = total[slot, y, z, x] + own[near, y, z, x]
            return carry

        lax.fori_loop(0, 16, body, 0)
        first_copy(k).start()

    def add_first(k):
        first_copy(k).wait_recv()
        slot, at = k % slots, k // 2

        def body(i, carry):
            if k % 2 == 0:
                y, z = i // 4, i % 4
                got_x[at, y, z] = got_x[at, y, z] + total[slot, y, z, gx]
            else:
                z, x = i // 2, i % 2
                got_y[at, z, x] = got_y[at, z, x] + total[slot, gy, z, x]
            return carry

        lax.fori_loop(0, 8, body, 0)
        second_copy(k).start()

    def add_second(k):
        second_copy(k).wait_recv()
        at = k // 2

        def body(z, carry):
            if k % 2 == 0:
                got2[k, z] = got2[k, z] + got_x[at, gy, z]
            else:
                got2[k, z] = got2[k, z] + got_y[at, z, gx]
            return carry

        lax.fori_loop(0, 4, body, 0)
        for item in last_copies(k):
            item.start()

    def add_last(k):
        for item in last_copies(k):
            item.wait()
        rest = got3[k, 0].astype(F32) + got3[k, 1].astype(F32) + got3[k, 2].astype(F32)
        out[k] = got2[k, h].astype(F32) + rest

    for k in range(CHUNKS):
        exchange(k)
    load(0)
    for step in range(CHUNKS + 4):
        if step + 1 < CHUNKS:
            load(step + 1)
        if step < CHUNKS:
            add_core(step)
        if 0 <= step - 2 < CHUNKS:
            add_first(step - 2)
        if 0 <= step - 3 < CHUNKS:
            add_second(step - 3)
        if 0 <= step - 4 < CHUNKS:
            add_last(step - 4)
    for k in range(CHUNKS):
        for item in core_copies(k):
            item.wait_send()
        if k >= CHUNKS - slots:
            first_copy(k).wait_send()
        second_copy(k).wait_send()


def sum_square(sizes, parts, wide_parts):
    if sizes != (8, 4):
        return [
            jnp.stack(
                [
                    lax.psum_scatter(
                        lax.psum_scatter(g, "head", scatter_dimension=0, tiled=True),
                        "clip",
                        scatter_dimension=1,
                        tiled=True,
                    ).astype(F32)
                    for g in a
                ]
            )
            for a in (parts, wide_parts)
        ]
    ins = [g.reshape(4, 2, 2, 80, C) for g in parts]
    ins += [g.reshape(4, 2, 2, 4, 80, C) for g in wide_parts]
    own, _ = pl.pallas_call(
        sum_kernel,
        out_shape=(
            jax.ShapeDtypeStruct((CHUNKS, 80, C), F32),
            jax.ShapeDtypeStruct((CHUNKS, 2, 4, 2, 80, C), BF),
        ),
        in_specs=[pl.BlockSpec(memory_space=pl.ANY)] * 12,
        out_specs=(pl.BlockSpec(memory_space=pltpu.VMEM), pl.BlockSpec(memory_space=pl.ANY)),
        scratch_shapes=[
            pltpu.VMEM((4, 2, 4, 2, 80, C), BF),
            pltpu.VMEM((2, 2, 4, 2, 80, C), BF),
            pltpu.VMEM((5, 2, 4, 80, C), BF),
            pltpu.VMEM((4, 4, 2, 80, C), BF),
            pltpu.VMEM((CHUNKS, 4, 80, C), BF),
            pltpu.VMEM((CHUNKS, 3, 80, C), BF),
            pltpu.SemaphoreType.DMA((CHUNKS, 7)),
            pltpu.SemaphoreType.DMA((CHUNKS, 7)),
            pltpu.SemaphoreType.DMA((CHUNKS, 3)),
        ],
        compiler_params=pltpu.CompilerParams(
            collective_id=3, has_side_effects=True, vmem_limit_bytes=56 << 20
        ),
    )(*ins)
    own = own.astype(BF)
    square = lax.all_to_all(own[None, :5], "clip", 3, 0, tiled=True)
    wide = lax.all_to_all(own[5:].reshape(1, 320, C), "clip", 2, 0, tiled=True)
    square = square.reshape(2, 2, 2, 5, 80, 160).transpose(3, 0, 2, 1, 4, 5)
    wide = wide.reshape(2, 2, 2, 320, 160).transpose(0, 2, 1, 3, 4)
    return square.reshape(10, 320, 160).astype(F32), wide.reshape(2, C, 160).astype(F32)


def head_window(head):
    start = head * HD // 128 * 128
    return start, head * HD - start


def lane_mask(shape, low):
    lane = lax.broadcasted_iota(jnp.int32, shape, 1)
    return (lane >= low) & (lane < low + HD)


def dot_f32(a, b, dims):
    return lax.dot_general(a, b, (dims, ((), ())), preferred_element_type=F32)


def head_probs(q, k, bias):
    scores = dot_f32(q, k, ((1,), (1,))) * HD ** (-0.5) + bias
    top = jnp.max(scores, axis=1, keepdims=True)
    weights = jnp.exp(scores - top)
    return weights / jnp.sum(weights, axis=1, keepdims=True)


def attend_body(q_ref, k_ref, v_ref, bias_ref, o_ref, acc):
    acc[...] = jnp.zeros_like(acc)
    for head in range(HEADS):
        start, low = head_window(head)
        win = pl.ds(start, 256)
        q = q_ref[:, win]
        mask = lane_mask(q.shape, low)
        q = jnp.where(mask, q, jnp.zeros_like(q))
        probs = head_probs(q, k_ref[:, win], bias_ref[...])
        out = dot_f32(probs.astype(BF), v_ref[:, win], ((1,), (0,)))
        acc[:, win] += jnp.where(mask, out, 0.0)
    o_ref[...] = acc[...].astype(BF)


def attend(q, k, v, bias):
    return pl.pallas_call(
        attend_body,
        out_shape=jax.ShapeDtypeStruct(q.shape, BF),
        scratch_shapes=[pltpu.VMEM(q.shape, F32)],
        compiler_params=pltpu.CompilerParams(vmem_limit_bytes=40 << 20),
    )(q, k, v, bias)


def attend_back_kernel(with_keys, q_ref, k_ref, v_ref, bias_ref, g_ref, *refs):
    if with_keys:
        dq_ref, dk_ref, dv_ref, dq, dk, dv = refs
        dk[...] = jnp.zeros_like(dk)
        dv[...] = jnp.zeros_like(dv)
    else:
        dq_ref, dq = refs
    dq[...] = jnp.zeros_like(dq)
    for head in range(HEADS):
        start, low = head_window(head)
        win = pl.ds(start, 256)
        q, k, v, g = q_ref[:, win], k_ref[:, win], v_ref[:, win], g_ref[:, win]
        mask = lane_mask(q.shape, low)
        q = jnp.where(mask, q, jnp.zeros_like(q))
        g = jnp.where(mask, g, jnp.zeros_like(g))
        probs = head_probs(q, k, bias_ref[...])
        dp = dot_f32(g, v, ((1,), (1,)))
        ds = probs * (dp - jnp.sum(dp * probs, axis=1, keepdims=True)) * HD ** (-0.5)
        ds = ds.astype(BF)
        dq[:, win] += jnp.where(mask, dot_f32(ds, k, ((1,), (0,))), 0.0)
        if with_keys:
            dk[:, win] += dot_f32(ds, q, ((0,), (0,)))
            dv[:, win] += dot_f32(probs.astype(BF), g, ((0,), (0,)))
    dq_ref[...] = dq[...].astype(BF)
    if with_keys:
        dk_ref[...] = dk[...].astype(BF)
        dv_ref[...] = dv[...].astype(BF)


def attend_back(q, k, v, bias, g, with_keys=True):
    count = 3 if with_keys else 1
    return pl.pallas_call(
        functools.partial(attend_back_kernel, with_keys),
        out_shape=(jax.ShapeDtypeStruct(q.shape, BF),) * count,
        scratch_shapes=[pltpu.VMEM(q.shape, F32)] * count,
        compiler_params=pltpu.CompilerParams(vmem_limit_bytes=48 << 20),
    )(q, k, v, bias, g)


def group_mean(per_channel):
    width = C // GROUPS
    means = jnp.mean(per_channel.reshape(-1, GROUPS, width), axis=-1) / PIX
    return jnp.repeat(means, width, axis=1)[:, None, :]


def gn_stats(x):
    center = group_mean(jnp.sum(x, axis=1))
    centered = x - center
    variance = group_mean(jnp.sum(centered * centered, axis=1))
    return center, lax.rsqrt(variance + GROUP_EPS)


def gn(x, stats, gain, shift):
    return (x - stats[0]) * stats[1] * gain + shift


def gn_back(dy, x, stats, gain):
    z = (x - stats[0]) * stats[1]
    gd = dy * gain
    mean_gd = group_mean(jnp.sum(gd, axis=1))
    mean_gz = group_mean(jnp.sum(gd * z, axis=1))
    return (gd - mean_gd - z * mean_gz) * stats[1]


def ln_stats(x):
    center = jnp.mean(x, axis=-1, keepdims=True)
    centered = x - center
    variance = jnp.mean(centered * centered, axis=-1, keepdims=True)
    return center, lax.rsqrt(variance + LAYER_EPS)


def ln(x, stats, gain, shift):
    return (x - stats[0]) * stats[1] * gain + shift


def ln_back(dy, x, stats, gain):
    z = (x - stats[0]) * stats[1]
    gd = dy * gain
    mean_gd = jnp.mean(gd, axis=-1, keepdims=True)
    mean_gz = jnp.mean(gd * z, axis=-1, keepdims=True)
    return (gd - mean_gd - z * mean_gz) * stats[1]


def ln_param_grads(dy, x, stats):
    z = (x - stats[0]) * stats[1]
    return jnp.sum(dy * z, axis=0), jnp.sum(dy, axis=0)


def silu_back(dy, v):
    gate = jax.nn.sigmoid(v)
    return dy * gate * (1.0 + v * (1.0 - gate))


def gelu_exact(v):
    return jax.nn.gelu(v, approximate=False)


def gelu_erf(v):
    return 0.5 * v * (1.0 + lax.erf(v * math.sqrt(0.5)))


def gelu_exact_slope(v):
    density = jnp.exp(-0.5 * v * v) * (1.0 / math.sqrt(2.0 * math.pi))
    return 0.5 * (1.0 + lax.erf(v * math.sqrt(0.5))) + v * density


def gelu_tanh(v):
    return jax.nn.gelu(v, approximate=True)


def gelu_tanh_slope(v):
    k = math.sqrt(2.0 / math.pi)
    t = jnp.tanh(k * (v + 0.044715 * v * v * v))
    return 0.5 * (1.0 + t) + 0.5 * v * (1.0 - t * t) * k * (1.0 + 3.0 * 0.044715 * v * v)


def frame_table():
    frame_pos = jnp.arange(FMAX, dtype=F32)[:, None]
    channel = jnp.arange(C)
    frequency = jnp.exp((channel - channel % 2).astype(F32) * (-math.log(10000.0) / C))
    angles = frame_pos * frequency[None, :]
    return jnp.where(channel[None, :] % 2 == 0, jnp.sin(angles), jnp.cos(angles))


def time_table(timesteps):
    half_width = C // 2
    frequency = jnp.exp(jnp.arange(half_width, dtype=F32) * (-math.log(10000.0) / half_width))
    angles = timesteps.astype(F32)[:, None] * frequency[None, :]
    return jnp.concatenate([jnp.cos(angles), jnp.sin(angles)], axis=1)


def through(x, w):
    return dot_f32(x, w, ((1,), (0,)))


def against(x, w):
    return dot_f32(x, w, ((1,), (1,)))


def outer(a, b):
    return dot_f32(a, b, ((0,), (0,))).astype(BF)


def windows(x, flipped):
    frames = x.shape[0]
    padded = jnp.pad(x.reshape(frames, SIDE, SIDE, C), ((0, 0), (1, 1), (1, 1), (0, 0)))
    pieces = []
    for tap in range(9):
        dy, dx = tap // 3, tap % 3
        if flipped:
            dy, dx = 2 - dy, 2 - dx
        pieces.append(padded[:, dy : dy + SIDE, dx : dx + SIDE].reshape(frames * PIX, C))
    return pieces


def conv(x, w):
    return through(jnp.concatenate(windows(x, False), axis=1), w.reshape(9 * C, C))


def conv_back(g, w):
    stacked = jnp.stack(windows(g, True), axis=1)
    return lax.dot_general(
        stacked, w, (((1, 2), (0, 2)), ((), ())), preferred_element_type=F32
    )


def update(weight, moment, average, gradient, step_rate):
    moment_new = MOMENTUM * moment + gradient
    weight_new = weight - step_rate * (gradient + MOMENTUM * moment_new)
    average_new = AVERAGE_DECAY * average + (1.0 - AVERAGE_DECAY) * weight_new
    return (moment_new, average_new, weight_new)


def forward_plain(frozen, x0, Q, time_in, text, geglu_bias, spatial_bias, cross_bias):
    time_w, conv1_w, conv2_w, in_w, self_w, self_o, cross_qw, cross_w, cross_o = frozen[:9]
    ffn_value, ffn_gate, ffn_down, out_w = frozen[9:]
    geglu_f = lax.all_gather(geglu_bias, "head", axis=1, tiled=True)

    def flat(x):
        return x.reshape(-1, C)

    act1 = silu(gn(x0, gn_stats(x0), Q[0], Q[1])).astype(BF)
    hid1 = (conv(act1, conv1_w) + through(time_in, time_w[0]) + Q[2] + Q[3]).reshape(x0.shape)
    act2 = silu(gn(hid1, gn_stats(hid1), Q[4], Q[5])).astype(BF)
    first = x0 + conv(act2, conv2_w).reshape(x0.shape) + Q[6]
    spatial_in = flat(gn(first, gn_stats(first), Q[7], Q[8]).astype(BF))
    state0 = through(spatial_in, in_w[0]) + Q[9]
    norm1 = ln(state0, ln_stats(state0), Q[10], Q[11]).astype(BF)
    self_q, self_k, self_v = (against(norm1, self_w[i]).astype(BF) for i in range(3))
    self_att = attend(self_q, self_k, self_v, spatial_bias)
    state1 = state0 + through(self_att, self_o[0]) + Q[12]
    norm2 = ln(state1, ln_stats(state1), Q[13], Q[14]).astype(BF)
    cross_q = against(norm2, cross_qw[0]).astype(BF)
    text_k, text_v = (against(text, cross_w[i]).astype(BF) for i in (0, 1))
    cross_att = attend(cross_q, text_k, text_v, cross_bias)
    state2 = state1 + through(cross_att, cross_o[0]) + Q[15]
    norm3 = ln(state2, ln_stats(state2), Q[16], Q[17]).astype(BF)
    value_in = (against(norm3, ffn_value[0]) + geglu_f[0]).astype(BF)
    gate_in = (against(norm3, ffn_gate[0]) + geglu_f[1]).astype(BF)
    mixed = (value_in.astype(F32) * gelu_erf(gate_in.astype(F32))).astype(BF)
    state3 = (state2 + through(mixed, ffn_down[0]) + Q[18]).astype(BF)
    second = flat(first) + through(state3, out_w[0]) + Q[19]
    states = (flat(hid1), flat(first), state0, state1, state2, second)
    return states + (self_q, self_k, self_v, cross_q, text_k, text_v, value_in, gate_in)


def per_device(
    sizes,
    latents,
    cotangent,
    frames,
    timesteps,
    text,
    conv_weight,
    time_weight,
    frozen_params,
    spatial_square,
    cross_kv,
    spatial_ffn,
    geglu_bias,
    projections,
    feedforward,
    up_bias,
    vectors,
    projections_moment,
    feedforward_moment,
    up_bias_moment,
    vectors_moment,
    projections_average,
    feedforward_average,
    up_bias_average,
    vectors_average,
):
    Q = frozen_params
    n_head = sizes[1]
    head_index = lax.axis_index("head")
    clip_index = lax.axis_index("clip")
    own_frames = latents.shape[1]
    tokens = own_frames * PIX
    own_pixels = PIX // n_head
    columns = FMAX * own_pixels

    def framed(x):
        return x.reshape(own_frames, PIX, C)

    def flat(x):
        return x.reshape(tokens, C)

    def to_pixels(x):
        x = lax.all_to_all(framed(x), "head", 1, 0, tiled=True)
        return x.reshape(columns, C)

    def to_frames(x):
        x = lax.all_to_all(x.reshape(FMAX, own_pixels, C), "head", 0, 1, tiled=True)
        return x.reshape(tokens, C)

    frame_of = jnp.arange(tokens) // PIX
    spatial_bias = jnp.where(frame_of[:, None] == frame_of[None, :], 0.0, MASK_FILL).astype(F32)
    column = jnp.arange(columns)
    same_pixel = (column % own_pixels)[:, None] == (column % own_pixels)[None, :]
    key_there = (column // own_pixels)[None, :] < frames[0]
    temporal_bias = jnp.where(same_pixel & key_there, 0.0, MASK_FILL).astype(F32)
    text_len = text.shape[1]
    text_rows = 128
    cross_bias = jnp.broadcast_to(
        jnp.where(jnp.arange(text_rows)[None, :] < text_len, 0.0, MASK_FILL), (tokens, text_rows)
    ).astype(F32)
    codes = jnp.repeat(frame_table(), own_pixels, axis=0)
    own_frame = head_index * own_frames + jnp.arange(own_frames)
    frame_mask = (own_frame < frames[0]).astype(F32)[:, None, None]

    x0 = latents[0].astype(F32)
    grad_out = frame_mask * cotangent[0].astype(F32)
    arrays = frozen_arrays(conv_weight, time_weight, spatial_square, cross_kv, spatial_ffn)
    small = pack_small(vectors, up_bias)
    time_in = jax.nn.silu(time_table(timesteps)).astype(BF)
    text_pad = jnp.pad(text[0], ((0, text_rows - text_len), (0, 0)))
    if sizes == (8, 4):
        frozen, trained, small, saved = forward_fused(
            arrays,
            small,
            projections,
            feedforward,
            latents.reshape(tokens, C),
            Q,
            time_in,
            text_pad,
            geglu_bias,
            (spatial_bias, cross_bias),
        )
    else:
        frozen, trained, small = gather_plain(arrays, small, projections, feedforward)
        saved = forward_plain(
            frozen, x0, Q, time_in, text_pad, geglu_bias, spatial_bias, cross_bias
        )
    time_w, conv1_w, conv2_w, in_w, self_w, self_o, cross_qw, cross_w, cross_o = frozen[:9]
    ffn_value, ffn_gate, ffn_down, out_w = frozen[9:]
    square_w, ffn_w = trained
    vector_f, bias_f = unpack_small(sizes, small, vectors, up_bias)
    hid1, first, state0, state1, state2, second = saved[:6]
    self_q, self_k, self_v, cross_q, text_k, text_v, value_in, gate_in = saved[6:]
    hid1, first, second = framed(hid1), framed(first), framed(second)
    value_in, gate_in = value_in.astype(F32), gate_in.astype(F32)

    stats3 = gn_stats(second)
    normed = to_pixels(gn(second, stats3, vector_f[0], vector_f[1]).astype(BF))
    entered = through(normed, square_w[0]) + vector_f[2]

    def temporal_in(x, gain_row, wq):
        stats = ln_stats(x)
        t = (ln(x, stats, vector_f[gain_row], vector_f[gain_row + 1]) + codes).astype(BF)
        qkv = [against(t, square_w[wq + i]).astype(BF) for i in range(3)]
        return stats, t, qkv

    tl1, t1, qkv1 = temporal_in(entered, 3, 3)
    att1 = attend(*qkv1, temporal_bias)
    block1 = entered + through(att1, square_w[1]) + vector_f[5]
    tl2, t2, qkv2 = temporal_in(block1, 6, 7)
    att2 = attend(*qkv2, temporal_bias)
    block2 = block1 + through(att2, square_w[6]) + vector_f[8]
    tl3 = ln_stats(block2)
    t3 = ln(block2, tl3, vector_f[9], vector_f[10]).astype(BF)
    inner = against(t3, ffn_w[0]) + bias_f
    spread = gelu_tanh(inner).astype(BF)
    stream = (block2 + through(spread, ffn_w[1]) + vector_f[11]).astype(BF)
    moved = to_frames(through(stream, square_w[2]).astype(BF)).astype(F32)
    output = (frame_mask * (second + framed(moved) + vector_f[12])).astype(BF)[None]

    g_out = to_pixels(grad_out.astype(BF))
    col = lambda v: jnp.sum(v.astype(F32), axis=0)
    G = {}
    G[2] = outer(stream, g_out)
    grad_stream = against(g_out, square_w[2])
    g_ffn = grad_stream.astype(BF)
    grad_down = outer(spread, g_ffn)
    g_inner = (gelu_tanh_slope(inner) * against(g_ffn, ffn_w[1])).astype(BF)
    grad_up = outer(g_inner, t3)
    grad_t3 = through(g_inner, ffn_w[0])
    grad_b2 = grad_stream + ln_back(grad_t3, block2, tl3, vector_f[9])
    dgain3, dshift3 = ln_param_grads(grad_t3, block2, tl3)

    def temporal_back(grad, x, stats, t, qkv, att, gain_row, wo, wq):
        low = grad.astype(BF)
        G[wo] = outer(att, low)
        dqkv = attend_back(*qkv, temporal_bias, against(low, square_w[wo]).astype(BF))
        for i in range(3):
            G[wq + i] = outer(dqkv[i], t)
        grad_t = sum(through(dqkv[i], square_w[wq + i]) for i in range(3))
        grad_x = grad + ln_back(grad_t, x, stats, vector_f[gain_row])
        return grad_x, ln_param_grads(grad_t, x, stats), col(low)

    grad_b1, (dgain2, dshift2), dbias2 = temporal_back(
        grad_b2, block1, tl2, t2, qkv2, att2, 6, 6, 7
    )
    grad_e, (dgain1, dshift1), dbias1 = temporal_back(
        grad_b1, entered, tl1, t1, qkv1, att1, 3, 1, 3
    )
    g_entry = grad_e.astype(BF)
    G[0] = outer(normed, g_entry)
    grad_normed = framed(to_frames(against(g_entry, square_w[0]).astype(BF)).astype(F32))
    z = (second - stats3[0]) * stats3[1]
    dgain0 = jnp.sum(grad_normed * z, axis=(0, 1))
    dshift0 = jnp.sum(grad_normed, axis=(0, 1))
    grad_second = grad_out + gn_back(grad_normed, second, stats3, vector_f[0])

    grad_vector = jnp.stack(
        [
            dgain0,
            dshift0,
            col(g_entry),
            dgain1,
            dshift1,
            dbias1,
            dgain2,
            dshift2,
            dbias2,
            dgain3,
            dshift3,
            col(g_ffn),
            col(g_out),
        ]
    )
    small = jnp.concatenate([grad_vector.reshape(-1), col(g_inner)])
    small = lax.psum(small, ("clip", "head"))
    total_vector = small[: 13 * C].reshape(13, C)
    total_bias = small[13 * C :].reshape(-1, 128)
    own_vector = lax.dynamic_slice_in_dim(
        total_vector, clip_index * vectors.shape[1], vectors.shape[1], 1
    )
    own_bias = lax.dynamic_slice(
        total_bias,
        (head_index * up_bias.shape[0], clip_index * up_bias.shape[1]),
        up_bias.shape,
    )
    own_square, own_wide = sum_square(sizes, [G[i] for i in range(10)], [grad_up, grad_down])

    stats0, stats1, stats2 = gn_stats(x0), gn_stats(hid1), gn_stats(first)
    sl1, sl2, sl3 = ln_stats(state0), ln_stats(state1), ln_stats(state2)
    g_po = flat(grad_second).astype(BF)
    grad_s3 = against(g_po, out_w[0])
    g_fb = grad_s3.astype(BF)
    grad_mixed = against(g_fb, ffn_down[0])
    g_value = (gelu_exact(gate_in) * grad_mixed).astype(BF)
    g_gate = (value_in * gelu_exact_slope(gate_in) * grad_mixed).astype(BF)
    grad_n3 = through(g_value, ffn_value[0]) + through(g_gate, ffn_gate[0])
    grad_s2 = grad_s3 + ln_back(grad_n3, state2, sl3, Q[16])
    g_cb = grad_s2.astype(BF)
    (g_cq,) = attend_back(
        cross_q, text_k, text_v, cross_bias, against(g_cb, cross_o[0]).astype(BF), False
    )
    grad_s1 = grad_s2 + ln_back(through(g_cq, cross_qw[0]), state1, sl2, Q[13])
    g_sb = grad_s1.astype(BF)
    dself = attend_back(
        self_q, self_k, self_v, spatial_bias, against(g_sb, self_o[0]).astype(BF)
    )
    grad_n1 = sum(through(dself[i], self_w[i]) for i in range(3))
    grad_s0 = grad_s1 + ln_back(grad_n1, state0, sl1, Q[10])
    g_pi = grad_s0.astype(BF)
    grad_gn = framed(against(g_pi, in_w[0]))
    grad_first = grad_second + gn_back(grad_gn, first, stats2, Q[7])

    grad_act2 = framed(conv_back(grad_first.astype(BF), conv2_w))
    grad_n = silu_back(grad_act2, gn(hid1, stats1, Q[4], Q[5]))
    grad_hid1 = gn_back(grad_n, hid1, stats1, Q[4])
    grad_act1 = framed(conv_back(grad_hid1.astype(BF), conv1_w))
    grad_n = silu_back(grad_act1, gn(x0, stats0, Q[0], Q[1]))
    input_gradient = (grad_first + gn_back(grad_n, x0, stats0, Q[0])).astype(BF)[None]

    square_parts = update(
        projections, projections_moment, projections_average, own_square, RATE_MATRIX
    )
    ffn_parts = update(feedforward, feedforward_moment, feedforward_average, own_wide, RATE_MATRIX)
    bias_parts = update(up_bias, up_bias_moment, up_bias_average, own_bias, RATE_VECTOR)
    vector_parts = update(vectors, vectors_moment, vectors_average, own_vector, RATE_VECTOR)
    return (output, input_gradient) + square_parts + ffn_parts + bias_parts + vector_parts


def solution(mesh):
    sizes = (mesh.shape["clip"], mesh.shape["head"])
    return jax.shard_map(
        functools.partial(per_device, sizes),
        mesh=mesh,
        in_specs=(
            P("clip", "head", None, None),
            P("clip", "head", None, None),
            P("clip"),
            P("clip"),
            P("clip", None, None),
            P(None, None, "head", None),
            P("head", None),
            P(),
            P(None, "head", None),
            P(None, "head", None),
            P(None, "head", None),
            P(None, "head"),
            P(None, "head", "clip"),
            P(None, "head", "clip"),
            P("head", "clip"),
            P(None, "clip"),
            P(None, "head", "clip"),
            P(None, "head", "clip"),
            P("head", "clip"),
            P(None, "clip"),
            P(None, "head", "clip"),
            P(None, "head", "clip"),
            P("head", "clip"),
            P(None, "clip"),
        ),
        out_specs=(
            P("clip", "head", None, None),
            P("clip", "head", None, None),
            P(None, "head", "clip"),
            P(None, "head", "clip"),
            P(None, "head", "clip"),
            P(None, "head", "clip"),
            P(None, "head", "clip"),
            P(None, "head", "clip"),
            P("head", "clip"),
            P("head", "clip"),
            P("head", "clip"),
            P(None, "clip"),
            P(None, "clip"),
            P(None, "clip"),
        ),
        check_vma=False,
    )
```

```python
import functools
import math

import jax
import jax.numpy as jnp
from jax import lax
from jax.experimental import pallas as pl
from jax.experimental.pallas import tpu as pltpu
from jax.sharding import PartitionSpec as P

C = 1280
HD = 160
HEADS = C // HD
GROUPS = 32
FMAX = 24
SIDE = 8
PIX = 64
TEXT_LEN = 77
BF = jnp.bfloat16
F32 = jnp.float32
MESH = pl.DeviceIdType.MESH

MOMENTUM = 0.9
RATE_MATRIX = 0.0002
RATE_VECTOR = 0.002
AVERAGE_DECAY = 0.7
GROUP_EPS = 1e-06
LAYER_EPS = 1e-05
MASK_FILL = -1e30


def place():
    c = lax.axis_index("clip")
    h = lax.axis_index("head")
    core, gx, gy = c % 2, (c // 2) % 2, c // 4
    partners = {
        "x": (c + 2 - 4 * gx, h),
        "y": (c + 4 - 8 * gy, h),
        "core": (c + 1 - 2 * core, h),
    }
    heads = [h, h + 1 - 2 * (h % 2), h + 2 - 4 * (h // 2), 3 - h]
    return c, h, core, gx, gy, partners, heads


def greet(devices):
    barrier = pltpu.get_barrier_semaphore()
    for device in devices:
        pl.semaphore_signal(barrier, inc=1, device_id=device, device_id_type=MESH)
    pl.semaphore_wait(barrier, len(devices))


class Gather:

    def __init__(self, jobs, ins, outs, send, recv, load_sem, store_sem, hold):
        self.jobs = jobs
        self.sems = (send, recv, load_sem, store_sem)
        self.hold = hold
        c, h, core, gx, gy, partners, heads = place()
        self.c, self.h, self.core, self.gx, self.gy = c, h, core, gx, gy
        self.xp, self.yp, self.cp = partners["x"], partners["y"], partners["core"]
        self.heads = heads
        self.views = [self.view(job, ins, outs) for job in jobs]

    def peers(self):
        return [self.xp, self.yp, self.cp] + [(self.c, self.heads[j]) for j in (1, 2, 3)]

    def copy(self, a, j, kind, src, dst, device):
        return pltpu.make_async_remote_copy(
            src_ref=src,
            dst_ref=dst,
            send_sem=self.sems[0].at[a, j, kind],
            recv_sem=self.sems[1].at[a, j, kind],
            device_id=device,
            device_id_type=MESH,
        )

    def view(self, job, ins, outs):
        kind, i_ref, o_ref, lo, at, n = job[0], ins[job[1]], outs[job[2]], job[3], job[4], job[5]
        core, gx, gy, h = self.core, self.gx, self.gy, self.h
        part, into = pl.ds(lo, n), pl.ds(at, n)
        if kind == "frozen":
            shard = i_ref.shape[-2]
            rows = shard // 4
            half = o_ref.shape[-1] // 2
            lanes = pl.ds(pl.multiple_of(core * half, 128), half)
            src = i_ref.at[part, pl.ds(pl.multiple_of((gy * 2 + gx) * rows, 16), rows), lanes]

            def slot(z, y, x, n0=0, nn=n, r0=0, rr=rows):
                first = pl.multiple_of(z * shard + (y * 2 + x) * rows + r0, 16)
                return o_ref.at[pl.ds(at + n0, nn), pl.ds(first, rr), lanes]

            def bundle(z):
                return o_ref.at[into, pl.ds(pl.multiple_of(z * shard, 16), shard), lanes]

            own = pl.ds(pl.multiple_of(h * shard, 16), shard)
            local = [(i_ref.at[lo + i], o_ref.at[at + i, own]) for i in range(n)]
        else:
            rows = i_ref.shape[-2]
            src = i_ref.at[part]

            def slot(z, y, x, n0=0, nn=n, r0=0, rr=rows):
                first = pl.multiple_of(((z * 2 + core) * 2 + x) * rows + r0, 16)
                return o_ref.at[pl.ds(at + n0, nn), y, pl.ds(first, rr)]

            def bundle(z):
                first = pl.multiple_of((z * 2 + core) * 2 * rows, 16)
                return o_ref.at[into, :, pl.ds(first, 2 * rows)]

            here = pl.ds(pl.multiple_of(((h * 2 + core) * 2 + gx) * rows, 16), rows)
            local = [(i_ref.at[lo + i], o_ref.at[at + i, gy, here]) for i in range(n)]
        if n >= 4 or n == 2:
            first = dict(n0=0, nn=(n + 1) // 2)
            second = dict(n0=(n + 1) // 2, nn=n - (n + 1) // 2)
        else:
            top = (rows // 2 + 15) // 16 * 16
            first, second = dict(r0=0, rr=top), dict(r0=top, rr=rows - top)
        return kind, src, slot, bundle, local, first, second

    def local_copies(self, a):
        buf = self.hold.at[a % self.hold.shape[0]]
        triples = []
        for i, (src, dst) in enumerate(self.views[a][4]):
            rows, cols = src.shape
            triples.append((src, buf.at[pl.ds(i * rows, rows), pl.ds(0, cols)], dst))
        return triples

    def numbers(self, a):
        return (1, 2, 3) if self.views[a][0] == "frozen" else (0, 1, 2, 3)

    def fetch(self, a):
        src, slot = self.views[a][1:3]
        for j in (1, 2, 3):
            there = (self.c, self.heads[j])
            self.copy(a, j, 0, src, slot(self.h, self.gy, self.gx), there).start()

    def trade(self, a):
        src, slot = self.views[a][1:3]
        locals_ = self.local_copies(a)
        for k, (inp, mid, out) in enumerate(locals_):
            pltpu.make_async_copy(inp, mid, self.sems[2].at[a, k]).start()
        for j in self.numbers(a):
            here = slot(self.heads[j], self.gy, self.gx)
            if j:
                self.copy(a, j, 0, src, here, (self.c, self.heads[j])).wait_recv()
            give = here if j else src
            self.copy(a, j, 1, give, here, self.xp).start()
            self.copy(a, j, 2, give, here, self.yp).start()
        for k, (inp, mid, out) in enumerate(locals_):
            pltpu.make_async_copy(inp, mid, self.sems[2].at[a, k]).wait()
            pltpu.make_async_copy(mid, out, self.sems[3].at[a, k]).start()

    def forward(self, a):
        kind, src, slot, bundle, local, first, second = self.views[a]
        gx, gy, xp, yp = self.gx, self.gy, self.xp, self.yp
        for j in self.numbers(a):
            z = self.heads[j]
            from_x, from_y = slot(z, gy, 1 - gx), slot(z, 1 - gy, gx)
            self.copy(a, j, 1, from_x, from_x, xp).wait_recv()
            piece = slot(z, gy, 1 - gx, **first)
            self.copy(a, j, 3, piece, piece, yp).start()
            self.copy(a, j, 2, from_y, from_y, yp).wait_recv()
            piece = slot(z, 1 - gy, gx, **second)
            self.copy(a, j, 4, piece, piece, xp).start()
        for k, (inp, mid, out) in enumerate(self.local_copies(a)):
            pltpu.make_async_copy(mid, out, self.sems[3].at[a, k]).wait()

    def share(self, a):
        kind, src, slot, bundle, local, first, second = self.views[a]
        gx, gy, xp, yp = self.gx, self.gy, self.xp, self.yp
        for j in self.numbers(a):
            z = self.heads[j]
            piece = slot(z, 1 - gy, 1 - gx, **first)
            self.copy(a, j, 3, piece, piece, yp).wait_recv()
            piece = slot(z, 1 - gy, 1 - gx, **second)
            self.copy(a, j, 4, piece, piece, xp).wait_recv()
            whole = bundle(z)
            self.copy(a, j, 5, whole, whole, self.cp).start()

    def finish(self, a):
        kind, src, slot, bundle, local, first, second = self.views[a]
        gx, gy, xp, yp = self.gx, self.gy, self.xp, self.yp
        for j in self.numbers(a):
            z = self.heads[j]
            whole = bundle(z)
            self.copy(a, j, 5, whole, whole, self.cp).wait()
            here = slot(z, gy, gx)
            give = here if j else src
            if j:
                self.copy(a, j, 0, src, here, (self.c, z)).wait_send()
            self.copy(a, j, 1, give, here, xp).wait_send()
            self.copy(a, j, 2, give, here, yp).wait_send()
            piece = slot(z, gy, 1 - gx, **first)
            self.copy(a, j, 3, piece, piece, yp).wait_send()
            piece = slot(z, 1 - gy, gx, **second)
            self.copy(a, j, 4, piece, piece, xp).wait_send()

    def run(self, units, ahead=2):
        count = len(self.jobs)
        done, at = 0, 0

        def work(most):
            nonlocal at
            while at < len(units) and units[at][0] <= done and most > 0:
                units[at][1]()
                at += 1
                most -= 1

        for a in range(min(ahead, count)):
            self.fetch(a)
        work(2)
        for step in range(count + 3):
            if step < count:
                self.trade(step)
                work(2)
            if step + ahead < count:
                self.fetch(step + ahead)
            if 0 <= step - 1 < count:
                self.forward(step - 1)
                work(2)
            if 0 <= step - 2 < count:
                self.share(step - 2)
                work(2)
            if 0 <= step - 3 < count:
                self.finish(step - 3)
                done = step - 2
                work(2)
        work(len(units))


FROZEN = [(0, 0, 1), (1, 0, 9), (1, 9, 9), (2, 0, 1), (2, 1, 3), (2, 4, 1), (2, 5, 1)]
FROZEN += [(3, 0, 2), (2, 6, 1), (4, 0, 1), (4, 1, 1), (4, 2, 1), (2, 7, 1)]


def frozen_arrays(conv_weight, time_weight, spatial_square, cross_kv, spatial_ffn):
    return [
        time_weight[None],
        conv_weight.reshape((18,) + conv_weight.shape[2:]),
        spatial_square,
        cross_kv,
        spatial_ffn,
    ]


def gather_plain(arrays, small, projections, feedforward):
    small = lax.all_gather(lax.all_gather(small, "head", axis=0), "clip", axis=0)
    frozen = [
        lax.all_gather(arrays[i][lo : lo + n], "head", axis=1, tiled=True) for i, lo, n in FROZEN
    ]
    trained = [
        lax.all_gather(
            lax.all_gather(a.astype(BF), "clip", axis=2, tiled=True), "head", axis=1, tiled=True
        )
        for a in (projections, feedforward)
    ]
    return frozen, trained, small


TILE = 256


def stream(count, tiles, body, sem, slots):
    def begin(i):
        for p, (src, dst) in enumerate(tiles(i, i % slots)):
            pltpu.make_async_copy(src, dst, sem.at[i % slots, p]).start()

    for i in range(min(slots - 1, count)):
        begin(i)

    def step(i, carry):
        @pl.when(i + slots - 1 < count)
        def _():
            begin(i + slots - 1)

        for p, (src, dst) in enumerate(tiles(i, i % slots)):
            pltpu.make_async_copy(src, dst, sem.at[i % slots, p]).wait()
        body(i, i % slots)
        return carry

    lax.fori_loop(0, count, step, 0)


def tile_at(i):
    return pl.ds(pl.multiple_of(i * TILE, TILE), TILE)


def through_tiles(x, w, buf, sem, sink):
    slots = buf.shape[0]

    def tiles(i, slot):
        return [(w.at[:, tile_at(i)], buf.at[slot])]

    def body(i, slot):
        sink(tile_at(i), dot_f32(x[...], buf[slot], ((1,), (0,))))

    stream(w.shape[1] // TILE, tiles, body, sem, slots)


def against_tiles(x, w, buf, sem, sink):
    slots, width = buf.shape[0], w.shape[1]
    lanes = pl.ds(0, width)

    def tiles(i, slot):
        return [(w.at[tile_at(i)], buf.at[slot, :, lanes])]

    def body(i, slot):
        sink(tile_at(i), dot_f32(x[...], buf[slot, :, lanes], ((1,), (1,))))

    stream(w.shape[0] // TILE, tiles, body, sem, slots)


def frame_rows(f):
    return pl.ds(pl.multiple_of(f * PIX, PIX), PIX)


def norm_rows(x, q, gain, out):
    def body(f, carry):
        rows = frame_rows(f)
        v = x[rows, :]
        v = v - jnp.mean(v, axis=1, keepdims=True)
        scale = lax.rsqrt(jnp.mean(v * v, axis=1, keepdims=True) + LAYER_EPS)
        out[rows, :] = (v * scale * q[gain : gain + 1] + q[gain + 1 : gain + 2]).astype(out.dtype)
        return carry

    lax.fori_loop(0, x.shape[0] // PIX, body, 0)


def dot_exact(a, b):
    return lax.dot_general(
        a, b, (((1,), (0,)), ((), ())), precision=lax.Precision.HIGHEST, preferred_element_type=F32
    )


def group_spread(sums, fold):
    means = dot_exact(sums, fold[...]) * (1.0 / (C // GROUPS * PIX))
    return lax.dot_general(
        means,
        fold[...],
        (((1,), (1,)), ((), ())),
        precision=lax.Precision.HIGHEST,
        preferred_element_type=F32,
    )


def group_stats(x, fold, stat):
    frames = x.shape[0] // PIX
    stat[0] = jnp.zeros_like(stat[0])
    stat[1] = jnp.zeros_like(stat[1])
    for f in range(frames):
        block = x[f * PIX : (f + 1) * PIX, :].astype(F32)
        stat[0, f : f + 1] = jnp.sum(block, axis=0, keepdims=True)
    stat[0] = group_spread(stat[0], fold)
    for f in range(frames):
        block = x[f * PIX : (f + 1) * PIX, :].astype(F32) - stat[0, f : f + 1]
        stat[1, f : f + 1] = jnp.sum(block * block, axis=0, keepdims=True)
    stat[1] = lax.rsqrt(group_spread(stat[1], fold) + GROUP_EPS)


def group_apply(x, stat, q, gain, out, act):
    for f in range(x.shape[0] // PIX):
        rows = slice(f * PIX, (f + 1) * PIX)
        v = (x[rows, :].astype(F32) - stat[0, f : f + 1]) * stat[1, f : f + 1]
        out[rows, :] = act(v * q[gain : gain + 1] + q[gain + 1 : gain + 2]).astype(out.dtype)


def group_matrix():
    group = jnp.arange(C) // (C // GROUPS)
    return (group[:, None] == jnp.arange(128)[None, :]).astype(F32)


def make_windows(x, win, flipped):
    tokens = x.shape[0]

    def body(j, carry):
        lanes = pl.ds(pl.multiple_of(j * 128, 128), 128)
        v = x[:, lanes]
        row = lax.broadcasted_iota(jnp.int32, v.shape, 0)
        py, px = row // SIDE % SIDE, row % SIDE
        for tap in range(9):
            dy, dx = tap // 3 - 1, tap % 3 - 1
            if flipped:
                dy, dx = -dy, -dx
            shift = (-(dy * SIDE + dx)) % tokens
            moved = pltpu.roll(v, shift, 0) if shift else v
            ok = (py + dy >= 0) & (py + dy < SIDE) & (px + dx >= 0) & (px + dx < SIDE)
            win[tap, :, lanes] = jnp.where(ok, moved, 0.0).astype(win.dtype)
        return carry

    lax.fori_loop(0, C // 128, body, 0)


def silu(v):
    return v / (1.0 + jnp.exp(-v))


def forward_kernel(jobs, needs, n_gather, n_out, *refs):
    ins, refs = refs[:n_gather], refs[n_gather:]
    lat, q, time_in, text, gate_bias, fold = refs[:6]
    outs, refs = refs[6 : 6 + n_out], refs[6 + n_out :]
    hid1, first, state0, state1, state2, second = refs[:6]
    self_q, self_k, self_v, cross_q, text_k, text_v, value_out, gate_out = refs[6:14]
    (
        send, recv, load_sem, store_sem, hold,
        bias_send, bias_recv, bias_all, col_sem, row_sem, save_sem,
        win, col_buf, row_buf, stage, acc, tmp, nrm, att, stat, extra,
    ) = refs[14:]
    (time_w, conv1, conv2, in_w, qkv_w, self_o, cross_w, text_w, cross_o, value_w, gate_w,
     down_w, out_w) = outs[:13]
    comm = Gather(jobs, ins, outs, send, recv, load_sem, store_sem, hold)
    greet(comm.peers())

    def bias_copy(j):
        return pltpu.make_async_remote_copy(
            src_ref=gate_bias,
            dst_ref=bias_all.at[comm.h],
            send_sem=bias_send.at[j],
            recv_sem=bias_recv.at[j],
            device_id=(comm.c, comm.heads[j]),
            device_id_type=MESH,
        )

    for j in (1, 2, 3):
        bias_copy(j).start()
    bias_all[comm.h] = gate_bias[...]

    def bias_in():
        for j in (1, 2, 3):
            bias_copy(j).wait()

    def time_unit():
        def sink(lanes, tile):
            extra[:, lanes] = tile + q[2:3, lanes] + q[3:4, lanes]

        through_tiles(time_in, time_w.at[0], col_buf, col_sem, sink)

    def act1_unit():
        group_stats(lat, fold, stat)
        group_apply(lat, stat, q, 0, tmp, silu)

    def windows_unit():
        make_windows(tmp, win, False)

    def conv_unit(w, tap):
        def sink(lanes, tile):
            if tap == 0:
                acc[:, lanes] = tile
            else:
                acc[:, lanes] += tile

        through_tiles(win.at[tap], w.at[tap], col_buf, col_sem, sink)

    def act2_unit():
        hid1[...] = acc[...] + extra[0:1]
        group_stats(hid1, fold, stat)
        group_apply(hid1, stat, q, 4, tmp, silu)

    def first_unit():
        first[...] = lat[...].astype(F32) + acc[...] + q[6:7]
        group_stats(first, fold, stat)
        group_apply(first, stat, q, 7, nrm, lambda v: v)

    def add_unit(x, w, base, bias, out, norm):
        def sink(lanes, tile):
            total = tile + q[bias : bias + 1, lanes]
            out[:, lanes] = total if base is None else total + base[:, lanes]

        through_tiles(x, w.at[0], col_buf, col_sem, sink)
        if norm is not None:
            norm_rows(out, q, norm, nrm)

    def project_unit(x, w, out):
        def sink(lanes, tile):
            out[:, lanes] = tile.astype(BF)

        against_tiles(x, w, row_buf, row_sem, sink)

    def attend_unit(qr, kr, vr, bias):
        attend_body(qr, kr, vr, bias, att, tmp)

    def save(i, k):
        dst = (value_out, gate_out)[k].at[:, tile_at(i)]
        return pltpu.make_async_copy(stage.at[i % 2, k], dst, save_sem.at[i % 2, k])

    def ffn_unit(part, parts):
        per = value_w.shape[1] // TILE // parts
        start = part * per

        def tiles(i, slot):
            rows = tile_at(start + i)
            return [
                (value_w.at[0, rows], row_buf.at[slot * 3]),
                (gate_w.at[0, rows], row_buf.at[slot * 3 + 1]),
                (down_w.at[0, rows], row_buf.at[slot * 3 + 2]),
            ]

        def body(i, slot):
            tile = start + i
            lanes = tile_at(tile % 5)
            z = tile // 5
            x = nrm[...]
            value = dot_f32(x, row_buf[slot * 3], ((1,), (1,))) + bias_all[z, 0:1, lanes]
            gate = dot_f32(x, row_buf[slot * 3 + 1], ((1,), (1,))) + bias_all[z, 1:2, lanes]
            mixed = (value * gelu_erf(gate)).astype(BF)

            @pl.when(tile >= 2)
            def _():
                save(tile - 2, 0).wait()
                save(tile - 2, 1).wait()

            stage[tile % 2, 0] = value.astype(BF)
            stage[tile % 2, 1] = gate.astype(BF)
            save(tile, 0).start()
            save(tile, 1).start()
            acc[...] += dot_f32(mixed, row_buf[slot * 3 + 2], ((1,), (0,)))

        if part == 0:
            acc[...] = state2[...] + q[18:19]
        stream(per, tiles, body, row_sem, 2)
        if part == parts - 1:
            for tile in (value_w.shape[1] // TILE - 2, value_w.shape[1] // TILE - 1):
                save(tile, 0).wait()
                save(tile, 1).wait()
            nrm[...] = acc[...].astype(BF)

    P_ = functools.partial
    units = [(0, act1_unit), (0, windows_unit), (needs["time"], time_unit)]
    units += [(needs["conv1", t], P_(conv_unit, conv1, t)) for t in range(9)]
    units += [(0, act2_unit), (0, windows_unit)]
    units += [(needs["conv2", t], P_(conv_unit, conv2, t)) for t in range(9)]
    units += [(0, first_unit)]
    units += [(needs["in"], P_(add_unit, nrm, in_w, None, 9, state0, 10))]
    units += [
        (needs["qkv"], P_(project_unit, nrm, qkv_w.at[i], o))
        for i, o in enumerate((self_q, self_k, self_v))
    ]
    units += [(0, P_(attend_unit, self_q, self_k, self_v, spatial_mask))]
    units += [(needs["self_o"], P_(add_unit, att, self_o, state0, 12, state1, 13))]
    units += [(needs["cross"], P_(project_unit, nrm, cross_w.at[0], cross_q))]
    units += [(needs["text"], P_(project_unit, text, text_w.at[0], text_k))]
    units += [(needs["text"], P_(project_unit, text, text_w.at[1], text_v))]
    units += [(0, P_(attend_unit, cross_q, text_k, text_v, text_mask))]
    units += [(needs["cross_o"], P_(add_unit, att, cross_o, state1, 15, state2, 16))]
    units += [(0, bias_in)]
    units += [(needs["ffn"], P_(ffn_unit, i, 5)) for i in range(5)]
    units += [(needs["out"], P_(add_unit, nrm, out_w, first, 19, second, None))]
    comm.run(units)


def forward_fused(arrays, small, projections, feedforward, lat, q, time_in, text, gate_bias):
    tokens = lat.shape[0]
    square = projections.astype(BF).reshape(5, 2, 2, 2, 80, 160).transpose(0, 1, 3, 2, 4, 5)
    wide = feedforward.astype(BF).reshape(2, 2, 2, 320, 160).transpose(0, 2, 1, 3, 4)
    square = lax.all_to_all(square.reshape(5, 8, 80, 160), "clip", 1, 3, tiled=True)
    wide = lax.all_to_all(wide.reshape(8, 320, 160), "clip", 0, 2, tiled=True)
    ins = arrays + [square.reshape(5, 80, C), wide.reshape(1, 320, C), small[None]]
    shapes, jobs, needs = [], [], {}
    names = ["time", "conv1", "conv2", "in", "qkv", "self_o", "cross", "text", "cross_o"]
    names += ["value", "gate", "ffn", "out"]
    for o, (i, lo, n) in enumerate(FROZEN):
        rows, cols = ins[i].shape[1:]
        shapes.append((n, 4 * rows, cols))
        step = 3 if n == 9 else n
        for at in range(0, n, step):
            jobs.append(("frozen", i, o, lo + at, at, step))
            if n == 9:
                for t in range(at, at + step):
                    needs[names[o], t] = len(jobs)
        needs[names[o]] = len(jobs)
    shapes += [(5, 2, C, C), (1, 2, 4 * C, C), (1, 2, 16 * small.shape[0], C)]
    jobs += [("own", 7, 15, 0, 0, 1), ("own", 5, 13, 0, 0, 2), ("own", 5, 13, 2, 2, 3)]
    jobs += [("own", 6, 14, 0, 0, 1)]
    count = len(jobs)
    most = max(j[5] * ins[j[1]].shape[1] for j in jobs)
    any_spec, vmem = pl.BlockSpec(memory_space=pl.ANY), pl.BlockSpec(memory_space=pltpu.VMEM)
    wide_f32 = jax.ShapeDtypeStruct((tokens, C), F32)
    wide_bf = jax.ShapeDtypeStruct((tokens, C), BF)
    text_bf = jax.ShapeDtypeStruct((text.shape[0], C), BF)
    hidden = jax.ShapeDtypeStruct((tokens, 4 * C), BF)
    fold = group_matrix()
    dma = pltpu.SemaphoreType.DMA
    outs = pl.pallas_call(
        functools.partial(forward_kernel, jobs, needs, len(ins), len(shapes)),
        out_shape=tuple(jax.ShapeDtypeStruct(shape, BF) for shape in shapes)
        + (wide_f32,) * 6
        + (wide_bf,) * 4
        + (text_bf,) * 2
        + (hidden,) * 2,
        in_specs=[any_spec] * len(ins) + [vmem] * 6,
        out_specs=(any_spec,) * len(shapes) + (vmem,) * 12 + (any_spec,) * 2,
        scratch_shapes=[
            dma((count, 4, 6)),
            dma((count, 4, 6)),
            dma((count, 4)),
            dma((count, 4)),
            pltpu.VMEM((2, most, C), BF),
            dma((4,)),
            dma((4,)),
            pltpu.VMEM((4, 8, C), F32),
            dma((3, 1)),
            dma((6, 3)),
            dma((2, 2)),
            pltpu.VMEM((9, tokens, C), BF),
            pltpu.VMEM((3, C, TILE), BF),
            pltpu.VMEM((6, TILE, C), BF),
            pltpu.VMEM((2, 2, tokens, TILE), BF),
            pltpu.VMEM((tokens, C), F32),
            pltpu.VMEM((tokens, C), F32),
            pltpu.VMEM((tokens, C), BF),
            pltpu.VMEM((tokens, C), BF),
            pltpu.VMEM((2, 8, C), F32),
            pltpu.VMEM((16, C), F32),
        ],
        compiler_params=pltpu.CompilerParams(
            collective_id=1, has_side_effects=True, vmem_limit_bytes=60 << 20
        ),
    )(
        *ins,
        lat,
        jnp.pad(q, ((0, 4), (0, 0))),
        jnp.pad(time_in, ((0, 15), (0, 0))),
        text,
        jnp.pad(gate_bias, ((0, 6), (0, 0))),
        fold,
    )
    frozen, saved = outs[:13], outs[16:]
    packed = outs[15].reshape(2, 4, 2, 2, -1).transpose(0, 3, 2, 1, 4)
    trained = [outs[13].reshape(10, C, C), outs[14].reshape(2, 4 * C, C)]
    return frozen, trained, packed.reshape(8, 4, -1), saved


def pack_small(vectors, up_bias):
    flat = jnp.concatenate([a.astype(BF).reshape(-1) for a in (vectors, up_bias)])
    return jnp.pad(flat, (0, 32 * C - flat.shape[0])).reshape(32, C)


def unpack_small(sizes, packed, vectors, up_bias):
    packed = packed.reshape(sizes[0], sizes[1], -1).astype(F32)
    vector = packed[:, 0, : vectors.size].reshape((sizes[0],) + vectors.shape)
    bias = packed[:, :, vectors.size : vectors.size + up_bias.size]
    bias = bias.reshape(sizes + up_bias.shape).transpose(1, 2, 0, 3)
    return vector.transpose(1, 0, 2).reshape(vectors.shape[0], C), bias.reshape(1, -1)


def sum_plain(parts, wide_parts, small):
    sums = [
        jnp.stack(
            [
                lax.psum_scatter(
                    lax.psum_scatter(g, "head", scatter_dimension=0, tiled=True),
                    "clip",
                    scatter_dimension=1,
                    tiled=True,
                ).astype(F32)
                for g in a
            ]
        )
        for a in (parts, wide_parts)
    ]
    return sums + [lax.psum(small, ("clip", "head"))[lax.axis_index("clip")]]


def head_window(head):
    start = head * HD // 128 * 128
    return start, head * HD - start


def lane_mask(shape, low):
    lane = lax.broadcasted_iota(jnp.int32, shape, 1)
    return (lane >= low) & (lane < low + HD)


def dot_f32(a, b, dims):
    return lax.dot_general(a, b, (dims, ((), ())), preferred_element_type=F32)


def spatial_mask(shape):
    row = lax.broadcasted_iota(jnp.int32, shape, 0)
    return row // PIX == lax.broadcasted_iota(jnp.int32, shape, 1) // PIX


def text_mask(shape):
    return lax.broadcasted_iota(jnp.int32, shape, 1) < TEXT_LEN


def head_probs(q, k, bias):
    scores = dot_f32(q, k, ((1,), (1,))) * HD ** (-0.5)
    if callable(bias):
        scores = jnp.where(bias(scores.shape), scores, MASK_FILL)
    else:
        scores = scores + bias[...]
    top = jnp.max(scores, axis=1, keepdims=True)
    weights = jnp.exp(scores - top)
    return weights / jnp.sum(weights, axis=1, keepdims=True)


def attend_body(q_ref, k_ref, v_ref, bias_ref, o_ref, acc):
    acc[...] = jnp.zeros_like(acc)
    for head in range(HEADS):
        start, low = head_window(head)
        win = pl.ds(start, 256)
        q = q_ref[:, win]
        mask = lane_mask(q.shape, low)
        q = jnp.where(mask, q, jnp.zeros_like(q))
        probs = head_probs(q, k_ref[:, win], bias_ref)
        out = dot_f32(probs.astype(BF), v_ref[:, win], ((1,), (0,)))
        acc[:, win] += jnp.where(mask, out, 0.0)
    o_ref[...] = acc[...].astype(BF)


def attend(q, k, v, bias):
    return pl.pallas_call(
        attend_body,
        out_shape=jax.ShapeDtypeStruct(q.shape, BF),
        scratch_shapes=[pltpu.VMEM(q.shape, F32)],
        compiler_params=pltpu.CompilerParams(vmem_limit_bytes=40 << 20),
    )(q, k, v, bias)


def attend_back_body(with_keys, q_ref, k_ref, v_ref, bias_ref, g_ref, *refs):
    if with_keys:
        dq_ref, dk_ref, dv_ref, dq, dk, dv = refs
        dk[...] = jnp.zeros_like(dk)
        dv[...] = jnp.zeros_like(dv)
    else:
        dq_ref, dq = refs
    dq[...] = jnp.zeros_like(dq)
    for head in range(HEADS):
        start, low = head_window(head)
        win = pl.ds(start, 256)
        q, k, v, g = q_ref[:, win], k_ref[:, win], v_ref[:, win], g_ref[:, win]
        mask = lane_mask(q.shape, low)
        q = jnp.where(mask, q, jnp.zeros_like(q))
        g = jnp.where(mask, g, jnp.zeros_like(g))
        probs = head_probs(q, k, bias_ref)
        dp = dot_f32(g, v, ((1,), (1,)))
        ds = probs * (dp - jnp.sum(dp * probs, axis=1, keepdims=True)) * HD ** (-0.5)
        ds = ds.astype(BF)
        dq[:, win] += jnp.where(mask, dot_f32(ds, k, ((1,), (0,))), 0.0)
        if with_keys:
            dk[:, win] += dot_f32(ds, q, ((0,), (0,)))
            dv[:, win] += dot_f32(probs.astype(BF), g, ((0,), (0,)))
    dq_ref[...] = dq[...].astype(BF)
    if with_keys:
        dk_ref[...] = dk[...].astype(BF)
        dv_ref[...] = dv[...].astype(BF)


def attend_back(q, k, v, bias, g, with_keys=True):
    count = 3 if with_keys else 1
    return pl.pallas_call(
        functools.partial(attend_back_body, with_keys),
        out_shape=(jax.ShapeDtypeStruct(q.shape, BF),) * count,
        scratch_shapes=[pltpu.VMEM(q.shape, F32)] * count,
        compiler_params=pltpu.CompilerParams(vmem_limit_bytes=48 << 20),
    )(q, k, v, bias, g)


def group_mean(per_channel):
    width = C // GROUPS
    means = jnp.mean(per_channel.reshape(-1, GROUPS, width), axis=-1) / PIX
    return jnp.repeat(means, width, axis=1)[:, None, :]


def gn_stats(x):
    center = group_mean(jnp.sum(x, axis=1))
    centered = x - center
    variance = group_mean(jnp.sum(centered * centered, axis=1))
    return center, lax.rsqrt(variance + GROUP_EPS)


def gn(x, stats, gain, shift):
    return (x - stats[0]) * stats[1] * gain + shift


def gn_back(dy, x, stats, gain):
    z = (x - stats[0]) * stats[1]
    gd = dy * gain
    mean_gd = group_mean(jnp.sum(gd, axis=1))
    mean_gz = group_mean(jnp.sum(gd * z, axis=1))
    return (gd - mean_gd - z * mean_gz) * stats[1]


def ln_stats(x):
    center = jnp.mean(x, axis=-1, keepdims=True)
    centered = x - center
    variance = jnp.mean(centered * centered, axis=-1, keepdims=True)
    return center, lax.rsqrt(variance + LAYER_EPS)


def ln(x, stats, gain, shift):
    return (x - stats[0]) * stats[1] * gain + shift


def ln_back(dy, x, stats, gain):
    z = (x - stats[0]) * stats[1]
    gd = dy * gain
    mean_gd = jnp.mean(gd, axis=-1, keepdims=True)
    mean_gz = jnp.mean(gd * z, axis=-1, keepdims=True)
    return (gd - mean_gd - z * mean_gz) * stats[1]


def ln_param_grads(dy, x, stats):
    z = (x - stats[0]) * stats[1]
    return jnp.sum(dy * z, axis=0), jnp.sum(dy, axis=0)


def silu_back(dy, v):
    gate = jax.nn.sigmoid(v)
    return dy * gate * (1.0 + v * (1.0 - gate))


def gelu_exact(v):
    return jax.nn.gelu(v, approximate=False)


def gelu_erf(v):
    return 0.5 * v * (1.0 + lax.erf(v * math.sqrt(0.5)))


def gelu_exact_slope(v):
    density = jnp.exp(-0.5 * v * v) * (1.0 / math.sqrt(2.0 * math.pi))
    return 0.5 * (1.0 + lax.erf(v * math.sqrt(0.5))) + v * density


def gelu_tanh(v):
    return jax.nn.gelu(v, approximate=True)


def gelu_tanh_slope(v):
    k = math.sqrt(2.0 / math.pi)
    t = jnp.tanh(k * (v + 0.044715 * v * v * v))
    return 0.5 * (1.0 + t) + 0.5 * v * (1.0 - t * t) * k * (1.0 + 3.0 * 0.044715 * v * v)


def frame_table():
    frame_pos = jnp.arange(FMAX, dtype=F32)[:, None]
    channel = jnp.arange(C)
    frequency = jnp.exp((channel - channel % 2).astype(F32) * (-math.log(10000.0) / C))
    angles = frame_pos * frequency[None, :]
    return jnp.where(channel[None, :] % 2 == 0, jnp.sin(angles), jnp.cos(angles))


def time_table(timesteps):
    half_width = C // 2
    frequency = jnp.exp(jnp.arange(half_width, dtype=F32) * (-math.log(10000.0) / half_width))
    angles = timesteps.astype(F32)[:, None] * frequency[None, :]
    return jnp.concatenate([jnp.cos(angles), jnp.sin(angles)], axis=1)


def through(x, w):
    return dot_f32(x, w, ((1,), (0,)))


def against(x, w):
    return dot_f32(x, w, ((1,), (1,)))


def outer(a, b):
    return dot_f32(a, b, ((0,), (0,))).astype(BF)


def windows(x, flipped):
    frames = x.shape[0]
    padded = jnp.pad(x.reshape(frames, SIDE, SIDE, C), ((0, 0), (1, 1), (1, 1), (0, 0)))
    pieces = []
    for tap in range(9):
        dy, dx = tap // 3, tap % 3
        if flipped:
            dy, dx = 2 - dy, 2 - dx
        pieces.append(padded[:, dy : dy + SIDE, dx : dx + SIDE].reshape(frames * PIX, C))
    return pieces


def conv(x, w):
    return through(jnp.concatenate(windows(x, False), axis=1), w.reshape(9 * C, C))


def conv_back(g, w):
    stacked = jnp.stack(windows(g, True), axis=1)
    return lax.dot_general(
        stacked, w, (((1, 2), (0, 2)), ((), ())), preferred_element_type=F32
    )


def update(weight, moment, average, gradient, step_rate):
    moment_new = MOMENTUM * moment + gradient
    weight_new = weight - step_rate * (gradient + MOMENTUM * moment_new)
    average_new = AVERAGE_DECAY * average + (1.0 - AVERAGE_DECAY) * weight_new
    return (moment_new, average_new, weight_new)


CHUNKS = 9


class GradientSum:
    def __init__(self, grads, landed, columns, bufs, sems, frees):
        self.grads, self.landed, self.columns = grads, landed, columns
        self.total, self.own, self.got_x, self.got_y, self.got2, self.got3, self.deal = bufs
        self.send, self.recv, self.load_sem = sems
        self.free_x, self.free_y, self.free2_x, self.free2_y, self.free3 = frees
        c, h, core, gx, gy, partners, heads = place()
        self.c, self.h, self.core, self.gx, self.gy = c, h, core, gx, gy
        self.xp, self.yp, self.cp = partners["x"], partners["y"], partners["core"]
        self.heads = heads
        self.plane = []
        for d in range(8):
            core_d, x_d, y_d = d % 2, d // 2 % 2, d // 4
            self.plane.append(
                (gy + y_d - 2 * gy * y_d) * 4
                + (gx + x_d - 2 * gx * x_d) * 2
                + core
                + core_d
                - 2 * core * core_d
            )

    def peers(self):
        return [(self.plane[d], self.h) for d in range(1, 8)] + [
            (self.c, self.heads[j]) for j in (1, 2, 3)
        ]

    def block(self, k, y):
        if k < 5:
            return self.grads[2 * k + y]
        return self.grads[10 + y].at[:, :, :, k - 5]

    def copy(self, k, kind, src, dst, device):
        return pltpu.make_async_remote_copy(
            src_ref=src,
            dst_ref=dst,
            send_sem=self.send.at[k, kind],
            recv_sem=self.recv.at[k, kind],
            device_id=device,
            device_id_type=MESH,
        )

    def core_copies(self, k):
        return [
            self.copy(k, y, self.block(k, y).at[:, 1 - self.core], self.landed.at[k, y], self.cp)
            for y in (0, 1)
        ]

    def landed_copy(self, k):
        slot = self.total.at[k % self.total.shape[0]]
        return pltpu.make_async_copy(self.landed.at[k], slot, self.load_sem.at[k, 0])

    def own_copies(self, k):
        return [
            pltpu.make_async_copy(
                self.block(k, y).at[:, self.core], self.own.at[y], self.load_sem.at[k, 1 + y]
            )
            for y in (0, 1)
        ]

    def first_copy(self, k):
        held = self.total.at[k % self.total.shape[0]]
        at = k // 2 % 2
        if k % 2 == 0:
            return self.copy(k, 2, held.at[:, :, 1 - self.gx], self.got_x.at[at], self.xp)
        return self.copy(k, 2, held.at[1 - self.gy], self.got_y.at[at], self.yp)

    def second_copy(self, k):
        at = k // 2 % 2
        if k % 2 == 0:
            return self.copy(k, 3, self.got_x.at[at, 1 - self.gy], self.got2.at[k % 4], self.yp)
        return self.copy(k, 3, self.got_y.at[at, :, 1 - self.gx], self.got2.at[k % 4], self.xp)

    def last_copies(self, k):
        return [
            self.copy(
                k,
                3 + j,
                self.got2.at[k % 4, self.heads[j]],
                self.got3.at[k % 2, j - 1],
                (self.c, self.heads[j]),
            )
            for j in (1, 2, 3)
        ]

    def deal_copies(self, k):
        at = self.columns.at[k, self.c]
        return [
            self.copy(k, 6 + d, self.deal.at[k % 2, self.plane[d]], at, (self.plane[d], self.h))
            for d in range(1, 8)
        ]

    def deal_own(self, k):
        src = self.deal.at[k % 2, self.c]
        return pltpu.make_async_copy(src, self.columns.at[k, self.c], self.load_sem.at[k, 3])

    def signal(self, sem, device):
        pl.semaphore_signal(sem, inc=1, device_id=device, device_id_type=MESH)

    def exchange(self, k):
        for item in self.core_copies(k):
            item.start()

    def load(self, k):
        for item in self.core_copies(k):
            item.wait_recv()
        if k >= self.total.shape[0]:
            self.first_copy(k - self.total.shape[0]).wait_send()
        self.landed_copy(k).start()

    def load_own(self, k):
        for item in self.own_copies(k):
            item.start()

    def add_core(self, k):
        self.landed_copy(k).wait()
        for item in self.own_copies(k):
            item.wait()
        slot = k % self.total.shape[0]
        total, own = self.total, self.own

        def body(i, carry):
            y, z, x = i // 8, i // 2 % 4, i % 2
            total[slot, y, z, x] = total[slot, y, z, x] + own[y, z, x]
            return carry

        lax.fori_loop(0, 16, body, 0)
        if k + 1 < CHUNKS:
            self.load_own(k + 1)
        if k >= 4:
            pl.semaphore_wait(self.free_x if k % 2 == 0 else self.free_y, 1)
        self.first_copy(k).start()

    def add_first(self, k):
        self.first_copy(k).wait_recv()
        slot, at = k % self.total.shape[0], k // 2 % 2
        total, got_x, got_y = self.total, self.got_x, self.got_y
        gx, gy = self.gx, self.gy

        def body(i, carry):
            if k % 2 == 0:
                y, z = i // 4, i % 4
                got_x[at, y, z] = got_x[at, y, z] + total[slot, y, z, gx]
            else:
                z, x = i // 2, i % 2
                got_y[at, z, x] = got_y[at, z, x] + total[slot, gy, z, x]
            return carry

        lax.fori_loop(0, 8, body, 0)
        if k >= 4:
            pl.semaphore_wait(self.free2_y if k % 2 == 0 else self.free2_x, 1)
        self.second_copy(k).start()

    def add_second(self, k):
        self.second_copy(k).wait_recv()
        at = k // 2 % 2
        got_x, got_y, got2 = self.got_x, self.got_y, self.got2

        def body(z, carry):
            if k % 2 == 0:
                got2[k % 4, z] = got2[k % 4, z] + got_x[at, self.gy, z]
            else:
                got2[k % 4, z] = got2[k % 4, z] + got_y[at, z, self.gx]
            return carry

        lax.fori_loop(0, 4, body, 0)
        self.second_copy(k).wait_send()
        if k + 4 < CHUNKS:
            if k % 2 == 0:
                self.signal(self.free_x, self.xp)
            else:
                self.signal(self.free_y, self.yp)
        for j, item in enumerate(self.last_copies(k)):
            if k >= 2:
                pl.semaphore_wait(self.free3.at[j], 1)
            item.start()

    def add_last(self, k):
        for item in self.last_copies(k):
            item.wait()
        got3, at = self.got3, k % 2
        rest = got3[at, 0].astype(F32) + got3[at, 1].astype(F32) + got3[at, 2].astype(F32)
        result = (self.got2[k % 4, self.h].astype(F32) + rest).astype(BF)
        if k + 4 < CHUNKS:
            if k % 2 == 0:
                self.signal(self.free2_y, self.yp)
            else:
                self.signal(self.free2_x, self.xp)
        if k + 2 < CHUNKS:
            for j in (1, 2, 3):
                self.signal(self.free3.at[j - 1], (self.c, self.heads[j]))
        if k >= 2:
            self.deal_done(k - 2)
        for d in range(8):
            self.deal[k % 2, d] = result[:, d * HD : (d + 1) * HD]
        for item in self.deal_copies(k):
            item.start()
        self.deal_own(k).start()

    def deal_done(self, k):
        for item in self.deal_copies(k):
            item.wait_send()
        self.deal_own(k).wait()

    def run(self, units):
        at = 0

        def work(most):
            nonlocal at
            for unit in units[at : at + most]:
                unit()
            at += most

        for k in range(CHUNKS):
            self.exchange(k)
        self.load_own(0)
        work(1)
        self.load(0)
        for step in range(CHUNKS + 4):
            if step < CHUNKS:
                self.add_core(step)
                work(2)
            if 0 <= step - 2 < CHUNKS:
                self.add_first(step - 2)
                work(1)
            if step + 1 < CHUNKS:
                self.load(step + 1)
            if 0 <= step - 3 < CHUNKS:
                self.add_second(step - 3)
                work(2)
            if 0 <= step - 4 < CHUNKS:
                self.add_last(step - 4)
                work(1)
        work(len(units))
        for k in range(CHUNKS):
            for item in self.core_copies(k):
                item.wait_send()
            if k >= CHUNKS - self.total.shape[0]:
                self.first_copy(k).wait_send()
            for item in self.deal_copies(k):
                item.wait_recv()
        for k in (CHUNKS - 2, CHUNKS - 1):
            self.deal_done(k)


class SmallSum:
    def __init__(self, total, small, out, got1, got2, send, recv):
        self.t, self.small, self.out = total, small, out
        self.got1, self.got2, self.send, self.recv = got1, got2, send, recv

    def copy(self, i, src, dst, device):
        return pltpu.make_async_remote_copy(
            src_ref=src,
            dst_ref=dst,
            send_sem=self.send.at[i],
            recv_sem=self.recv.at[i],
            device_id=device,
            device_id_type=MESH,
        )

    def plane_copies(self):
        t = self.t
        return [
            self.copy(d, self.small.at[t.plane[d]], self.got1.at[t.c], (t.plane[d], t.h))
            for d in range(1, 8)
        ]

    def head_copies(self):
        t = self.t
        return [
            self.copy(7 + j, self.out, self.got2.at[j - 1], (t.c, t.heads[j])) for j in (1, 2, 3)
        ]

    def first(self):
        for item in self.plane_copies():
            item.start()
        self.got1[self.t.c] = self.small[self.t.c]

    def second(self):
        for item in self.plane_copies():
            item.wait()
        self.out[...] = jnp.sum(self.got1[...], axis=0)
        for item in self.head_copies():
            item.start()

    def last(self):
        for item in self.head_copies():
            item.wait()
        self.out[...] += jnp.sum(self.got2[...], axis=0)


def norm_back_rows(dy, x, q, gain, out):
    def body(f, carry):
        rows = frame_rows(f)
        v = x[rows, :]
        v = v - jnp.mean(v, axis=1, keepdims=True)
        scale = lax.rsqrt(jnp.mean(v * v, axis=1, keepdims=True) + LAYER_EPS)
        z = v * scale
        gd = dy[rows, :] * q[gain : gain + 1]
        m1 = jnp.mean(gd, axis=1, keepdims=True)
        m2 = jnp.mean(gd * z, axis=1, keepdims=True)
        out[rows, :] = out[rows, :] + (gd - m1 - z * m2) * scale
        return carry

    lax.fori_loop(0, x.shape[0] // PIX, body, 0)


def group_back(dy, x, q, gain, with_silu, fold, stat, sums, sink):
    group_stats(x, fold, stat)
    frames = x.shape[0] // PIX
    sums[0] = jnp.zeros_like(sums[0])
    sums[1] = jnp.zeros_like(sums[1])

    def normal(f):
        block = x[f * PIX : (f + 1) * PIX, :].astype(F32)
        return (block - stat[0, f : f + 1]) * stat[1, f : f + 1]

    for f in range(frames):
        rows = slice(f * PIX, (f + 1) * PIX)
        z = normal(f)
        g = dy[rows, :]
        if with_silu:
            v = z * q[gain : gain + 1] + q[gain + 1 : gain + 2]
            gate = 1.0 / (1.0 + jnp.exp(-v))
            g = g * gate * (1.0 + v * (1.0 - gate))
        gd = g * q[gain : gain + 1]
        dy[rows, :] = gd
        sums[0, f : f + 1] = jnp.sum(gd, axis=0, keepdims=True)
        sums[1, f : f + 1] = jnp.sum(gd * z, axis=0, keepdims=True)
    sums[0] = group_spread(sums[0], fold)
    sums[1] = group_spread(sums[1], fold)
    for f in range(frames):
        rows = slice(f * PIX, (f + 1) * PIX)
        dx = dy[rows, :] - sums[0, f : f + 1] - normal(f) * sums[1, f : f + 1]
        sink(rows, dx * stat[1, f : f + 1])


def backward_kernel(n_weights, *refs):
    grads, refs = refs[:12], refs[12:]
    weights, refs = refs[:n_weights], refs[n_weights:]
    conv1, conv2, in_w, qkv_w, self_o, cross_w, cross_o, value_w, gate_w, down_w, out_w = weights
    hid1, first, state0, state1, state2, lat, value_in, gate_in = refs[:8]
    self_q, self_k, self_v, cross_q, text_k, text_v = refs[8:14]
    g_second, q, fold, small = refs[14:18]
    columns, grad_in, small_out, landed = refs[18:22]
    (
        total, own, got_x, got_y, got2, got3, deal,
        send, recv, load_sem, free_x, free_y, free2_x, free2_y, free3,
        small1, small2, small_send, small_recv,
        col_sem, row_sem, pair_sem, in_sem,
        win, col_buf, row_buf, pair, gs, acc, tmp, xb, low, stat, sums,
    ) = refs[22:]
    comm = GradientSum(
        grads,
        landed,
        columns,
        (total, own, got_x, got_y, got2, got3, deal),
        (send, recv, load_sem),
        (free_x, free_y, free2_x, free2_y, free3),
    )
    tiny = SmallSum(comm, small, small_out, small1, small2, small_send, small_recv)
    greet(comm.peers())
    tiny.first()

    def bring(pairs):
        copies = [
            pltpu.make_async_copy(src, dst, in_sem.at[i]) for i, (src, dst) in enumerate(pairs)
        ]
        for item in copies:
            item.start()
        for item in copies:
            item.wait()

    def against_unit(x, w, out):
        def sink(lanes, tile):
            out[:, lanes] = tile.astype(out.dtype)

        against_tiles(x, w, row_buf, row_sem, sink)

    def start_unit():
        bring([(g_second, tmp)])
        low[...] = tmp[...].astype(BF)
        against_unit(low, out_w.at[0], gs)
        low[...] = gs[...].astype(BF)
        acc[...] = jnp.zeros_like(acc)

    def ffn_unit(part, parts):
        per = value_w.shape[1] // TILE // parts
        start = part * per

        def tiles(i, slot):
            rows = tile_at(start + i)
            return [
                (value_w.at[0, rows], row_buf.at[slot * 3]),
                (gate_w.at[0, rows], row_buf.at[slot * 3 + 1]),
                (down_w.at[0, rows], row_buf.at[slot * 3 + 2]),
                (value_in.at[:, rows], pair.at[slot, 0]),
                (gate_in.at[:, rows], pair.at[slot, 1]),
            ]

        def body(i, slot):
            g = dot_f32(low[...], row_buf[slot * 3 + 2], ((1,), (1,)))
            value, gate = pair[slot, 0].astype(F32), pair[slot, 1].astype(F32)
            phi = 0.5 * (1.0 + lax.erf(gate * math.sqrt(0.5)))
            density = jnp.exp(-0.5 * gate * gate) * (1.0 / math.sqrt(2.0 * math.pi))
            g_value = (gate * phi * g).astype(BF)
            g_gate = (value * (phi + gate * density) * g).astype(BF)
            acc[...] += dot_f32(g_value, row_buf[slot * 3], ((1,), (0,)))
            acc[...] += dot_f32(g_gate, row_buf[slot * 3 + 1], ((1,), (0,)))

        stream(per, tiles, body, pair_sem, 2)

    def norm_unit(state, gain):
        bring([(state, xb)])
        norm_back_rows(acc, xb, q, gain, gs)
        low[...] = gs[...].astype(BF)

    def cross_unit():
        rows = text_k.shape[0]
        keys, values = win.at[1, pl.ds(0, rows)], win.at[2, pl.ds(0, rows)]
        bring([(cross_q, win.at[0]), (text_k, keys), (text_v, values)])
        attend_back_body(False, win.at[0], keys, values, text_mask, win.at[6], win.at[3], tmp)

    def self_unit():
        bring([(self_q, win.at[0]), (self_k, win.at[1]), (self_v, win.at[2])])
        attend_back_body(
            True,
            win.at[0],
            win.at[1],
            win.at[2],
            spatial_mask,
            win.at[6],
            win.at[3],
            win.at[4],
            win.at[5],
            tmp,
            acc,
            xb,
        )

    def through_unit(x, w, fresh):
        def sink(lanes, tile):
            if fresh:
                acc[:, lanes] = tile
            else:
                acc[:, lanes] += tile

        through_tiles(x, w, col_buf, col_sem, sink)

    def first_unit():
        bring([(first, xb), (g_second, gs)])

        def sink(rows, dx):
            gs[rows, :] = gs[rows, :] + dx

        group_back(acc, xb, q, 7, False, fold, stat, sums, sink)

    def hid_unit():
        bring([(hid1, xb)])

        def sink(rows, dx):
            tmp[rows, :] = dx

        group_back(acc, xb, q, 4, True, fold, stat, sums, sink)

    def last_unit():
        bring([(lat, low)])

        def sink(rows, dx):
            low[rows, :] = (gs[rows, :] + dx).astype(BF)

        group_back(acc, low, q, 0, True, fold, stat, sums, sink)
        bring([(low, grad_in)])

    def windows_unit(x):
        make_windows(x, win, True)

    def conv_unit(w, tap):
        def sink(lanes, tile):
            if tap == 0:
                acc[:, lanes] = tile
            else:
                acc[:, lanes] += tile

        against_tiles(win.at[tap], w.at[tap], row_buf, row_sem, sink)

    P_ = functools.partial
    units = [start_unit] + [P_(ffn_unit, i, 10) for i in range(10)]
    units += [tiny.second, P_(norm_unit, state2, 16)]
    units += [P_(against_unit, low, cross_o.at[0], win.at[6]), cross_unit]
    units += [P_(through_unit, win.at[3], cross_w.at[0], True), P_(norm_unit, state1, 13)]
    units += [tiny.last, P_(against_unit, low, self_o.at[0], win.at[6]), self_unit]
    units += [P_(through_unit, win.at[3 + i], qkv_w.at[i], i == 0) for i in range(3)]
    units += [P_(norm_unit, state0, 10), P_(against_unit, low, in_w.at[0], acc), first_unit]
    units += [P_(windows_unit, gs)] + [P_(conv_unit, conv2, t) for t in range(9)]
    units += [hid_unit, P_(windows_unit, tmp)] + [P_(conv_unit, conv1, t) for t in range(9)]
    units += [last_unit]
    comm.run(units)


def backward_fused(parts, wide_parts, small, frozen, saved, lat, grad_second, q):
    tokens = lat.shape[0]
    ins = [g.reshape(4, 2, 2, 80, C) for g in parts]
    ins += [g.reshape(4, 2, 2, 4, 80, C) for g in wide_parts]
    weights = [frozen[i] for i in (1, 2, 3, 4, 5, 6, 8, 9, 10, 11, 12)]
    hid1, first, state0, state1, state2 = saved[:5]
    kept = [hid1, first, state0, state1, state2, lat, saved[12], saved[13]] + list(saved[6:12])
    fold = group_matrix()
    any_spec, vmem = pl.BlockSpec(memory_space=pl.ANY), pl.BlockSpec(memory_space=pltpu.VMEM)
    dma = pltpu.SemaphoreType.DMA
    rows = small.shape[1]
    columns, grad_in, small_sum, _ = pl.pallas_call(
        functools.partial(backward_kernel, len(weights)),
        out_shape=(
            jax.ShapeDtypeStruct((CHUNKS, 8, 80, HD), BF),
            jax.ShapeDtypeStruct((tokens, C), BF),
            jax.ShapeDtypeStruct((rows, 128), F32),
            jax.ShapeDtypeStruct((CHUNKS, 2, 4, 2, 80, C), BF),
        ),
        in_specs=[any_spec] * (13 + len(weights) + len(kept)) + [vmem] * 3,
        out_specs=(any_spec, any_spec, vmem, any_spec),
        scratch_shapes=[
            pltpu.VMEM((3, 2, 4, 2, 80, C), BF),
            pltpu.VMEM((2, 4, 2, 80, C), BF),
            pltpu.VMEM((2, 2, 4, 80, C), BF),
            pltpu.VMEM((2, 4, 2, 80, C), BF),
            pltpu.VMEM((4, 4, 80, C), BF),
            pltpu.VMEM((2, 3, 80, C), BF),
            pltpu.VMEM((2, 8, 80, HD), BF),
            dma((CHUNKS, 14)),
            dma((CHUNKS, 14)),
            dma((CHUNKS, 4)),
            pltpu.SemaphoreType.REGULAR,
            pltpu.SemaphoreType.REGULAR,
            pltpu.SemaphoreType.REGULAR,
            pltpu.SemaphoreType.REGULAR,
            pltpu.SemaphoreType.REGULAR((3,)),
            pltpu.VMEM((8, rows, 128), F32),
            pltpu.VMEM((3, rows, 128), F32),
            dma((11,)),
            dma((11,)),
            dma((2, 1)),
            dma((6, 1)),
            dma((2, 5)),
            dma((3,)),
            pltpu.VMEM((9, tokens, C), BF),
            pltpu.VMEM((2, C, TILE), BF),
            pltpu.VMEM((6, TILE, C), BF),
            pltpu.VMEM((2, 2, tokens, TILE), BF),
            pltpu.VMEM((tokens, C), F32),
            pltpu.VMEM((tokens, C), F32),
            pltpu.VMEM((tokens, C), F32),
            pltpu.VMEM((tokens, C), F32),
            pltpu.VMEM((tokens, C), BF),
            pltpu.VMEM((2, 8, C), F32),
            pltpu.VMEM((2, 8, C), F32),
        ],
        compiler_params=pltpu.CompilerParams(
            collective_id=3, has_side_effects=True, vmem_limit_bytes=62 << 20
        ),
    )(*ins, *weights, *kept, grad_second, jnp.pad(q, ((0, 4), (0, 0))), fold, small)
    square = columns[:5].reshape(5, 2, 2, 2, 80, HD).transpose(0, 1, 3, 2, 4, 5)
    wide = columns[5:].reshape(4, 2, 2, 2, 80, HD).transpose(1, 3, 2, 0, 4, 5)
    sums = [square.reshape(10, 320, HD).astype(F32), wide.reshape(2, C, HD).astype(F32)]
    return sums + [small_sum], grad_in


def forward_plain(frozen, x0, Q, time_in, text, geglu_bias, spatial_bias, cross_bias):
    time_w, conv1_w, conv2_w, in_w, self_w, self_o, cross_qw, cross_w, cross_o = frozen[:9]
    ffn_value, ffn_gate, ffn_down, out_w = frozen[9:]
    geglu_f = lax.all_gather(geglu_bias, "head", axis=1, tiled=True)

    def flat(x):
        return x.reshape(-1, C)

    act1 = silu(gn(x0, gn_stats(x0), Q[0], Q[1])).astype(BF)
    hid1 = (conv(act1, conv1_w) + through(time_in, time_w[0]) + Q[2] + Q[3]).reshape(x0.shape)
    act2 = silu(gn(hid1, gn_stats(hid1), Q[4], Q[5])).astype(BF)
    first = x0 + conv(act2, conv2_w).reshape(x0.shape) + Q[6]
    spatial_in = flat(gn(first, gn_stats(first), Q[7], Q[8]).astype(BF))
    state0 = through(spatial_in, in_w[0]) + Q[9]
    norm1 = ln(state0, ln_stats(state0), Q[10], Q[11]).astype(BF)
    self_q, self_k, self_v = (against(norm1, self_w[i]).astype(BF) for i in range(3))
    self_att = attend(self_q, self_k, self_v, spatial_bias)
    state1 = state0 + through(self_att, self_o[0]) + Q[12]
    norm2 = ln(state1, ln_stats(state1), Q[13], Q[14]).astype(BF)
    cross_q = against(norm2, cross_qw[0]).astype(BF)
    text_k, text_v = (against(text, cross_w[i]).astype(BF) for i in (0, 1))
    cross_att = attend(cross_q, text_k, text_v, cross_bias)
    state2 = state1 + through(cross_att, cross_o[0]) + Q[15]
    norm3 = ln(state2, ln_stats(state2), Q[16], Q[17]).astype(BF)
    value_in = (against(norm3, ffn_value[0]) + geglu_f[0]).astype(BF)
    gate_in = (against(norm3, ffn_gate[0]) + geglu_f[1]).astype(BF)
    mixed = (value_in.astype(F32) * gelu_erf(gate_in.astype(F32))).astype(BF)
    state3 = (state2 + through(mixed, ffn_down[0]) + Q[18]).astype(BF)
    second = flat(first) + through(state3, out_w[0]) + Q[19]
    states = (flat(hid1), flat(first), state0, state1, state2, second)
    return states + (self_q, self_k, self_v, cross_q, text_k, text_v, value_in, gate_in)


def backward_plain(frozen, saved, x0, Q, grad_second, spatial_bias, cross_bias):
    time_w, conv1_w, conv2_w, in_w, self_w, self_o, cross_qw, cross_w, cross_o = frozen[:9]
    ffn_value, ffn_gate, ffn_down, out_w = frozen[9:]
    hid1, first, state0, state1, state2 = saved[:5]
    self_q, self_k, self_v, cross_q, text_k, text_v, value_in, gate_in = saved[6:]
    hid1, first = hid1.reshape(x0.shape), first.reshape(x0.shape)
    value_in, gate_in = value_in.astype(F32), gate_in.astype(F32)

    def flat(x):
        return x.reshape(-1, C)

    def framed(x):
        return x.reshape(x0.shape)

    stats0, stats1, stats2 = gn_stats(x0), gn_stats(hid1), gn_stats(first)
    sl1, sl2, sl3 = ln_stats(state0), ln_stats(state1), ln_stats(state2)
    g_po = flat(grad_second).astype(BF)
    grad_s3 = against(g_po, out_w[0])
    g_fb = grad_s3.astype(BF)
    grad_mixed = against(g_fb, ffn_down[0])
    g_value = (gelu_exact(gate_in) * grad_mixed).astype(BF)
    g_gate = (value_in * gelu_exact_slope(gate_in) * grad_mixed).astype(BF)
    grad_n3 = through(g_value, ffn_value[0]) + through(g_gate, ffn_gate[0])
    grad_s2 = grad_s3 + ln_back(grad_n3, state2, sl3, Q[16])
    g_cb = grad_s2.astype(BF)
    (g_cq,) = attend_back(
        cross_q, text_k, text_v, cross_bias, against(g_cb, cross_o[0]).astype(BF), False
    )
    grad_s1 = grad_s2 + ln_back(through(g_cq, cross_qw[0]), state1, sl2, Q[13])
    g_sb = grad_s1.astype(BF)
    dself = attend_back(
        self_q, self_k, self_v, spatial_bias, against(g_sb, self_o[0]).astype(BF)
    )
    grad_n1 = sum(through(dself[i], self_w[i]) for i in range(3))
    grad_s0 = grad_s1 + ln_back(grad_n1, state0, sl1, Q[10])
    g_pi = grad_s0.astype(BF)
    grad_gn = framed(against(g_pi, in_w[0]))
    grad_first = grad_second + gn_back(grad_gn, first, stats2, Q[7])

    grad_act2 = framed(conv_back(grad_first.astype(BF), conv2_w))
    grad_n = silu_back(grad_act2, gn(hid1, stats1, Q[4], Q[5]))
    grad_hid1 = gn_back(grad_n, hid1, stats1, Q[4])
    grad_act1 = framed(conv_back(grad_hid1.astype(BF), conv1_w))
    grad_n = silu_back(grad_act1, gn(x0, stats0, Q[0], Q[1]))
    return (grad_first + gn_back(grad_n, x0, stats0, Q[0])).astype(BF)


def per_device(
    sizes,
    latents,
    cotangent,
    frames,
    timesteps,
    text,
    conv_weight,
    time_weight,
    frozen_params,
    spatial_square,
    cross_kv,
    spatial_ffn,
    geglu_bias,
    projections,
    feedforward,
    up_bias,
    vectors,
    projections_moment,
    feedforward_moment,
    up_bias_moment,
    vectors_moment,
    projections_average,
    feedforward_average,
    up_bias_average,
    vectors_average,
):
    Q = frozen_params
    n_head = sizes[1]
    head_index = lax.axis_index("head")
    own_frames = latents.shape[1]
    tokens = own_frames * PIX
    own_pixels = PIX // n_head
    columns = FMAX * own_pixels

    def framed(x):
        return x.reshape(own_frames, PIX, C)

    def flat(x):
        return x.reshape(tokens, C)

    def to_pixels(x):
        x = lax.all_to_all(framed(x), "head", 1, 0, tiled=True)
        return x.reshape(columns, C)

    def to_frames(x):
        x = lax.all_to_all(x.reshape(FMAX, own_pixels, C), "head", 0, 1, tiled=True)
        return x.reshape(tokens, C)

    frame_of = jnp.arange(tokens) // PIX
    spatial_bias = jnp.where(frame_of[:, None] == frame_of[None, :], 0.0, MASK_FILL).astype(F32)
    column = jnp.arange(columns)
    same_pixel = (column % own_pixels)[:, None] == (column % own_pixels)[None, :]
    key_there = (column // own_pixels)[None, :] < frames[0]
    temporal_bias = jnp.where(same_pixel & key_there, 0.0, MASK_FILL).astype(F32)
    text_len = text.shape[1]
    text_rows = 128
    cross_bias = jnp.broadcast_to(
        jnp.where(jnp.arange(text_rows)[None, :] < text_len, 0.0, MASK_FILL), (tokens, text_rows)
    ).astype(F32)
    codes = jnp.repeat(frame_table(), own_pixels, axis=0)
    own_frame = head_index * own_frames + jnp.arange(own_frames)
    frame_mask = (own_frame < frames[0]).astype(F32)[:, None, None]

    x0 = latents[0].astype(F32)
    grad_out = frame_mask * cotangent[0].astype(F32)
    arrays = frozen_arrays(conv_weight, time_weight, spatial_square, cross_kv, spatial_ffn)
    small = pack_small(vectors, up_bias)
    time_in = jax.nn.silu(time_table(timesteps)).astype(BF)
    text_pad = jnp.pad(text[0], ((0, text_rows - text_len), (0, 0)))
    if sizes == (8, 4):
        frozen, trained, small, saved = forward_fused(
            arrays,
            small,
            projections,
            feedforward,
            latents.reshape(tokens, C),
            Q,
            time_in,
            text_pad,
            geglu_bias,
        )
    else:
        frozen, trained, small = gather_plain(arrays, small, projections, feedforward)
        saved = forward_plain(
            frozen, x0, Q, time_in, text_pad, geglu_bias, spatial_bias, cross_bias
        )
    square_w, ffn_w = trained
    vector_f, bias_f = unpack_small(sizes, small, vectors, up_bias)
    second = framed(saved[5])

    stats3 = gn_stats(second)
    normed = to_pixels(gn(second, stats3, vector_f[0], vector_f[1]).astype(BF))
    entered = through(normed, square_w[0]) + vector_f[2]

    def temporal_in(x, gain_row, wq):
        stats = ln_stats(x)
        t = (ln(x, stats, vector_f[gain_row], vector_f[gain_row + 1]) + codes).astype(BF)
        qkv = [against(t, square_w[wq + i]).astype(BF) for i in range(3)]
        return stats, t, qkv

    tl1, t1, qkv1 = temporal_in(entered, 3, 3)
    att1 = attend(*qkv1, temporal_bias)
    block1 = entered + through(att1, square_w[1]) + vector_f[5]
    tl2, t2, qkv2 = temporal_in(block1, 6, 7)
    att2 = attend(*qkv2, temporal_bias)
    block2 = block1 + through(att2, square_w[6]) + vector_f[8]
    tl3 = ln_stats(block2)
    t3 = ln(block2, tl3, vector_f[9], vector_f[10]).astype(BF)
    inner = against(t3, ffn_w[0]) + bias_f
    spread = gelu_tanh(inner).astype(BF)
    stream = (block2 + through(spread, ffn_w[1]) + vector_f[11]).astype(BF)
    moved = to_frames(through(stream, square_w[2]).astype(BF)).astype(F32)
    output = (frame_mask * (second + framed(moved) + vector_f[12])).astype(BF)[None]

    g_out = to_pixels(grad_out.astype(BF))
    col = lambda v: jnp.sum(v.astype(F32), axis=0)
    G = {}
    G[2] = outer(stream, g_out)
    grad_stream = against(g_out, square_w[2])
    g_ffn = grad_stream.astype(BF)
    grad_down = outer(spread, g_ffn)
    g_inner = (gelu_tanh_slope(inner) * against(g_ffn, ffn_w[1])).astype(BF)
    grad_up = outer(g_inner, t3)
    grad_t3 = through(g_inner, ffn_w[0])
    grad_b2 = grad_stream + ln_back(grad_t3, block2, tl3, vector_f[9])
    dgain3, dshift3 = ln_param_grads(grad_t3, block2, tl3)

    def temporal_back(grad, x, stats, t, qkv, att, gain_row, wo, wq):
        low = grad.astype(BF)
        G[wo] = outer(att, low)
        dqkv = attend_back(*qkv, temporal_bias, against(low, square_w[wo]).astype(BF))
        for i in range(3):
            G[wq + i] = outer(dqkv[i], t)
        grad_t = sum(through(dqkv[i], square_w[wq + i]) for i in range(3))
        grad_x = grad + ln_back(grad_t, x, stats, vector_f[gain_row])
        return grad_x, ln_param_grads(grad_t, x, stats), col(low)

    grad_b1, (dgain2, dshift2), dbias2 = temporal_back(
        grad_b2, block1, tl2, t2, qkv2, att2, 6, 6, 7
    )
    grad_e, (dgain1, dshift1), dbias1 = temporal_back(
        grad_b1, entered, tl1, t1, qkv1, att1, 3, 1, 3
    )
    g_entry = grad_e.astype(BF)
    G[0] = outer(normed, g_entry)
    grad_normed = framed(to_frames(against(g_entry, square_w[0]).astype(BF)).astype(F32))
    z = (second - stats3[0]) * stats3[1]
    dgain0 = jnp.sum(grad_normed * z, axis=(0, 1))
    dshift0 = jnp.sum(grad_normed, axis=(0, 1))
    grad_second = grad_out + gn_back(grad_normed, second, stats3, vector_f[0])

    grad_vector = jnp.stack(
        [
            dgain0,
            dshift0,
            col(g_entry),
            dgain1,
            dshift1,
            dbias1,
            dgain2,
            dshift2,
            dbias2,
            dgain3,
            dshift3,
            col(g_ffn),
            col(g_out),
        ]
    )
    n_clip, k = sizes[0], vectors.shape[1]
    vector_blocks = grad_vector.reshape(13, n_clip, k).transpose(1, 0, 2).reshape(n_clip, -1)
    bias_blocks = col(g_inner).reshape(-1, n_clip, up_bias.shape[1]).transpose(1, 0, 2)
    small = jnp.concatenate([vector_blocks, bias_blocks.reshape(n_clip, -1)], axis=1)
    fill = -small.shape[1] % 1024
    small = jnp.pad(small, ((0, 0), (0, fill))).reshape(n_clip, -1, 128)
    parts = [G[i] for i in range(10)]
    if sizes == (8, 4):
        sums, input_gradient = backward_fused(
            parts,
            [grad_up, grad_down],
            small,
            frozen,
            saved,
            latents.reshape(tokens, C),
            flat(grad_second),
            Q,
        )
        input_gradient = framed(input_gradient)[None]
    else:
        sums = sum_plain(parts, [grad_up, grad_down], small)
        input_gradient = backward_plain(
            frozen, saved, x0, Q, grad_second, spatial_bias, cross_bias
        )[None]
    own_square, own_wide, own_small = sums
    own_small = own_small.reshape(-1)
    own_vector = own_small[: 13 * k].reshape(13, k)
    own_bias = lax.dynamic_slice_in_dim(
        own_small[13 * k : 13 * k + n_head * up_bias.size],
        head_index * up_bias.size,
        up_bias.size,
        0,
    ).reshape(up_bias.shape)

    square_parts = update(
        projections, projections_moment, projections_average, own_square, RATE_MATRIX
    )
    ffn_parts = update(feedforward, feedforward_moment, feedforward_average, own_wide, RATE_MATRIX)
    bias_parts = update(up_bias, up_bias_moment, up_bias_average, own_bias, RATE_VECTOR)
    vector_parts = update(vectors, vectors_moment, vectors_average, own_vector, RATE_VECTOR)
    return (output, input_gradient) + square_parts + ffn_parts + bias_parts + vector_parts


def solution(mesh):
    sizes = (mesh.shape["clip"], mesh.shape["head"])
    return jax.shard_map(
        functools.partial(per_device, sizes),
        mesh=mesh,
        in_specs=(
            P("clip", "head", None, None),
            P("clip", "head", None, None),
            P("clip"),
            P("clip"),
            P("clip", None, None),
            P(None, None, "head", None),
            P("head", None),
            P(),
            P(None, "head", None),
            P(None, "head", None),
            P(None, "head", None),
            P(None, "head"),
            P(None, "head", "clip"),
            P(None, "head", "clip"),
            P("head", "clip"),
            P(None, "clip"),
            P(None, "head", "clip"),
            P(None, "head", "clip"),
            P("head", "clip"),
            P(None, "clip"),
            P(None, "head", "clip"),
            P(None, "head", "clip"),
            P("head", "clip"),
            P(None, "clip"),
        ),
        out_specs=(
            P("clip", "head", None, None),
            P("clip", "head", None, None),
            P(None, "head", "clip"),
            P(None, "head", "clip"),
            P(None, "head", "clip"),
            P(None, "head", "clip"),
            P(None, "head", "clip"),
            P(None, "head", "clip"),
            P("head", "clip"),
            P("head", "clip"),
            P("head", "clip"),
            P(None, "clip"),
            P(None, "clip"),
            P(None, "clip"),
        ),
        check_vma=False,
    )
```

```python
import functools
import math

import jax
import jax.numpy as jnp
from jax import lax
from jax.experimental import pallas as pl
from jax.experimental.pallas import tpu as pltpu
from jax.sharding import PartitionSpec as P

C = 1280
HD = 160
HEADS = C // HD
GROUPS = 32
FMAX = 24
SIDE = 8
PIX = 64
TEXT_LEN = 77
BF = jnp.bfloat16
F32 = jnp.float32
MESH = pl.DeviceIdType.MESH

MOMENTUM = 0.9
RATE_MATRIX = 0.0002
RATE_VECTOR = 0.002
AVERAGE_DECAY = 0.7
GROUP_EPS = 1e-06
LAYER_EPS = 1e-05
MASK_FILL = -1e30


def place():
    c = lax.axis_index("clip")
    h = lax.axis_index("head")
    core, gx, gy = c % 2, (c // 2) % 2, c // 4
    partners = {
        "x": (c + 2 - 4 * gx, h),
        "y": (c + 4 - 8 * gy, h),
        "core": (c + 1 - 2 * core, h),
    }
    heads = [h, h + 1 - 2 * (h % 2), h + 2 - 4 * (h // 2), 3 - h]
    return c, h, core, gx, gy, partners, heads


def plane_of(core, gx, gy):
    plane = []
    for d in range(8):
        core_d, x_d, y_d = d % 2, d // 2 % 2, d // 4
        plane.append(
            (gy + y_d - 2 * gy * y_d) * 4
            + (gx + x_d - 2 * gx * x_d) * 2
            + core
            + core_d
            - 2 * core * core_d
        )
    return plane


def greet(devices):
    barrier = pltpu.get_barrier_semaphore()
    for device in devices:
        pl.semaphore_signal(barrier, inc=1, device_id=device, device_id_type=MESH)
    pl.semaphore_wait(barrier, len(devices))


class Gather:

    def __init__(self, jobs, ins, outs, send, recv, load_sem, store_sem, hold):
        self.jobs = jobs
        self.sems = (send, recv, load_sem, store_sem)
        self.hold = hold
        c, h, core, gx, gy, partners, heads = place()
        self.c, self.h, self.core, self.gx, self.gy = c, h, core, gx, gy
        self.xp, self.yp, self.cp = partners["x"], partners["y"], partners["core"]
        self.heads = heads
        self.plane = plane_of(core, gx, gy)
        self.views = [self.view(job, ins, outs) for job in jobs]

    def peers(self):
        return [(self.plane[d], self.h) for d in range(1, 8)] + [
            (self.c, self.heads[j]) for j in (1, 2, 3)
        ]

    def copy(self, a, j, kind, src, dst, device):
        return pltpu.make_async_remote_copy(
            src_ref=src,
            dst_ref=dst,
            send_sem=self.sems[0].at[a, j, kind],
            recv_sem=self.sems[1].at[a, j, kind],
            device_id=device,
            device_id_type=MESH,
        )

    def view(self, job, ins, outs):
        kind, i_ref, o_ref, lo, at, n = job[0], ins[job[1]], outs[job[2]], job[3], job[4], job[5]
        core, gx, gy, h = self.core, self.gx, self.gy, self.h
        part, into = pl.ds(lo, n), pl.ds(at, n)
        if kind == "frozen":
            shard = i_ref.shape[-2]
            rows = shard // 4
            half = o_ref.shape[-1] // 2
            lanes = pl.ds(pl.multiple_of(core * half, 128), half)
            src = i_ref.at[part, pl.ds(pl.multiple_of((gy * 2 + gx) * rows, 16), rows), lanes]

            def slot(z, y, x, n0=0, nn=n, r0=0, rr=rows):
                first = pl.multiple_of(z * shard + (y * 2 + x) * rows + r0, 16)
                return o_ref.at[pl.ds(at + n0, nn), pl.ds(first, rr), lanes]

            def bundle(z):
                return [o_ref.at[into, pl.ds(pl.multiple_of(z * shard, 16), shard), lanes]]

            own = pl.ds(pl.multiple_of(h * shard, 16), shard)
            local = [(i_ref.at[lo + i], o_ref.at[at + i, own]) for i in range(n)]
        else:
            whole = i_ref.shape[-2]
            low, rows = job[6:] if len(job) > 6 else (0, whole)
            src = i_ref.at[part, pl.ds(low, rows)]

            def slot(z, y, x, n0=0, nn=n, r0=0, rr=rows):
                first = pl.multiple_of(((z * 2 + core) * 2 + x) * whole + low + r0, 16)
                return o_ref.at[pl.ds(at + n0, nn), y, pl.ds(first, rr)]

            def bundle(z):
                first = pl.multiple_of((z * 2 + core) * 2 * whole + low, 16)
                if rows == whole:
                    return [o_ref.at[into, :, pl.ds(first, 2 * rows)]]
                return [o_ref.at[into, :, pl.ds(first + x * whole, rows)] for x in (0, 1)]

            here = pl.ds(pl.multiple_of(((h * 2 + core) * 2 + gx) * whole + low, 16), rows)
            local = [
                (i_ref.at[lo + i, pl.ds(low, rows)], o_ref.at[at + i, gy, here]) for i in range(n)
            ]
        if n >= 4 or n == 2:
            first = dict(n0=0, nn=(n + 1) // 2)
            second = dict(n0=(n + 1) // 2, nn=n - (n + 1) // 2)
        else:
            top = (rows // 2 + 15) // 16 * 16
            first, second = dict(r0=0, rr=top), dict(r0=top, rr=rows - top)
        return kind, src, slot, bundle, local, first, second

    def local_copies(self, a):
        buf = self.hold.at[a % self.hold.shape[0]]
        triples = []
        for i, (src, dst) in enumerate(self.views[a][4]):
            rows, cols = src.shape
            triples.append((src, buf.at[pl.ds(i * rows, rows), pl.ds(0, cols)], dst))
        return triples

    def numbers(self, a):
        return (1, 2, 3) if self.views[a][0] == "frozen" else (0, 1, 2, 3)

    def fetch(self, a):
        src, slot = self.views[a][1:3]
        for j in (1, 2, 3):
            there = (self.c, self.heads[j])
            self.copy(a, j, 0, src, slot(self.h, self.gy, self.gx), there).start()

    def trade(self, a):
        src, slot = self.views[a][1:3]
        locals_ = self.local_copies(a)
        for k, (inp, mid, out) in enumerate(locals_):
            pltpu.make_async_copy(inp, mid, self.sems[2].at[a, k]).start()
        for j in self.numbers(a):
            here = slot(self.heads[j], self.gy, self.gx)
            if j:
                self.copy(a, j, 0, src, here, (self.c, self.heads[j])).wait_recv()
            give = here if j else src
            self.copy(a, j, 1, give, here, self.xp).start()
            self.copy(a, j, 2, give, here, self.yp).start()
        for k, (inp, mid, out) in enumerate(locals_):
            pltpu.make_async_copy(inp, mid, self.sems[2].at[a, k]).wait()
            pltpu.make_async_copy(mid, out, self.sems[3].at[a, k]).start()

    def forward(self, a):
        kind, src, slot, bundle, local, first, second = self.views[a]
        gx, gy, xp, yp = self.gx, self.gy, self.xp, self.yp
        for j in self.numbers(a):
            z = self.heads[j]
            from_x, from_y = slot(z, gy, 1 - gx), slot(z, 1 - gy, gx)
            self.copy(a, j, 1, from_x, from_x, xp).wait_recv()
            piece = slot(z, gy, 1 - gx, **first)
            self.copy(a, j, 3, piece, piece, yp).start()
            self.copy(a, j, 2, from_y, from_y, yp).wait_recv()
            piece = slot(z, 1 - gy, gx, **second)
            self.copy(a, j, 4, piece, piece, xp).start()
        for k, (inp, mid, out) in enumerate(self.local_copies(a)):
            pltpu.make_async_copy(mid, out, self.sems[3].at[a, k]).wait()

    def share(self, a):
        kind, src, slot, bundle, local, first, second = self.views[a]
        gx, gy, xp, yp = self.gx, self.gy, self.xp, self.yp
        for j in self.numbers(a):
            z = self.heads[j]
            piece = slot(z, 1 - gy, 1 - gx, **first)
            self.copy(a, j, 3, piece, piece, yp).wait_recv()
            piece = slot(z, 1 - gy, 1 - gx, **second)
            self.copy(a, j, 4, piece, piece, xp).wait_recv()
            for i, whole in enumerate(bundle(z)):
                self.copy(a, j, 5 + i, whole, whole, self.cp).start()

    def finish(self, a):
        kind, src, slot, bundle, local, first, second = self.views[a]
        gx, gy, xp, yp = self.gx, self.gy, self.xp, self.yp
        for j in self.numbers(a):
            z = self.heads[j]
            for i, whole in enumerate(bundle(z)):
                self.copy(a, j, 5 + i, whole, whole, self.cp).wait()
            here = slot(z, gy, gx)
            give = here if j else src
            if j:
                self.copy(a, j, 0, src, here, (self.c, z)).wait_send()
            self.copy(a, j, 1, give, here, xp).wait_send()
            self.copy(a, j, 2, give, here, yp).wait_send()
            piece = slot(z, gy, 1 - gx, **first)
            self.copy(a, j, 3, piece, piece, yp).wait_send()
            piece = slot(z, 1 - gy, gx, **second)
            self.copy(a, j, 4, piece, piece, xp).wait_send()

    def run(self, units, ahead=2):
        count = len(self.jobs)
        done, at = 0, 0

        def work(most):
            nonlocal at
            while at < len(units) and units[at][0] <= done and most > 0:
                units[at][1]()
                at += 1
                most -= 1

        for a in range(min(ahead, count)):
            self.fetch(a)
        work(2)
        for step in range(count + 3):
            if step < count:
                self.trade(step)
                work(2)
            if step + ahead < count:
                self.fetch(step + ahead)
            if 0 <= step - 1 < count:
                self.forward(step - 1)
                work(2)
            if 0 <= step - 2 < count:
                self.share(step - 2)
                work(2)
            if 0 <= step - 3 < count:
                self.finish(step - 3)
                done = step - 2
                work(2)
        work(len(units))


FROZEN = [(0, 0, 1), (1, 0, 9), (1, 9, 9), (2, 0, 1), (2, 1, 3), (2, 4, 1), (2, 5, 1)]
FROZEN += [(3, 0, 2), (2, 6, 1), (4, 0, 1), (4, 1, 1), (4, 2, 1), (2, 7, 1)]


def frozen_arrays(conv_weight, time_weight, spatial_square, cross_kv, spatial_ffn):
    return [
        time_weight[None],
        conv_weight.reshape((18,) + conv_weight.shape[2:]),
        spatial_square,
        cross_kv,
        spatial_ffn,
    ]


def gather_plain(arrays, small, projections, feedforward):
    small = lax.all_gather(lax.all_gather(small, "head", axis=0), "clip", axis=0)
    frozen = [
        lax.all_gather(arrays[i][lo : lo + n], "head", axis=1, tiled=True) for i, lo, n in FROZEN
    ]
    trained = [
        lax.all_gather(
            lax.all_gather(a.astype(BF), "clip", axis=2, tiled=True), "head", axis=1, tiled=True
        )
        for a in (projections, feedforward)
    ]
    return frozen, trained, small


TILE = 256


def stream(count, tiles, body, sem, slots):
    def begin(i):
        for p, (src, dst) in enumerate(tiles(i, i % slots)):
            pltpu.make_async_copy(src, dst, sem.at[i % slots, p]).start()

    for i in range(min(slots - 1, count)):
        begin(i)

    def step(i, carry):
        @pl.when(i + slots - 1 < count)
        def _():
            begin(i + slots - 1)

        for p, (src, dst) in enumerate(tiles(i, i % slots)):
            pltpu.make_async_copy(src, dst, sem.at[i % slots, p]).wait()
        body(i, i % slots)
        return carry

    lax.fori_loop(0, count, step, 0)


def tile_at(i):
    return pl.ds(pl.multiple_of(i * TILE, TILE), TILE)


def through_tiles(x, w, buf, sem, sink):
    slots = buf.shape[0]

    def tiles(i, slot):
        return [(w.at[:, tile_at(i)], buf.at[slot])]

    def body(i, slot):
        sink(tile_at(i), dot_f32(x[...], buf[slot], ((1,), (0,))))

    stream(w.shape[1] // TILE, tiles, body, sem, slots)


def against_tiles(x, w, buf, sem, sink):
    slots, width = buf.shape[0], w.shape[1]
    lanes = pl.ds(0, width)

    def tiles(i, slot):
        return [(w.at[tile_at(i)], buf.at[slot, :, lanes])]

    def body(i, slot):
        sink(tile_at(i), dot_f32(x[...], buf[slot, :, lanes], ((1,), (1,))))

    stream(w.shape[0] // TILE, tiles, body, sem, slots)


def frame_rows(f):
    return pl.ds(pl.multiple_of(f * PIX, PIX), PIX)


def norm_rows(x, q, gain, out, codes=None):
    block = PIX if codes is None else x.shape[0] // FMAX

    def body(f, carry):
        rows = pl.ds(pl.multiple_of(f * block, block), block)
        v = x[rows, :]
        v = v - jnp.mean(v, axis=1, keepdims=True)
        scale = lax.rsqrt(jnp.mean(v * v, axis=1, keepdims=True) + LAYER_EPS)
        v = v * scale * q[gain : gain + 1] + q[gain + 1 : gain + 2]
        if codes is not None:
            v = v + codes[pl.ds(f, 1), :]
        out[rows, :] = v.astype(out.dtype)
        return carry

    lax.fori_loop(0, x.shape[0] // block, body, 0)


def dot_exact(a, b):
    return lax.dot_general(
        a, b, (((1,), (0,)), ((), ())), precision=lax.Precision.HIGHEST, preferred_element_type=F32
    )


def group_spread(sums, fold):
    means = dot_exact(sums, fold[...]) * (1.0 / (C // GROUPS * PIX))
    return lax.dot_general(
        means,
        fold[...],
        (((1,), (1,)), ((), ())),
        precision=lax.Precision.HIGHEST,
        preferred_element_type=F32,
    )


def group_stats(x, fold, stat):
    frames = x.shape[0] // PIX
    stat[0] = jnp.zeros_like(stat[0])
    stat[1] = jnp.zeros_like(stat[1])
    for f in range(frames):
        block = x[f * PIX : (f + 1) * PIX, :].astype(F32)
        stat[0, f : f + 1] = jnp.sum(block, axis=0, keepdims=True)
    stat[0] = group_spread(stat[0], fold)
    for f in range(frames):
        block = x[f * PIX : (f + 1) * PIX, :].astype(F32) - stat[0, f : f + 1]
        stat[1, f : f + 1] = jnp.sum(block * block, axis=0, keepdims=True)
    stat[1] = lax.rsqrt(group_spread(stat[1], fold) + GROUP_EPS)


def group_apply(x, stat, q, gain, out, act):
    for f in range(x.shape[0] // PIX):
        rows = slice(f * PIX, (f + 1) * PIX)
        v = (x[rows, :].astype(F32) - stat[0, f : f + 1]) * stat[1, f : f + 1]
        out[rows, :] = act(v * q[gain : gain + 1] + q[gain + 1 : gain + 2]).astype(out.dtype)


def group_matrix():
    group = jnp.arange(C) // (C // GROUPS)
    return (group[:, None] == jnp.arange(128)[None, :]).astype(F32)


def make_windows(x, win, flipped):
    tokens = x.shape[0]

    def body(j, carry):
        lanes = pl.ds(pl.multiple_of(j * 128, 128), 128)
        v = x[:, lanes]
        row = lax.broadcasted_iota(jnp.int32, v.shape, 0)
        py, px = row // SIDE % SIDE, row % SIDE
        for tap in range(9):
            dy, dx = tap // 3 - 1, tap % 3 - 1
            if flipped:
                dy, dx = -dy, -dx
            shift = (-(dy * SIDE + dx)) % tokens
            moved = pltpu.roll(v, shift, 0) if shift else v
            ok = (py + dy >= 0) & (py + dy < SIDE) & (px + dx >= 0) & (px + dx < SIDE)
            win[tap, :, lanes] = jnp.where(ok, moved, 0.0).astype(win.dtype)
        return carry

    lax.fori_loop(0, C // 128, body, 0)


def silu(v):
    return v / (1.0 + jnp.exp(-v))


ORDER = (0, 3, 4, 5, 1, 7, 8, 9, 6, 2)
AT = tuple(ORDER.index(i) for i in range(10))


def forward_kernel(jobs, needs, n_saved, *refs):
    ins, refs = refs[:5], refs[5:]
    square_blocks, wide_blocks, cot, vec_own, up_own = refs[:5]
    lat, q, time_in, text, gate_bias, fold, codes, tbias = refs[5:13]
    outs, refs = refs[13:28], refs[28:]
    saved, refs = refs[:n_saved], refs[n_saved:]
    g_pixels, vf, text_k, text_v = refs[:4]
    (
        send, recv, load_sem, store_sem, hold,
        bias_send, bias_recv, bias_all, col_sem, row_sem, save_sem,
        plane_send, plane_recv, hop_send, hop_recv, keep_sem, in_sem,
        square_land, wide_land, vec_land, up_land, square_full, wide_full, up_mine, up_all,
        win, col_buf, row_buf, stage, acc, tmp, nrm, att, stat, extra,
        hid1, first, state0, state1, state2, second, self_q, self_k, self_v, cross_q,
    ) = refs[4:]
    (time_w, conv1, conv2, in_w, qkv_w, self_o, cross_w, text_w, cross_o, value_w, gate_w,
     down_w, out_w, square_w, wide_w) = outs
    value_out, gate_out, inner_out, normed_out = saved[10:14]
    comm = Gather(
        jobs, list(ins) + [square_full, wide_full], outs, send, recv, load_sem, store_sem, hold
    )
    greet(comm.peers())
    c, h, heads, plane = comm.c, comm.h, comm.heads, comm.plane
    share = lat.shape[0] // 4

    def bias_copy(j):
        return pltpu.make_async_remote_copy(
            src_ref=gate_bias,
            dst_ref=bias_all.at[comm.h],
            send_sem=bias_send.at[j],
            recv_sem=bias_recv.at[j],
            device_id=(comm.c, comm.heads[j]),
            device_id_type=MESH,
        )

    for j in (1, 2, 3):
        bias_copy(j).start()
    bias_all[comm.h] = gate_bias[...]

    def bias_in():
        for j in (1, 2, 3):
            bias_copy(j).wait()

    def plane_copies():
        copies = []
        for d in range(1, 8):
            parts = (
                (square_blocks.at[plane[d]], square_land.at[c]),
                (wide_blocks.at[plane[d]], wide_land.at[c]),
                (vec_own, vec_land.at[c]),
                (up_own, up_land.at[c]),
            )
            for i, (src, dst) in enumerate(parts):
                copies.append(
                    pltpu.make_async_remote_copy(
                        src_ref=src,
                        dst_ref=dst,
                        send_sem=plane_send.at[i, d],
                        recv_sem=plane_recv.at[i, d],
                        device_id=(plane[d], h),
                        device_id_type=MESH,
                    )
                )
        return copies

    def plane_own():
        return [
            pltpu.make_async_copy(square_blocks.at[c], square_land.at[c], plane_send.at[0, 0]),
            pltpu.make_async_copy(wide_blocks.at[c], wide_land.at[c], plane_send.at[1, 0]),
        ]

    for item in plane_copies() + plane_own():
        item.start()
    vec_land[c] = vec_own[...]
    up_land[c] = up_own[...]

    def up_copy(j):
        return pltpu.make_async_remote_copy(
            src_ref=up_mine,
            dst_ref=up_all.at[h],
            send_sem=hop_send.at[2, j],
            recv_sem=hop_recv.at[2, j],
            device_id=(c, heads[j]),
            device_id_type=MESH,
        )

    def assemble_unit():
        for item in plane_copies() + plane_own():
            item.wait()
        for i in range(8):
            lanes = slice(i * HD, (i + 1) * HD)
            square_full[:, :, lanes] = square_land[i]
            wide_full[0, :, lanes] = wide_land[i]
            vf[:, lanes] = vec_land[i].astype(BF).astype(F32)
            up_mine[:, i * 16 : (i + 1) * 16] = up_land[i].astype(BF).astype(F32)
        for j in (1, 2, 3):
            up_copy(j).start()
        up_all[h] = up_mine[...]

    def cot_copies():
        at = g_pixels.at[pl.ds(h * cot.shape[0], cot.shape[0])]
        return [
            pltpu.make_async_remote_copy(
                src_ref=cot.at[:, heads[j]],
                dst_ref=at,
                send_sem=hop_send.at[0, j],
                recv_sem=hop_recv.at[0, j],
                device_id=(c, heads[j]),
                device_id_type=MESH,
            )
            for j in (1, 2, 3)
        ]

    def cot_own():
        at = g_pixels.at[pl.ds(h * cot.shape[0], cot.shape[0])]
        return pltpu.make_async_copy(cot.at[:, h], at, hop_send.at[0, 0])

    for item in cot_copies() + [cot_own()]:
        item.start()

    def keep(i, src):
        pltpu.make_async_copy(src, saved[i], keep_sem.at[i]).start()

    def kept(*pairs):
        for i, src in pairs:
            pltpu.make_async_copy(src, saved[i], keep_sem.at[i]).wait()

    def time_unit():
        def sink(lanes, tile):
            extra[:, lanes] = tile + q[2:3, lanes] + q[3:4, lanes]

        through_tiles(time_in, time_w.at[0], col_buf, col_sem, sink)

    def act1_unit():
        group_stats(lat, fold, stat)
        group_apply(lat, stat, q, 0, tmp, silu)

    def windows_unit():
        make_windows(tmp, win, False)

    def conv_unit(w, tap):
        def sink(lanes, tile):
            if tap == 0:
                acc[:, lanes] = tile
            else:
                acc[:, lanes] += tile

        through_tiles(win.at[tap], w.at[tap], col_buf, col_sem, sink)

    def act2_unit():
        hid1[...] = acc[...] + extra[0:1]
        keep(0, hid1)
        group_stats(hid1, fold, stat)
        group_apply(hid1, stat, q, 4, tmp, silu)

    def first_unit():
        first[...] = lat[...].astype(F32) + acc[...] + q[6:7]
        keep(1, first)
        group_stats(first, fold, stat)
        group_apply(first, stat, q, 7, nrm, lambda v: v)

    def add_unit(x, w, base, bias, out, norm, at):
        def sink(lanes, tile):
            total = tile + q[bias : bias + 1, lanes]
            out[:, lanes] = total if base is None else total + base[:, lanes]

        through_tiles(x, w.at[0], col_buf, col_sem, sink)
        keep(at, out)
        if norm is not None:
            norm_rows(out, q, norm, nrm)

    def project_unit(x, w, out, at=None):
        def sink(lanes, tile):
            out[:, lanes] = tile.astype(BF)

        against_tiles(x, w, row_buf, row_sem, sink)
        if at is not None:
            keep(at, out)

    def attend_unit(qr, kr, vr, bias):
        attend_body(qr, kr, vr, bias, att, tmp)

    def save(i, k):
        dst = (value_out, gate_out)[k].at[:, tile_at(i)]
        return pltpu.make_async_copy(stage.at[i % 2, k], dst, save_sem.at[i % 2, k])

    def ffn_unit(part, parts):
        per = value_w.shape[1] // TILE // parts
        start = part * per

        def tiles(i, slot):
            rows = tile_at(start + i)
            return [
                (value_w.at[0, rows], row_buf.at[slot * 3]),
                (gate_w.at[0, rows], row_buf.at[slot * 3 + 1]),
                (down_w.at[0, rows], row_buf.at[slot * 3 + 2]),
            ]

        def body(i, slot):
            tile = start + i
            lanes = tile_at(tile % 5)
            z = tile // 5
            x = nrm[...]
            value = dot_f32(x, row_buf[slot * 3], ((1,), (1,))) + bias_all[z, 0:1, lanes]
            gate = dot_f32(x, row_buf[slot * 3 + 1], ((1,), (1,))) + bias_all[z, 1:2, lanes]
            mixed = (value * gelu_erf(gate)).astype(BF)

            @pl.when(tile >= 2)
            def _():
                save(tile - 2, 0).wait()
                save(tile - 2, 1).wait()

            stage[tile % 2, 0] = value.astype(BF)
            stage[tile % 2, 1] = gate.astype(BF)
            save(tile, 0).start()
            save(tile, 1).start()
            acc[...] += dot_f32(mixed, row_buf[slot * 3 + 2], ((1,), (0,)))

        if part == 0:
            acc[...] = state2[...] + q[18:19]
        stream(per, tiles, body, row_sem, 2)
        if part == parts - 1:
            for tile in (value_w.shape[1] // TILE - 2, value_w.shape[1] // TILE - 1):
                save(tile, 0).wait()
                save(tile, 1).wait()
            nrm[...] = acc[...].astype(BF)

    def gone_unit():
        group_stats(second, fold, stat)
        per = PIX // 4
        for f in range(second.shape[0] // PIX):
            v = second[f * PIX : (f + 1) * PIX, :]
            v = (v - stat[0, f : f + 1]) * stat[1, f : f + 1]
            v = (v * vf[0:1] + vf[1:2]).astype(BF)
            for z in range(4):
                win[8, pl.ds(z * share + f * per, per), :] = v[z * per : (z + 1) * per]
        for item in hop_copies() + [hop_own()]:
            item.start()

    def hop_rows(z):
        return pl.ds(pl.multiple_of(z * share, 16), share)

    def hop_copies():
        return [
            pltpu.make_async_remote_copy(
                src_ref=win.at[8, hop_rows(heads[j])],
                dst_ref=normed_out.at[hop_rows(h)],
                send_sem=hop_send.at[1, j],
                recv_sem=hop_recv.at[1, j],
                device_id=(c, heads[j]),
                device_id_type=MESH,
            )
            for j in (1, 2, 3)
        ]

    def hop_own():
        src = win.at[8, hop_rows(h)]
        return pltpu.make_async_copy(src, normed_out.at[hop_rows(h)], hop_send.at[1, 0])

    def arrive_unit():
        for item in hop_copies() + [hop_own()]:
            item.wait()
        item = pltpu.make_async_copy(normed_out, nrm, in_sem.at[0])
        item.start()
        item.wait()
        for item in cot_copies() + [cot_own()]:
            item.wait()
        for j in (1, 2, 3):
            up_copy(j).wait()
        kept((0, hid1), (2, state0), (3, state1))
        kept((6, self_q), (7, self_k), (8, self_v), (9, cross_q))

    def motion_add_unit(x, wi, base, bias, out, norm, at, tat, code, before):
        def sink(lanes, tile):
            total = tile + vf[bias : bias + 1, lanes]
            out[:, lanes] = total if base is None else total + base[:, lanes]

        through_tiles(x, square_w.at[AT[wi] // 2, AT[wi] % 2], col_buf, col_sem, sink)
        keep(at, out)
        kept(*before)
        norm_rows(out, vf, norm, nrm, codes if code else None)
        keep(tat, nrm)

    def motion_project_unit(wi, out, at, before):
        kept(*before)
        project_unit(nrm, square_w.at[AT[wi] // 2, AT[wi] % 2], out, at)

    def motion_attend_unit(at, before):
        kept(*before)
        attend_body(self_q, self_k, self_v, tbias, att, tmp)
        keep(at, att)

    def inner_copy(i):
        src = stage.at[i % 2, 0]
        return pltpu.make_async_copy(src, inner_out.at[:, tile_at(i)], save_sem.at[i % 2, 0])

    def wide_unit(part, parts):
        count = wide_w.shape[2] // TILE
        per = count // parts
        start = part * per

        def tiles(i, slot):
            rows = tile_at(start + i)
            return [
                (wide_w.at[0, 0, rows], row_buf.at[slot * 3]),
                (wide_w.at[0, 1, rows], row_buf.at[slot * 3 + 1]),
            ]

        def body(i, slot):
            tile = start + i
            z, row = tile // 5, tile % 5 * 2
            bias = [up_all[z, pl.ds(row + k, 1), :] for k in (0, 1)]
            inner = dot_f32(nrm[...], row_buf[slot * 3], ((1,), (1,)))
            inner = inner + jnp.concatenate(bias, axis=1)

            @pl.when(tile >= 2)
            def _():
                inner_copy(tile - 2).wait()

            stage[tile % 2, 0] = inner.astype(BF)
            inner_copy(tile).start()
            acc[...] += dot_f32(gelu_tanh(inner).astype(BF), row_buf[slot * 3 + 1], ((1,), (0,)))

        if part == 0:
            acc[...] = state1[...] + vf[11:12]
        stream(per, tiles, body, row_sem, 2)
        if part == parts - 1:
            for tile in (count - 2, count - 1):
                inner_copy(tile).wait()
            kept((19, nrm))
            nrm[...] = acc[...].astype(BF)
            keep(22, nrm)

    def nothing():
        pass

    P_ = functools.partial
    units = [(0, act1_unit), (0, windows_unit), (0, assemble_unit), (needs["time"], time_unit)]
    units += [(needs["conv1", t], P_(conv_unit, conv1, t)) for t in range(9)]
    units += [(0, act2_unit), (0, windows_unit)]
    units += [(needs["conv2", t], P_(conv_unit, conv2, t)) for t in range(9)]
    units += [(0, first_unit)]
    units += [(needs["in"], P_(add_unit, nrm, in_w, None, 9, state0, 10, 2))]
    units += [
        (needs["qkv"], P_(project_unit, nrm, qkv_w.at[i], o, 6 + i))
        for i, o in enumerate((self_q, self_k, self_v))
    ]
    units += [(0, P_(attend_unit, self_q, self_k, self_v, spatial_mask))]
    units += [(needs["self_o"], P_(add_unit, att, self_o, state0, 12, state1, 13, 3))]
    units += [(needs["cross"], P_(project_unit, nrm, cross_w.at[0], cross_q, 9))]
    units += [(needs["text"], P_(project_unit, text, text_w.at[0], text_k))]
    units += [(needs["text"], P_(project_unit, text, text_w.at[1], text_v))]
    units += [(0, P_(attend_unit, cross_q, text_k, text_v, text_mask))]
    units += [(needs["cross_o"], P_(add_unit, att, cross_o, state1, 15, state2, 16, 4))]
    units += [(0, bias_in)]
    units += [(needs["ffn"], P_(ffn_unit, i, 5)) for i in range(5)]
    units += [(needs["out"], P_(add_unit, nrm, out_w, first, 19, second, None, 5))]
    entered, block1, block2 = hid1, state0, state1
    qkv = (self_q, self_k, self_v)
    units += [(0, gone_unit), (0, nothing), (0, nothing), (0, nothing), (0, arrive_unit)]
    units += [
        (
            needs["square", 0],
            P_(motion_add_unit, nrm, 0, None, 2, entered, 3, 14, 17, True, ()),
        )
    ]
    units += [
        (needs["square", 3 + i], P_(motion_project_unit, 3 + i, o, 23 + i, ()))
        for i, o in enumerate(qkv)
    ]
    units += [(0, P_(motion_attend_unit, 20, ()))]
    units += [
        (
            needs["square", 1],
            P_(motion_add_unit, att, 1, entered, 5, block1, 6, 15, 18, True, ((17, nrm),)),
        )
    ]
    units += [
        (needs["square", 7 + i], P_(motion_project_unit, 7 + i, o, 26 + i, ((23 + i, o),)))
        for i, o in enumerate(qkv)
    ]
    units += [(0, P_(motion_attend_unit, 21, ((20, att),)))]
    units += [
        (
            needs["square", 6],
            P_(motion_add_unit, att, 6, block1, 8, block2, 9, 16, 19, False, ((18, nrm),)),
        )
    ]
    units += [(needs["wide"], P_(wide_unit, i, 5)) for i in range(5)]
    comm.run(units)
    kept((1, first), (4, state2), (5, second), (14, entered), (15, block1), (16, block2))
    kept((21, att), (22, nrm))
    kept(*[(26 + i, o) for i, o in enumerate(qkv)])


def forward_fused(
    arrays, projections, feedforward, vectors, up_bias, lat, cot, q, time_in, text, gate_bias, tbias
):
    tokens = lat.shape[0]
    square = jnp.stack([projections[i] for i in ORDER]).astype(BF)
    square = square.reshape(5, 2, 2, 2, 80, HD).transpose(1, 3, 2, 0, 4, 5).reshape(8, 5, 80, HD)
    wide = feedforward.astype(BF).reshape(2, 2, 2, 320, HD).transpose(0, 2, 1, 3, 4)
    ins = list(arrays)
    shapes, jobs, needs = [], [], {}
    names = ["time", "conv1", "conv2", "in", "qkv", "self_o", "cross", "text", "cross_o"]
    names += ["value", "gate", "ffn", "out"]
    for o, (i, lo, n) in enumerate(FROZEN):
        rows, cols = ins[i].shape[1:]
        shapes.append((n, 4 * rows, cols))
        step = 3 if n == 9 else n
        for at in range(0, n, step):
            jobs.append(("frozen", i, o, lo + at, at, step))
            if n == 9:
                for t in range(at, at + step):
                    needs[names[o], t] = len(jobs)
        needs[names[o]] = len(jobs)
    shapes += [(5, 2, C, C), (1, 2, 4 * C, C)]
    for k in range(5):
        jobs.append(("own", 5, 13, k, k, 1))
        for i in ORDER[2 * k : 2 * k + 2]:
            needs["square", i] = len(jobs)
    jobs += [("own", 6, 14, 0, 0, 1, low, 80) for low in range(0, 320, 80)]
    needs["wide"] = len(jobs)
    count = len(jobs)
    most = max(j[5] * ins[j[1]].shape[1] for j in jobs if j[0] == "frozen")
    any_spec, vmem = pl.BlockSpec(memory_space=pl.ANY), pl.BlockSpec(memory_space=pltpu.VMEM)
    dma = pltpu.SemaphoreType.DMA

    def array(shape, dtype=BF):
        return jax.ShapeDtypeStruct(shape, dtype)

    f32, low, hidden = array((tokens, C), F32), array((tokens, C)), array((tokens, 4 * C))
    saved = [f32] * 6 + [low] * 4 + [hidden] * 3 + [low] + [f32] * 3 + [low] * 12
    outs = pl.pallas_call(
        functools.partial(forward_kernel, jobs, needs, len(saved)),
        out_shape=tuple(array(shape) for shape in shapes)
        + tuple(saved)
        + (
            array((FMAX, tokens // FMAX, C)),
            array((16, C), F32),
            array((text.shape[0], C)),
            array((text.shape[0], C)),
        ),
        in_specs=[any_spec] * 8 + [vmem] * 10,
        out_specs=(any_spec,) * (len(shapes) + len(saved) + 1) + (vmem,) * 3,
        scratch_shapes=[
            dma((count, 4, 7)),
            dma((count, 4, 7)),
            dma((count, 4)),
            dma((count, 4)),
            pltpu.VMEM((2, most, C), BF),
            dma((4,)),
            dma((4,)),
            pltpu.VMEM((4, 8, C), F32),
            dma((2, 1)),
            dma((6, 3)),
            dma((2, 2)),
            dma((4, 8)),
            dma((4, 8)),
            dma((3, 4)),
            dma((3, 4)),
            dma((len(saved),)),
            dma((1,)),
            pltpu.VMEM((8, 5, 80, HD), BF),
            pltpu.VMEM((8, 320, HD), BF),
            pltpu.VMEM((8, 16, HD), F32),
            pltpu.VMEM((8, 16, 16), F32),
            pltpu.VMEM((5, 80, C), BF),
            pltpu.VMEM((1, 320, C), BF),
            pltpu.VMEM((16, 128), F32),
            pltpu.VMEM((4, 16, 128), F32),
            pltpu.VMEM((9, tokens, C), BF),
            pltpu.VMEM((2, C, TILE), BF),
            pltpu.VMEM((6, TILE, C), BF),
            pltpu.VMEM((2, 2, tokens, TILE), BF),
            pltpu.VMEM((tokens, C), F32),
            pltpu.VMEM((tokens, C), F32),
            pltpu.VMEM((tokens, C), BF),
            pltpu.VMEM((tokens, C), BF),
            pltpu.VMEM((2, 8, C), F32),
            pltpu.VMEM((16, C), F32),
        ]
        + [pltpu.VMEM((tokens, C), F32)] * 6
        + [pltpu.VMEM((tokens, C), BF)] * 4,
        compiler_params=pltpu.CompilerParams(
            collective_id=1, has_side_effects=True, vmem_limit_bytes=60 << 20
        ),
    )(
        *ins,
        square,
        wide.reshape(8, 320, HD),
        cot.reshape(tokens // PIX, 4, PIX // 4, C),
        jnp.pad(vectors, ((0, 3), (0, 0))),
        jnp.pad(up_bias, ((0, 6), (0, 0))),
        lat,
        jnp.pad(q, ((0, 4), (0, 0))),
        jnp.pad(time_in, ((0, 15), (0, 0))),
        text,
        jnp.pad(gate_bias, ((0, 6), (0, 0))),
        group_matrix(),
        frame_table(),
        tbias,
    )
    frozen, trained, kept = outs[:13], (outs[13].reshape(10, C, C), outs[14][0]), outs[15:44]
    g_pixels, vf, text_k, text_v = outs[44:]
    states = tuple(kept[:10]) + (text_k, text_v) + tuple(kept[10:12])
    motion = (kept[13],) + tuple(kept[14:22]) + (kept[12],) + tuple(kept[22:29])
    return frozen, trained, states, motion, g_pixels.reshape(tokens, C), vf


def pack_small(vectors, up_bias):
    flat = jnp.concatenate([a.astype(BF).reshape(-1) for a in (vectors, up_bias)])
    return jnp.pad(flat, (0, 32 * C - flat.shape[0])).reshape(32, C)


def unpack_small(sizes, packed, vectors, up_bias):
    packed = packed.reshape(sizes[0], sizes[1], -1).astype(F32)
    vector = packed[:, 0, : vectors.size].reshape((sizes[0],) + vectors.shape)
    bias = packed[:, :, vectors.size : vectors.size + up_bias.size]
    bias = bias.reshape(sizes + up_bias.shape).transpose(1, 2, 0, 3)
    return vector.transpose(1, 0, 2).reshape(vectors.shape[0], C), bias.reshape(1, -1)


def sum_plain(parts, wide_parts, small):
    sums = [
        jnp.stack(
            [
                lax.psum_scatter(
                    lax.psum_scatter(g, "head", scatter_dimension=0, tiled=True),
                    "clip",
                    scatter_dimension=1,
                    tiled=True,
                ).astype(F32)
                for g in a
            ]
        )
        for a in (parts, wide_parts)
    ]
    return sums + [lax.psum(small, ("clip", "head"))]


def head_window(head):
    start = head * HD // 128 * 128
    return start, head * HD - start


def lane_mask(shape, low):
    lane = lax.broadcasted_iota(jnp.int32, shape, 1)
    return (lane >= low) & (lane < low + HD)


def dot_f32(a, b, dims):
    return lax.dot_general(a, b, (dims, ((), ())), preferred_element_type=F32)


def spatial_mask(shape):
    row = lax.broadcasted_iota(jnp.int32, shape, 0)
    return row // PIX == lax.broadcasted_iota(jnp.int32, shape, 1) // PIX


def text_mask(shape):
    return lax.broadcasted_iota(jnp.int32, shape, 1) < TEXT_LEN


def head_probs(q, k, bias):
    scores = dot_f32(q, k, ((1,), (1,))) * HD ** (-0.5)
    if callable(bias):
        scores = jnp.where(bias(scores.shape), scores, MASK_FILL)
    else:
        scores = scores + bias[...]
    top = jnp.max(scores, axis=1, keepdims=True)
    weights = jnp.exp(scores - top)
    return weights / jnp.sum(weights, axis=1, keepdims=True)


def attend_body(q_ref, k_ref, v_ref, bias_ref, o_ref, acc):
    acc[...] = jnp.zeros_like(acc)
    for head in range(HEADS):
        start, low = head_window(head)
        win = pl.ds(start, 256)
        q = q_ref[:, win]
        mask = lane_mask(q.shape, low)
        q = jnp.where(mask, q, jnp.zeros_like(q))
        probs = head_probs(q, k_ref[:, win], bias_ref)
        out = dot_f32(probs.astype(BF), v_ref[:, win], ((1,), (0,)))
        acc[:, win] += jnp.where(mask, out, 0.0)
    o_ref[...] = acc[...].astype(BF)


def attend(q, k, v, bias):
    return pl.pallas_call(
        attend_body,
        out_shape=jax.ShapeDtypeStruct(q.shape, BF),
        scratch_shapes=[pltpu.VMEM(q.shape, F32)],
        compiler_params=pltpu.CompilerParams(vmem_limit_bytes=40 << 20),
    )(q, k, v, bias)


def attend_back_body(with_keys, q_ref, k_ref, v_ref, bias_ref, g_ref, *refs):
    if with_keys:
        dq_ref, dk_ref, dv_ref, dq, dk, dv = refs
        dk[...] = jnp.zeros_like(dk)
        dv[...] = jnp.zeros_like(dv)
    else:
        dq_ref, dq = refs
    dq[...] = jnp.zeros_like(dq)
    for head in range(HEADS):
        start, low = head_window(head)
        win = pl.ds(start, 256)
        q, k, v, g = q_ref[:, win], k_ref[:, win], v_ref[:, win], g_ref[:, win]
        mask = lane_mask(q.shape, low)
        q = jnp.where(mask, q, jnp.zeros_like(q))
        g = jnp.where(mask, g, jnp.zeros_like(g))
        probs = head_probs(q, k, bias_ref)
        dp = dot_f32(g, v, ((1,), (1,)))
        ds = probs * (dp - jnp.sum(dp * probs, axis=1, keepdims=True)) * HD ** (-0.5)
        ds = ds.astype(BF)
        dq[:, win] += jnp.where(mask, dot_f32(ds, k, ((1,), (0,))), 0.0)
        if with_keys:
            dk[:, win] += dot_f32(ds, q, ((0,), (0,)))
            dv[:, win] += dot_f32(probs.astype(BF), g, ((0,), (0,)))
    dq_ref[...] = dq[...].astype(BF)
    if with_keys:
        dk_ref[...] = dk[...].astype(BF)
        dv_ref[...] = dv[...].astype(BF)


def attend_back(q, k, v, bias, g, with_keys=True):
    count = 3 if with_keys else 1
    return pl.pallas_call(
        functools.partial(attend_back_body, with_keys),
        out_shape=(jax.ShapeDtypeStruct(q.shape, BF),) * count,
        scratch_shapes=[pltpu.VMEM(q.shape, F32)] * count,
        compiler_params=pltpu.CompilerParams(vmem_limit_bytes=48 << 20),
    )(q, k, v, bias, g)


def group_mean(per_channel):
    width = C // GROUPS
    means = jnp.mean(per_channel.reshape(-1, GROUPS, width), axis=-1) / PIX
    return jnp.repeat(means, width, axis=1)[:, None, :]


def gn_stats(x):
    center = group_mean(jnp.sum(x, axis=1))
    centered = x - center
    variance = group_mean(jnp.sum(centered * centered, axis=1))
    return center, lax.rsqrt(variance + GROUP_EPS)


def gn(x, stats, gain, shift):
    return (x - stats[0]) * stats[1] * gain + shift


def gn_back(dy, x, stats, gain):
    z = (x - stats[0]) * stats[1]
    gd = dy * gain
    mean_gd = group_mean(jnp.sum(gd, axis=1))
    mean_gz = group_mean(jnp.sum(gd * z, axis=1))
    return (gd - mean_gd - z * mean_gz) * stats[1]


def ln_stats(x):
    center = jnp.mean(x, axis=-1, keepdims=True)
    centered = x - center
    variance = jnp.mean(centered * centered, axis=-1, keepdims=True)
    return center, lax.rsqrt(variance + LAYER_EPS)


def ln(x, stats, gain, shift):
    return (x - stats[0]) * stats[1] * gain + shift


def ln_back(dy, x, stats, gain):
    z = (x - stats[0]) * stats[1]
    gd = dy * gain
    mean_gd = jnp.mean(gd, axis=-1, keepdims=True)
    mean_gz = jnp.mean(gd * z, axis=-1, keepdims=True)
    return (gd - mean_gd - z * mean_gz) * stats[1]


def ln_param_grads(dy, x, stats):
    z = (x - stats[0]) * stats[1]
    return jnp.sum(dy * z, axis=0), jnp.sum(dy, axis=0)


def silu_back(dy, v):
    gate = jax.nn.sigmoid(v)
    return dy * gate * (1.0 + v * (1.0 - gate))


def gelu_exact(v):
    return jax.nn.gelu(v, approximate=False)


def gelu_erf(v):
    return 0.5 * v * (1.0 + lax.erf(v * math.sqrt(0.5)))


def gelu_exact_slope(v):
    density = jnp.exp(-0.5 * v * v) * (1.0 / math.sqrt(2.0 * math.pi))
    return 0.5 * (1.0 + lax.erf(v * math.sqrt(0.5))) + v * density


def gelu_tanh(v):
    return jax.nn.gelu(v, approximate=True)


def gelu_tanh_slope(v):
    k = math.sqrt(2.0 / math.pi)
    t = jnp.tanh(k * (v + 0.044715 * v * v * v))
    return 0.5 * (1.0 + t) + 0.5 * v * (1.0 - t * t) * k * (1.0 + 3.0 * 0.044715 * v * v)


def frame_table():
    frame_pos = jnp.arange(FMAX, dtype=F32)[:, None]
    channel = jnp.arange(C)
    frequency = jnp.exp((channel - channel % 2).astype(F32) * (-math.log(10000.0) / C))
    angles = frame_pos * frequency[None, :]
    return jnp.where(channel[None, :] % 2 == 0, jnp.sin(angles), jnp.cos(angles))


def time_table(timesteps):
    half_width = C // 2
    frequency = jnp.exp(jnp.arange(half_width, dtype=F32) * (-math.log(10000.0) / half_width))
    angles = timesteps.astype(F32)[:, None] * frequency[None, :]
    return jnp.concatenate([jnp.cos(angles), jnp.sin(angles)], axis=1)


def through(x, w):
    return dot_f32(x, w, ((1,), (0,)))


def against(x, w):
    return dot_f32(x, w, ((1,), (1,)))


def outer(a, b):
    return dot_f32(a, b, ((0,), (0,))).astype(BF)


def windows(x, flipped):
    frames = x.shape[0]
    padded = jnp.pad(x.reshape(frames, SIDE, SIDE, C), ((0, 0), (1, 1), (1, 1), (0, 0)))
    pieces = []
    for tap in range(9):
        dy, dx = tap // 3, tap % 3
        if flipped:
            dy, dx = 2 - dy, 2 - dx
        pieces.append(padded[:, dy : dy + SIDE, dx : dx + SIDE].reshape(frames * PIX, C))
    return pieces


def conv(x, w):
    return through(jnp.concatenate(windows(x, False), axis=1), w.reshape(9 * C, C))


def conv_back(g, w):
    stacked = jnp.stack(windows(g, True), axis=1)
    return lax.dot_general(
        stacked, w, (((1, 2), (0, 2)), ((), ())), preferred_element_type=F32
    )


def update(weight, moment, average, gradient, step_rate):
    moment_new = MOMENTUM * moment + gradient
    weight_new = weight - step_rate * (gradient + MOMENTUM * moment_new)
    average_new = AVERAGE_DECAY * average + (1.0 - AVERAGE_DECAY) * weight_new
    return (moment_new, average_new, weight_new)


PAIRS = ((2, 6), (7, 8), (9, 1), (3, 4), (5, 0))
CHUNKS = 4 + len(PAIRS)
LANDED = 2


class GradientSum:
    def __init__(self, grads, landed, columns, bufs, sems, frees):
        self.grads, self.landed, self.columns = grads, landed, columns
        self.total, self.own, self.got_x, self.got_y, self.got2, self.got3, self.deal = bufs
        self.send, self.recv, self.load_sem = sems
        self.free_x, self.free_y, self.free2_x, self.free2_y, self.free3, self.free_core = frees
        c, h, core, gx, gy, partners, heads = place()
        self.c, self.h, self.core, self.gx, self.gy = c, h, core, gx, gy
        self.xp, self.yp, self.cp = partners["x"], partners["y"], partners["core"]
        self.heads = heads
        self.plane = plane_of(core, gx, gy)

    def peers(self):
        return [(self.plane[d], self.h) for d in range(1, 8)] + [
            (self.c, self.heads[j]) for j in (1, 2, 3)
        ]

    def block(self, k, y, z, core):
        if k < 4:
            ref, base = self.grads[10 + y], z * C + k * 320
        else:
            ref, base = self.grads[PAIRS[k - 4][y]], z * 320
        return ref.at[pl.ds(pl.multiple_of(base + core * 160, 16), 160)]

    def x_rows(self, x):
        return pl.ds(pl.multiple_of(x * 80, 16), 80)

    def copy(self, k, kind, src, dst, device):
        return pltpu.make_async_remote_copy(
            src_ref=src,
            dst_ref=dst,
            send_sem=self.send.at[k, kind],
            recv_sem=self.recv.at[k, kind],
            device_id=device,
            device_id_type=MESH,
        )

    def core_copies(self, k):
        return [
            self.copy(
                k,
                y * 4 + z,
                self.block(k, y, z, 1 - self.core),
                self.landed.at[k % LANDED, y, z],
                self.cp,
            )
            for y in (0, 1)
            for z in range(4)
        ]

    def landed_copy(self, k):
        slot = self.total.at[k % self.total.shape[0]]
        return pltpu.make_async_copy(self.landed.at[k % LANDED], slot, self.load_sem.at[k, 0])

    def own_copies(self, k):
        return [
            pltpu.make_async_copy(
                self.block(k, y, z, self.core),
                self.own.at[y, z],
                self.load_sem.at[k, 1 + y * 4 + z],
            )
            for y in (0, 1)
            for z in range(4)
        ]

    def first_copy(self, k):
        held = self.total.at[k % self.total.shape[0]]
        at = k // 2 % 2
        if k % 2 == 0:
            src = held.at[:, :, self.x_rows(1 - self.gx)]
            return self.copy(k, 8, src, self.got_x.at[at], self.xp)
        return self.copy(k, 8, held.at[1 - self.gy], self.got_y.at[at], self.yp)

    def second_copy(self, k):
        at = k // 2 % 2
        if k % 2 == 0:
            return self.copy(k, 9, self.got_x.at[at, 1 - self.gy], self.got2.at[k % 4], self.yp)
        src = self.got_y.at[at, :, self.x_rows(1 - self.gx)]
        return self.copy(k, 9, src, self.got2.at[k % 4], self.xp)

    def last_copies(self, k):
        return [
            self.copy(
                k,
                9 + j,
                self.got2.at[k % 4, self.heads[j]],
                self.got3.at[k % 2, j - 1],
                (self.c, self.heads[j]),
            )
            for j in (1, 2, 3)
        ]

    def deal_copies(self, k):
        at = self.columns.at[k, self.c]
        return [
            self.copy(k, 12 + d, self.deal.at[k % 2, self.plane[d]], at, (self.plane[d], self.h))
            for d in range(1, 8)
        ]

    def deal_own(self, k):
        src = self.deal.at[k % 2, self.c]
        return pltpu.make_async_copy(src, self.columns.at[k, self.c], self.load_sem.at[k, 9])

    def signal(self, sem, device):
        pl.semaphore_signal(sem, inc=1, device_id=device, device_id_type=MESH)

    def exchange(self, k):
        if k >= LANDED:
            pl.semaphore_wait(self.free_core, 1)
        for item in self.core_copies(k):
            item.start()

    def load(self, k):
        for item in self.core_copies(k):
            item.wait_recv()
        if k >= self.total.shape[0]:
            self.first_copy(k - self.total.shape[0]).wait_send()
        self.landed_copy(k).start()

    def load_own(self, k):
        for item in self.own_copies(k):
            item.start()

    def add_core(self, k):
        self.landed_copy(k).wait()
        if k + LANDED < CHUNKS:
            self.signal(self.free_core, self.cp)
        for item in self.own_copies(k):
            item.wait()
        slot = k % self.total.shape[0]
        total, own = self.total, self.own

        def body(i, carry):
            y, z = i // 4, i % 4
            total[slot, y, z] = total[slot, y, z] + own[y, z]
            return carry

        lax.fori_loop(0, 8, body, 0)
        if k >= 4:
            pl.semaphore_wait(self.free_x if k % 2 == 0 else self.free_y, 1)
        self.first_copy(k).start()

    def add_first(self, k):
        self.first_copy(k).wait_recv()
        slot, at = k % self.total.shape[0], k // 2 % 2
        total, got_x, got_y = self.total, self.got_x, self.got_y
        gy, mine = self.gy, self.x_rows(self.gx)

        def body(i, carry):
            if k % 2 == 0:
                y, z = i // 4, i % 4
                got_x[at, y, z] = got_x[at, y, z] + total[slot, y, z, mine, :]
            else:
                z = i // 2
                half = self.x_rows(i % 2)
                got_y[at, z, half, :] = got_y[at, z, half, :] + total[slot, gy, z, half, :]
            return carry

        lax.fori_loop(0, 8, body, 0)
        if k >= 4:
            pl.semaphore_wait(self.free2_y if k % 2 == 0 else self.free2_x, 1)
        self.second_copy(k).start()

    def add_second(self, k):
        self.second_copy(k).wait_recv()
        at = k // 2 % 2
        got_x, got_y, got2 = self.got_x, self.got_y, self.got2
        mine = self.x_rows(self.gx)

        def body(z, carry):
            if k % 2 == 0:
                got2[k % 4, z] = got2[k % 4, z] + got_x[at, self.gy, z]
            else:
                got2[k % 4, z] = got2[k % 4, z] + got_y[at, z, mine, :]
            return carry

        lax.fori_loop(0, 4, body, 0)
        self.second_copy(k).wait_send()
        if k + 4 < CHUNKS:
            if k % 2 == 0:
                self.signal(self.free_x, self.xp)
            else:
                self.signal(self.free_y, self.yp)
        for j, item in enumerate(self.last_copies(k)):
            if k >= 2:
                pl.semaphore_wait(self.free3.at[j], 1)
            item.start()

    def add_last(self, k):
        for item in self.last_copies(k):
            item.wait()
        got3, at = self.got3, k % 2
        rest = got3[at, 0].astype(F32) + got3[at, 1].astype(F32) + got3[at, 2].astype(F32)
        result = (self.got2[k % 4, self.h].astype(F32) + rest).astype(BF)
        if k + 4 < CHUNKS:
            if k % 2 == 0:
                self.signal(self.free2_y, self.yp)
            else:
                self.signal(self.free2_x, self.xp)
        if k + 2 < CHUNKS:
            for j in (1, 2, 3):
                self.signal(self.free3.at[j - 1], (self.c, self.heads[j]))
        if k >= 2:
            self.deal_done(k - 2)
        for d in range(8):
            self.deal[k % 2, d] = result[:, d * HD : (d + 1) * HD]
        for item in self.deal_copies(k):
            item.start()
        self.deal_own(k).start()

    def deal_done(self, k):
        for item in self.deal_copies(k):
            item.wait_send()
        self.deal_own(k).wait()

    def run(self, units, ready):
        at, sent, added = 0, 0, 0

        def flush():
            nonlocal sent
            while sent < CHUNKS and ready[sent] <= at and sent < added + LANDED:
                self.exchange(sent)
                sent += 1

        def work(most):
            nonlocal at
            for unit in units[at : at + most]:
                unit()
                at += 1
                flush()

        def until(k):
            if sent <= k:
                work(ready[k] - at)

        until(0)
        self.load(0)
        self.load_own(0)
        for step in range(CHUNKS + 4):
            if step < CHUNKS:
                self.add_core(step)
                added += 1
                flush()
                work(2)
            if 0 <= step - 2 < CHUNKS:
                self.add_first(step - 2)
                work(2)
            if step + 1 < CHUNKS:
                until(step + 1)
                self.load(step + 1)
                self.load_own(step + 1)
            if 0 <= step - 3 < CHUNKS:
                self.add_second(step - 3)
                work(2)
            if 0 <= step - 4 < CHUNKS:
                self.add_last(step - 4)
                work(2)
        work(len(units))
        for k in range(CHUNKS):
            for item in self.core_copies(k):
                item.wait_send()
            if k >= CHUNKS - self.total.shape[0]:
                self.first_copy(k).wait_send()
            for item in self.deal_copies(k):
                item.wait_recv()
        for k in (CHUNKS - 2, CHUNKS - 1):
            self.deal_done(k)


SMALL_ROWS = 24


class SmallSum:
    def __init__(self, total, small, out, land, room, send, recv, sem):
        self.t, self.small, self.out, self.land, self.room = total, small, out, land, room
        self.send, self.recv, self.sem = send, recv, sem

    def rows(self, i):
        return pl.ds(pl.multiple_of(i * SMALL_ROWS, 8), SMALL_ROWS)

    def copy(self, i, src, dst, device):
        return pltpu.make_async_remote_copy(
            src_ref=src,
            dst_ref=dst,
            send_sem=self.send.at[i],
            recv_sem=self.recv.at[i],
            device_id=device,
            device_id_type=MESH,
        )

    def plane_copies(self):
        t = self.t
        at = self.land.at[self.rows(t.c)]
        return [self.copy(d, self.small, at, (t.plane[d], t.h)) for d in range(1, 8)]

    def head_copies(self):
        t = self.t
        return [
            self.copy(7 + j, self.out, self.land.at[self.rows(7 + j)], (t.c, t.heads[j]))
            for j in (1, 2, 3)
        ]

    def gather(self, places):
        copies = [
            pltpu.make_async_copy(
                self.land.at[self.rows(p)], self.room.at[self.rows(i)], self.sem.at[i]
            )
            for i, p in enumerate(places)
        ]
        for item in copies:
            item.start()
        for item in copies:
            item.wait()
        for i in range(len(places)):
            self.out[...] += self.room[self.rows(i), :]

    def first(self):
        for item in self.plane_copies():
            item.start()

    def second(self):
        for item in self.plane_copies():
            item.wait()
        self.out[...] = self.small[...]
        self.gather([self.t.plane[d] for d in range(1, 8)])
        for item in self.head_copies():
            item.start()

    def last(self):
        for item in self.head_copies():
            item.wait()
        self.gather([8, 9, 10])


def column_sum(x, rows=PIX):
    total = jnp.sum(x[0:rows, :].astype(F32), axis=0, keepdims=True)
    for f in range(1, x.shape[0] // rows):
        total += jnp.sum(x[f * rows : (f + 1) * rows, :].astype(F32), axis=0, keepdims=True)
    return total


def norm_back_rows(dy, x, q, gain, out, vec=None):
    def body(f, carry):
        rows = frame_rows(f)
        v = x[rows, :]
        v = v - jnp.mean(v, axis=1, keepdims=True)
        scale = lax.rsqrt(jnp.mean(v * v, axis=1, keepdims=True) + LAYER_EPS)
        z = v * scale
        g = dy[rows, :]
        if vec is not None:
            vec[gain : gain + 1] += jnp.sum(g * z, axis=0, keepdims=True)
            vec[gain + 1 : gain + 2] += jnp.sum(g, axis=0, keepdims=True)
        gd = g * q[gain : gain + 1]
        m1 = jnp.mean(gd, axis=1, keepdims=True)
        m2 = jnp.mean(gd * z, axis=1, keepdims=True)
        out[rows, :] = out[rows, :] + (gd - m1 - z * m2) * scale
        return carry

    lax.fori_loop(0, x.shape[0] // PIX, body, 0)


def group_back(dy, x, q, gain, with_silu, fold, stat, sums, sink, vec=None):
    group_stats(x, fold, stat)
    frames = x.shape[0] // PIX
    sums[0] = jnp.zeros_like(sums[0])
    sums[1] = jnp.zeros_like(sums[1])

    def normal(f):
        block = x[f * PIX : (f + 1) * PIX, :].astype(F32)
        return (block - stat[0, f : f + 1]) * stat[1, f : f + 1]

    for f in range(frames):
        rows = slice(f * PIX, (f + 1) * PIX)
        z = normal(f)
        g = dy[rows, :]
        if with_silu:
            v = z * q[gain : gain + 1] + q[gain + 1 : gain + 2]
            gate = 1.0 / (1.0 + jnp.exp(-v))
            g = g * gate * (1.0 + v * (1.0 - gate))
        if vec is not None:
            vec[gain : gain + 1] += jnp.sum(g * z, axis=0, keepdims=True)
            vec[gain + 1 : gain + 2] += jnp.sum(g, axis=0, keepdims=True)
        gd = g * q[gain : gain + 1]
        dy[rows, :] = gd
        sums[0, f : f + 1] = jnp.sum(gd, axis=0, keepdims=True)
        sums[1, f : f + 1] = jnp.sum(gd * z, axis=0, keepdims=True)
    sums[0] = group_spread(sums[0], fold)
    sums[1] = group_spread(sums[1], fold)
    for f in range(frames):
        rows = slice(f * PIX, (f + 1) * PIX)
        dx = dy[rows, :] - sums[0, f : f + 1] - normal(f) * sums[1, f : f + 1]
        sink(rows, dx * stat[1, f : f + 1])


def backward_kernel(n_weights, *refs):
    weights, refs = refs[:n_weights], refs[n_weights:]
    conv1, conv2, in_w, qkv_w, self_o, cross_w, cross_o, value_w, gate_w, down_w, out_w = weights[:11]
    square_w, wide_w = weights[11:]
    hid1, first, state0, state1, state2, second, lat, value_in, gate_in = refs[:9]
    self_q, self_k, self_v, cross_q, text_k, text_v = refs[9:15]
    normed, entered, block1, block2, t1, t2, t3, att1, att2, inner, stream_in = refs[15:26]
    qkv1, qkv2, g_pixels, g_frames = refs[26:29], refs[29:32], refs[32], refs[33]
    q, vf, fold, tbias, alive = refs[34:39]
    columns, grad_in, output, small_out = refs[39:43]
    landed, hop_land, small_land, g_second = refs[43:47]
    grads, refs = refs[47:59], refs[59:]
    (
        total, own, got_x, got_y, got2, got3, deal,
        send, recv, load_sem, free_x, free_y, free2_x, free2_y, free3, free_core,
        hop_send, hop_recv, small_send, small_recv, small_sem,
        col_sem, row_sem, pair_sem, in_sem, out_sem,
        win, col_buf, row_buf, pair, gs, acc, tmp, xb, low, stat, sums, vec,
    ) = refs
    comm = GradientSum(
        grads,
        landed,
        columns,
        (total, own, got_x, got_y, got2, got3, deal),
        (send, recv, load_sem),
        (free_x, free_y, free2_x, free2_y, free3, free_core),
    )
    tiny = SmallSum(comm, vec, small_out, small_land, tmp, small_send, small_recv, small_sem)
    greet(comm.peers())
    frames = gs.shape[0] // PIX
    share = gs.shape[0] // 4

    def bring(pairs):
        copies = [
            pltpu.make_async_copy(src, dst, in_sem.at[i]) for i, (src, dst) in enumerate(pairs)
        ]
        for item in copies:
            item.start()
        for item in copies:
            item.wait()

    def hop_rows(z):
        return pl.ds(pl.multiple_of(z * share, 16), share)

    def hop_copies(i):
        return [
            pltpu.make_async_remote_copy(
                src_ref=win.at[2, hop_rows(comm.heads[j])],
                dst_ref=hop_land.at[i, comm.h],
                send_sem=hop_send.at[i, j],
                recv_sem=hop_recv.at[i, j],
                device_id=(comm.c, comm.heads[j]),
                device_id_type=MESH,
            )
            for j in (1, 2, 3)
        ]

    def hop_own(i):
        src = win.at[2, hop_rows(comm.h)]
        return pltpu.make_async_copy(src, hop_land.at[i, comm.h], hop_send.at[i, 0])

    def hop_start(i):
        for item in hop_copies(i):
            item.start()
        hop_own(i).start()

    def hop_end(i, sink):
        for item in hop_copies(i):
            item.wait()
        hop_own(i).wait()
        bring([(hop_land.at[i, z], win.at[2, pl.ds(z * share, share)]) for z in range(4)])
        per = share // frames
        for f in range(frames):
            parts = [win[2, pl.ds(z * share + f * per, per), :] for z in range(4)]
            sink(f, slice(f * PIX, (f + 1) * PIX), jnp.concatenate(parts, axis=0).astype(F32))

    def stage_copy(i, slot, g):
        src = win.at[7 + slot, pl.ds(0, TILE)]
        return pltpu.make_async_copy(src, g.at[tile_at(i)], out_sem.at[slot])

    def outer_unit(a, b, g):
        count = g.shape[0] // TILE

        def body(i, carry):
            slot = i % 2

            @pl.when(i >= 2)
            def _():
                stage_copy(i - 2, slot, g).wait()

            tile = dot_f32(a[:, tile_at(i)], b[...], ((0,), (0,)))
            win[7 + slot, pl.ds(0, TILE), :] = tile.astype(BF)
            stage_copy(i, slot, g).start()
            return carry

        lax.fori_loop(0, count, body, 0)
        for i in (count - 2, count - 1):
            stage_copy(i, i % 2, g).wait()

    def leave_unit():
        vec[...] = jnp.zeros_like(vec)
        bring([(stream_in, win.at[0]), (g_pixels, win.at[1]), (t3, win.at[3])])

        def sink(lanes, tile):
            win[2, :, lanes] = tile.astype(BF)

        through_tiles(win.at[0], square_w.at[AT[2]], col_buf, col_sem, sink)
        hop_start(0)
        vec[12:13] = column_sum(win.at[1])

    def stream_unit():
        against_unit(win.at[1], square_w.at[AT[2]], gs)
        low[...] = gs[...].astype(BF)
        vec[11:12] = column_sum(low)
        acc[...] = jnp.zeros_like(acc)

    def wide_copy(i, slot, j):
        src = win.at[5 + 2 * slot + j, pl.ds(0, TILE)]
        return pltpu.make_async_copy(src, grads[10 + j].at[tile_at(i)], out_sem.at[2 * slot + j])

    def wide_unit(part, parts):
        count = wide_w.shape[1] // TILE
        per = count // parts
        start = part * per

        def tiles(i, slot):
            rows = tile_at(start + i)
            return [
                (wide_w.at[0, rows], row_buf.at[slot * 3]),
                (wide_w.at[1, rows], row_buf.at[slot * 3 + 1]),
                (inner.at[:, rows], pair.at[slot, 0]),
            ]

        def body(i, slot):
            tile = start + i
            to = tile % 2
            g = dot_f32(low[...], row_buf[slot * 3 + 1], ((1,), (1,)))
            inner_tile = pair[slot, 0].astype(F32)
            g = gelu_tanh_slope(inner_tile) * g
            g_low = g.astype(BF)
            rows = pl.ds(13 + tile // 5, 1)
            vec[rows, tile_at(tile % 5)] = jnp.sum(g_low.astype(F32), axis=0, keepdims=True)
            acc[...] += dot_f32(g_low, row_buf[slot * 3], ((1,), (0,)))

            @pl.when(tile >= 2)
            def _():
                wide_copy(tile - 2, to, 0).wait()
                wide_copy(tile - 2, to, 1).wait()

            up = dot_f32(g_low, win[3], ((0,), (0,)))
            win[5 + 2 * to, pl.ds(0, TILE), :] = up.astype(BF)
            wide_copy(tile, to, 0).start()
            down = dot_f32(gelu_tanh(inner_tile).astype(BF), low[...], ((0,), (0,)))
            win[6 + 2 * to, pl.ds(0, TILE), :] = down.astype(BF)
            wide_copy(tile, to, 1).start()

        stream(per, tiles, body, pair_sem, 2)
        if part == parts - 1:
            for tile in (count - 2, count - 1):
                wide_copy(tile, tile % 2, 0).wait()
                wide_copy(tile, tile % 2, 1).wait()

    def output_unit():
        bring([(second, tmp)])

        def sink(f, rows, moved):
            result = alive[f : f + 1, 0:1] * (tmp[rows, :] + moved + vf[12:13])
            win[4, rows, :] = result.astype(BF)

        hop_end(0, sink)
        bring([(win.at[4], output)])

    def motion_norm_unit(state, gain, bias):
        bring([(state, xb)])
        norm_back_rows(acc, xb, vf, gain, gs, vec)
        low[...] = gs[...].astype(BF)
        vec[bias : bias + 1] = column_sum(low)

    def motion_out_unit(att, wo):
        bring([(att, win.at[0])])
        outer_unit(win.at[0], low, grads[wo])
        against_unit(low, square_w.at[AT[wo]], win.at[6])

    def motion_attend_unit(qkv, t):
        bring([(qkv[0], win.at[0]), (qkv[1], win.at[1]), (qkv[2], win.at[2])])
        attend_back_body(
            True,
            win.at[0],
            win.at[1],
            win.at[2],
            tbias,
            win.at[6],
            win.at[3],
            win.at[4],
            win.at[5],
            tmp,
            acc,
            xb,
        )
        bring([(t, win.at[0])])

    def entry_unit():
        bring([(normed, win.at[0])])
        outer_unit(win.at[0], low, grads[0])

    def entry_back_unit():
        against_unit(low, square_w.at[AT[0]], win.at[2])
        hop_start(1)

    def second_unit():
        def sink(f, rows, moved):
            acc[rows, :] = moved

        hop_end(1, sink)
        bring([(second, xb), (g_frames, low)])

        def put(rows, dx):
            gs[rows, :] = low[rows, :].astype(F32) + dx

        group_back(acc, xb, vf, 0, False, fold, stat, sums, put, vec)
        low[...] = gs[...].astype(BF)
        bring([(gs, g_second)])
        tiny.first()

    def against_unit(x, w, out):
        def sink(lanes, tile):
            out[:, lanes] = tile.astype(out.dtype)

        against_tiles(x, w, row_buf, row_sem, sink)

    def start_unit():
        against_unit(low, out_w.at[0], gs)
        low[...] = gs[...].astype(BF)
        acc[...] = jnp.zeros_like(acc)

    def ffn_unit(part, parts):
        per = value_w.shape[1] // TILE // parts
        start = part * per

        def tiles(i, slot):
            rows = tile_at(start + i)
            return [
                (value_w.at[0, rows], row_buf.at[slot * 3]),
                (gate_w.at[0, rows], row_buf.at[slot * 3 + 1]),
                (down_w.at[0, rows], row_buf.at[slot * 3 + 2]),
                (value_in.at[:, rows], pair.at[slot, 0]),
                (gate_in.at[:, rows], pair.at[slot, 1]),
            ]

        def body(i, slot):
            g = dot_f32(low[...], row_buf[slot * 3 + 2], ((1,), (1,)))
            value, gate = pair[slot, 0].astype(F32), pair[slot, 1].astype(F32)
            phi = 0.5 * (1.0 + lax.erf(gate * math.sqrt(0.5)))
            density = jnp.exp(-0.5 * gate * gate) * (1.0 / math.sqrt(2.0 * math.pi))
            g_value = (gate * phi * g).astype(BF)
            g_gate = (value * (phi + gate * density) * g).astype(BF)
            acc[...] += dot_f32(g_value, row_buf[slot * 3], ((1,), (0,)))
            acc[...] += dot_f32(g_gate, row_buf[slot * 3 + 1], ((1,), (0,)))

        stream(per, tiles, body, pair_sem, 2)

    def norm_unit(state, gain):
        bring([(state, xb)])
        norm_back_rows(acc, xb, q, gain, gs)
        low[...] = gs[...].astype(BF)

    def cross_unit():
        rows = text_k.shape[0]
        keys, values = win.at[1, pl.ds(0, rows)], win.at[2, pl.ds(0, rows)]
        bring([(cross_q, win.at[0]), (text_k, keys), (text_v, values)])
        attend_back_body(False, win.at[0], keys, values, text_mask, win.at[6], win.at[3], tmp)

    def self_unit():
        bring([(self_q, win.at[0]), (self_k, win.at[1]), (self_v, win.at[2])])
        attend_back_body(
            True,
            win.at[0],
            win.at[1],
            win.at[2],
            spatial_mask,
            win.at[6],
            win.at[3],
            win.at[4],
            win.at[5],
            tmp,
            acc,
            xb,
        )

    def through_unit(x, w, fresh):
        def sink(lanes, tile):
            if fresh:
                acc[:, lanes] = tile
            else:
                acc[:, lanes] += tile

        through_tiles(x, w, col_buf, col_sem, sink)

    def first_unit():
        bring([(first, xb), (g_second, gs)])

        def sink(rows, dx):
            gs[rows, :] = gs[rows, :] + dx

        group_back(acc, xb, q, 7, False, fold, stat, sums, sink)

    def hid_unit():
        bring([(hid1, xb)])

        def sink(rows, dx):
            tmp[rows, :] = dx

        group_back(acc, xb, q, 4, True, fold, stat, sums, sink)

    def last_unit():
        bring([(lat, low)])

        def sink(rows, dx):
            low[rows, :] = (gs[rows, :] + dx).astype(BF)

        group_back(acc, low, q, 0, True, fold, stat, sums, sink)
        bring([(low, grad_in)])

    def windows_unit(x):
        make_windows(x, win, True)

    def conv_unit(w, tap):
        def sink(lanes, tile):
            if tap == 0:
                acc[:, lanes] = tile
            else:
                acc[:, lanes] += tile

        against_tiles(win.at[tap], w.at[tap], row_buf, row_sem, sink)

    P_ = functools.partial
    def nothing():
        pass

    ready = [0] * CHUNKS
    units = [leave_unit, P_(outer_unit, win.at[0], win.at[1], grads[2]), stream_unit]
    units += [P_(wide_unit, i, 10) for i in range(10)]
    ready[0:4] = [len(units)] * 4
    units += [output_unit, P_(motion_norm_unit, block2, 9, 8)]
    done = {2: 0}
    for state, t, qkv, att, wo, wq, gain, bias in (
        (block1, t2, qkv2, att2, 6, 7, 6, 5),
        (entered, t1, qkv1, att1, 1, 3, 3, 2),
    ):
        units += [P_(motion_out_unit, att, wo)]
        done[wo] = len(units)
        units += [P_(motion_attend_unit, qkv, t)]
        for i in range(3):
            units += [P_(outer_unit, win.at[3 + i], win.at[0], grads[wq + i])]
            done[wq + i] = len(units)
        units += [P_(through_unit, win.at[3 + i], square_w.at[AT[wq + i]], i == 0) for i in range(3)]
        units += [P_(motion_norm_unit, state, gain, bias)]
    units += [entry_unit]
    done[0] = len(units)
    for k, (one, other) in enumerate(PAIRS):
        ready[4 + k] = max(done[one], done[other])
    units += [entry_back_unit, nothing, nothing, nothing, nothing, second_unit]
    units += [start_unit] + [P_(ffn_unit, i, 10) for i in range(10)]
    units += [tiny.second, P_(norm_unit, state2, 16)]
    units += [P_(against_unit, low, cross_o.at[0], win.at[6]), cross_unit]
    units += [P_(through_unit, win.at[3], cross_w.at[0], True), P_(norm_unit, state1, 13)]
    units += [tiny.last, P_(against_unit, low, self_o.at[0], win.at[6]), self_unit]
    units += [P_(through_unit, win.at[3 + i], qkv_w.at[i], i == 0) for i in range(3)]
    units += [P_(norm_unit, state0, 10), P_(against_unit, low, in_w.at[0], acc), first_unit]
    units += [P_(windows_unit, gs)] + [P_(conv_unit, conv2, t) for t in range(9)]
    units += [hid_unit, P_(windows_unit, tmp)] + [P_(conv_unit, conv1, t) for t in range(9)]
    units += [last_unit]
    comm.run(units, ready)


def backward_fused(frozen, trained, saved, motion, lat, g_pixels, g_frames, q, vf, tbias, alive):
    tokens = lat.shape[0]
    weights = [frozen[i] for i in (1, 2, 3, 4, 5, 6, 8, 9, 10, 11, 12)] + list(trained)
    kept = list(saved[:6]) + [lat, saved[12], saved[13]] + list(saved[6:12])
    kept += list(motion) + [g_pixels, g_frames]
    fold = group_matrix()
    any_spec, vmem = pl.BlockSpec(memory_space=pl.ANY), pl.BlockSpec(memory_space=pltpu.VMEM)
    dma, count = pltpu.SemaphoreType.DMA, pltpu.SemaphoreType.REGULAR

    def array(shape, dtype=BF):
        return jax.ShapeDtypeStruct(shape, dtype)

    outs = pl.pallas_call(
        functools.partial(backward_kernel, len(weights)),
        out_shape=(
            array((CHUNKS, 8, 80, HD)),
            array((tokens, C)),
            array((tokens, C)),
            array((SMALL_ROWS, C), F32),
            array((LANDED, 2, 4, 160, C)),
            array((2, 4, tokens // 4, C)),
            array((11 * SMALL_ROWS, C), F32),
            array((tokens, C), F32),
        )
        + (array((C, C)),) * 10
        + (array((4 * C, C)),) * 2,
        in_specs=[any_spec] * (len(weights) + len(kept)) + [vmem] * 5,
        out_specs=(any_spec,) * 3 + (vmem,) + (any_spec,) * 16,
        scratch_shapes=[
            pltpu.VMEM((3, 2, 4, 160, C), BF),
            pltpu.VMEM((2, 4, 160, C), BF),
            pltpu.VMEM((2, 2, 4, 80, C), BF),
            pltpu.VMEM((2, 4, 160, C), BF),
            pltpu.VMEM((4, 4, 80, C), BF),
            pltpu.VMEM((2, 3, 80, C), BF),
            pltpu.VMEM((2, 8, 80, HD), BF),
            dma((CHUNKS, 20)),
            dma((CHUNKS, 20)),
            dma((CHUNKS, 10)),
            count,
            count,
            count,
            count,
            count((3,)),
            count,
            dma((2, 4)),
            dma((2, 4)),
            dma((11,)),
            dma((11,)),
            dma((7,)),
            dma((2, 1)),
            dma((6, 1)),
            dma((2, 5)),
            dma((4,)),
            dma((4,)),
            pltpu.VMEM((9, tokens, C), BF),
            pltpu.VMEM((2, C, TILE), BF),
            pltpu.VMEM((6, TILE, C), BF),
            pltpu.VMEM((2, 2, tokens, TILE), BF),
            pltpu.VMEM((tokens, C), F32),
            pltpu.VMEM((tokens, C), F32),
            pltpu.VMEM((tokens, C), F32),
            pltpu.VMEM((tokens, C), F32),
            pltpu.VMEM((tokens, C), BF),
            pltpu.VMEM((2, 8, C), F32),
            pltpu.VMEM((2, 8, C), F32),
            pltpu.VMEM((SMALL_ROWS, C), F32),
        ],
        compiler_params=pltpu.CompilerParams(
            collective_id=3, has_side_effects=True, vmem_limit_bytes=62 << 20
        ),
    )(*weights, *kept, jnp.pad(q, ((0, 4), (0, 0))), vf, fold, tbias, alive)
    columns, grad_in, output, small = outs[:4]
    square = columns[4:].reshape(len(PAIRS), 2, 2, 2, 80, HD).transpose(0, 1, 3, 2, 4, 5)
    square = square.reshape(10, 320, HD)
    at = [pair.index(i) + 2 * k for i in range(10) for k, pair in enumerate(PAIRS) if i in pair]
    square = jnp.stack([square[i] for i in at]).astype(F32)
    wide = columns[:4].reshape(4, 2, 2, 2, 80, HD).transpose(1, 0, 3, 2, 4, 5)
    return output, grad_in, square, wide.reshape(2, C, HD).astype(F32), small


def forward_plain(frozen, x0, Q, time_in, text, geglu_bias, spatial_bias, cross_bias):
    time_w, conv1_w, conv2_w, in_w, self_w, self_o, cross_qw, cross_w, cross_o = frozen[:9]
    ffn_value, ffn_gate, ffn_down, out_w = frozen[9:]
    geglu_f = lax.all_gather(geglu_bias, "head", axis=1, tiled=True)

    def flat(x):
        return x.reshape(-1, C)

    act1 = silu(gn(x0, gn_stats(x0), Q[0], Q[1])).astype(BF)
    hid1 = (conv(act1, conv1_w) + through(time_in, time_w[0]) + Q[2] + Q[3]).reshape(x0.shape)
    act2 = silu(gn(hid1, gn_stats(hid1), Q[4], Q[5])).astype(BF)
    first = x0 + conv(act2, conv2_w).reshape(x0.shape) + Q[6]
    spatial_in = flat(gn(first, gn_stats(first), Q[7], Q[8]).astype(BF))
    state0 = through(spatial_in, in_w[0]) + Q[9]
    norm1 = ln(state0, ln_stats(state0), Q[10], Q[11]).astype(BF)
    self_q, self_k, self_v = (against(norm1, self_w[i]).astype(BF) for i in range(3))
    self_att = attend(self_q, self_k, self_v, spatial_bias)
    state1 = state0 + through(self_att, self_o[0]) + Q[12]
    norm2 = ln(state1, ln_stats(state1), Q[13], Q[14]).astype(BF)
    cross_q = against(norm2, cross_qw[0]).astype(BF)
    text_k, text_v = (against(text, cross_w[i]).astype(BF) for i in (0, 1))
    cross_att = attend(cross_q, text_k, text_v, cross_bias)
    state2 = state1 + through(cross_att, cross_o[0]) + Q[15]
    norm3 = ln(state2, ln_stats(state2), Q[16], Q[17]).astype(BF)
    value_in = (against(norm3, ffn_value[0]) + geglu_f[0]).astype(BF)
    gate_in = (against(norm3, ffn_gate[0]) + geglu_f[1]).astype(BF)
    mixed = (value_in.astype(F32) * gelu_erf(gate_in.astype(F32))).astype(BF)
    state3 = (state2 + through(mixed, ffn_down[0]) + Q[18]).astype(BF)
    second = flat(first) + through(state3, out_w[0]) + Q[19]
    states = (flat(hid1), flat(first), state0, state1, state2, second)
    return states + (self_q, self_k, self_v, cross_q, text_k, text_v, value_in, gate_in)


def motion_plain(trained, second, vector_f, bias_f, codes, temporal_bias, to_pixels):
    square_w, ffn_w = trained
    normed = to_pixels(gn(second, gn_stats(second), vector_f[0], vector_f[1]).astype(BF))
    entered = through(normed, square_w[0]) + vector_f[2]

    def temporal_in(x, gain_row, wq):
        t = ln(x, ln_stats(x), vector_f[gain_row], vector_f[gain_row + 1]) + codes
        t = t.astype(BF)
        return t, [against(t, square_w[wq + i]).astype(BF) for i in range(3)]

    t1, qkv1 = temporal_in(entered, 3, 3)
    att1 = attend(*qkv1, temporal_bias)
    block1 = entered + through(att1, square_w[1]) + vector_f[5]
    t2, qkv2 = temporal_in(block1, 6, 7)
    att2 = attend(*qkv2, temporal_bias)
    block2 = block1 + through(att2, square_w[6]) + vector_f[8]
    t3 = ln(block2, ln_stats(block2), vector_f[9], vector_f[10]).astype(BF)
    inner = against(t3, ffn_w[0]) + bias_f
    spread = gelu_tanh(inner).astype(BF)
    stream = (block2 + through(spread, ffn_w[1]) + vector_f[11]).astype(BF)
    motion = (normed, entered, block1, block2, t1, t2, t3, att1, att2, inner.astype(BF), stream)
    return motion + tuple(qkv1) + tuple(qkv2)


def motion_back_plain(
    trained, motion, g_out, grad_out, second, vector_f, temporal_bias, to_frames
):
    square_w, ffn_w = trained
    normed, entered, block1, block2, t1, t2, t3, att1, att2, inner, stream = motion[:11]
    qkv1, qkv2 = motion[11:14], motion[14:17]
    spread = gelu_tanh(inner.astype(F32)).astype(BF)
    tl1, tl2, tl3 = ln_stats(entered), ln_stats(block1), ln_stats(block2)
    stats3 = gn_stats(second)
    col = lambda v: jnp.sum(v.astype(F32), axis=0)
    G = {}
    G[2] = outer(stream, g_out)
    grad_stream = against(g_out, square_w[2])
    g_ffn = grad_stream.astype(BF)
    grad_down = outer(spread, g_ffn)
    g_inner = (gelu_tanh_slope(inner.astype(F32)) * against(g_ffn, ffn_w[1])).astype(BF)
    grad_up = outer(g_inner, t3)
    grad_t3 = through(g_inner, ffn_w[0])
    grad_b2 = grad_stream + ln_back(grad_t3, block2, tl3, vector_f[9])
    dgain3, dshift3 = ln_param_grads(grad_t3, block2, tl3)

    def temporal_back(grad, x, stats, t, qkv, att, gain_row, wo, wq):
        low = grad.astype(BF)
        G[wo] = outer(att, low)
        dqkv = attend_back(*qkv, temporal_bias, against(low, square_w[wo]).astype(BF))
        for i in range(3):
            G[wq + i] = outer(dqkv[i], t)
        grad_t = sum(through(dqkv[i], square_w[wq + i]) for i in range(3))
        grad_x = grad + ln_back(grad_t, x, stats, vector_f[gain_row])
        return grad_x, ln_param_grads(grad_t, x, stats), col(low)

    grad_b1, (dgain2, dshift2), dbias2 = temporal_back(
        grad_b2, block1, tl2, t2, qkv2, att2, 6, 6, 7
    )
    grad_e, (dgain1, dshift1), dbias1 = temporal_back(
        grad_b1, entered, tl1, t1, qkv1, att1, 3, 1, 3
    )
    g_entry = grad_e.astype(BF)
    G[0] = outer(normed, g_entry)
    grad_normed = to_frames(against(g_entry, square_w[0]).astype(BF)).astype(F32).reshape(second.shape)
    z = (second - stats3[0]) * stats3[1]
    dgain0 = jnp.sum(grad_normed * z, axis=(0, 1))
    dshift0 = jnp.sum(grad_normed, axis=(0, 1))
    grad_second = grad_out + gn_back(grad_normed, second, stats3, vector_f[0])

    grad_vector = jnp.stack(
        [
            dgain0,
            dshift0,
            col(g_entry),
            dgain1,
            dshift1,
            dbias1,
            dgain2,
            dshift2,
            dbias2,
            dgain3,
            dshift3,
            col(g_ffn),
            col(g_out),
        ]
    )
    fill = jnp.zeros((SMALL_ROWS - 17, C), F32)
    small = jnp.concatenate([grad_vector, col(g_inner).reshape(4, C), fill])
    return [G[i] for i in range(10)], [grad_up, grad_down], small, grad_second


def backward_plain(frozen, saved, x0, Q, grad_second, spatial_bias, cross_bias):
    time_w, conv1_w, conv2_w, in_w, self_w, self_o, cross_qw, cross_w, cross_o = frozen[:9]
    ffn_value, ffn_gate, ffn_down, out_w = frozen[9:]
    hid1, first, state0, state1, state2 = saved[:5]
    self_q, self_k, self_v, cross_q, text_k, text_v, value_in, gate_in = saved[6:]
    hid1, first = hid1.reshape(x0.shape), first.reshape(x0.shape)
    value_in, gate_in = value_in.astype(F32), gate_in.astype(F32)

    def flat(x):
        return x.reshape(-1, C)

    def framed(x):
        return x.reshape(x0.shape)

    stats0, stats1, stats2 = gn_stats(x0), gn_stats(hid1), gn_stats(first)
    sl1, sl2, sl3 = ln_stats(state0), ln_stats(state1), ln_stats(state2)
    g_po = flat(grad_second).astype(BF)
    grad_s3 = against(g_po, out_w[0])
    g_fb = grad_s3.astype(BF)
    grad_mixed = against(g_fb, ffn_down[0])
    g_value = (gelu_exact(gate_in) * grad_mixed).astype(BF)
    g_gate = (value_in * gelu_exact_slope(gate_in) * grad_mixed).astype(BF)
    grad_n3 = through(g_value, ffn_value[0]) + through(g_gate, ffn_gate[0])
    grad_s2 = grad_s3 + ln_back(grad_n3, state2, sl3, Q[16])
    g_cb = grad_s2.astype(BF)
    (g_cq,) = attend_back(
        cross_q, text_k, text_v, cross_bias, against(g_cb, cross_o[0]).astype(BF), False
    )
    grad_s1 = grad_s2 + ln_back(through(g_cq, cross_qw[0]), state1, sl2, Q[13])
    g_sb = grad_s1.astype(BF)
    dself = attend_back(
        self_q, self_k, self_v, spatial_bias, against(g_sb, self_o[0]).astype(BF)
    )
    grad_n1 = sum(through(dself[i], self_w[i]) for i in range(3))
    grad_s0 = grad_s1 + ln_back(grad_n1, state0, sl1, Q[10])
    g_pi = grad_s0.astype(BF)
    grad_gn = framed(against(g_pi, in_w[0]))
    grad_first = grad_second + gn_back(grad_gn, first, stats2, Q[7])

    grad_act2 = framed(conv_back(grad_first.astype(BF), conv2_w))
    grad_n = silu_back(grad_act2, gn(hid1, stats1, Q[4], Q[5]))
    grad_hid1 = gn_back(grad_n, hid1, stats1, Q[4])
    grad_act1 = framed(conv_back(grad_hid1.astype(BF), conv1_w))
    grad_n = silu_back(grad_act1, gn(x0, stats0, Q[0], Q[1]))
    return (grad_first + gn_back(grad_n, x0, stats0, Q[0])).astype(BF)


def per_device(
    sizes,
    latents,
    cotangent,
    frames,
    timesteps,
    text,
    conv_weight,
    time_weight,
    frozen_params,
    spatial_square,
    cross_kv,
    spatial_ffn,
    geglu_bias,
    projections,
    feedforward,
    up_bias,
    vectors,
    projections_moment,
    feedforward_moment,
    up_bias_moment,
    vectors_moment,
    projections_average,
    feedforward_average,
    up_bias_average,
    vectors_average,
):
    Q = frozen_params
    n_head = sizes[1]
    head_index = lax.axis_index("head")
    clip_index = lax.axis_index("clip")
    own_frames = latents.shape[1]
    tokens = own_frames * PIX
    own_pixels = PIX // n_head
    columns = FMAX * own_pixels

    def framed(x):
        return x.reshape(own_frames, PIX, C)

    def flat(x):
        return x.reshape(tokens, C)

    def to_pixels(x):
        x = lax.all_to_all(framed(x), "head", 1, 0, tiled=True)
        return x.reshape(columns, C)

    def to_frames(x):
        x = lax.all_to_all(x.reshape(FMAX, own_pixels, C), "head", 0, 1, tiled=True)
        return x.reshape(tokens, C)

    frame_of = jnp.arange(tokens) // PIX
    spatial_bias = jnp.where(frame_of[:, None] == frame_of[None, :], 0.0, MASK_FILL).astype(F32)
    column = jnp.arange(columns)
    same_pixel = (column % own_pixels)[:, None] == (column % own_pixels)[None, :]
    key_there = (column // own_pixels)[None, :] < frames[0]
    temporal_bias = jnp.where(same_pixel & key_there, 0.0, MASK_FILL).astype(F32)
    text_len = text.shape[1]
    text_rows = 128
    cross_bias = jnp.broadcast_to(
        jnp.where(jnp.arange(text_rows)[None, :] < text_len, 0.0, MASK_FILL), (tokens, text_rows)
    ).astype(F32)
    own_frame = head_index * own_frames + jnp.arange(own_frames)
    frame_mask = (own_frame < frames[0]).astype(F32)[:, None, None]

    x0 = latents[0].astype(F32)
    grad_out = frame_mask * cotangent[0].astype(F32)
    arrays = frozen_arrays(conv_weight, time_weight, spatial_square, cross_kv, spatial_ffn)
    time_in = jax.nn.silu(time_table(timesteps)).astype(BF)
    text_pad = jnp.pad(text[0], ((0, text_rows - text_len), (0, 0)))
    if sizes == (8, 4):
        lat = latents.reshape(tokens, C)
        g_frames = flat(grad_out.astype(BF))
        frozen, trained, saved, motion, g_out, vector_f = forward_fused(
            arrays,
            projections,
            feedforward,
            vectors,
            up_bias,
            lat,
            g_frames,
            Q,
            time_in,
            text_pad,
            geglu_bias,
            temporal_bias,
        )
        alive = jnp.pad(frame_mask[:, :, 0], ((0, 8 - own_frames), (0, 127)))
        output, input_gradient, own_square, own_wide, small = backward_fused(
            frozen, trained, saved, motion, lat, g_out, g_frames, Q, vector_f, temporal_bias, alive
        )
        output, input_gradient = framed(output)[None], framed(input_gradient)[None]
    else:
        small = pack_small(vectors, up_bias)
        frozen, trained, small = gather_plain(arrays, small, projections, feedforward)
        vector_f, bias_f = unpack_small(sizes, small, vectors, up_bias)
        saved = forward_plain(
            frozen, x0, Q, time_in, text_pad, geglu_bias, spatial_bias, cross_bias
        )
        second = framed(saved[5])
        codes = jnp.repeat(frame_table(), own_pixels, axis=0)
        motion = motion_plain(
            trained, second, vector_f, bias_f, codes, temporal_bias, to_pixels
        )
        g_out = to_pixels(grad_out.astype(BF))
        moved = to_frames(through(motion[10], trained[0][2]).astype(BF)).astype(F32)
        output = (frame_mask * (second + framed(moved) + vector_f[12])).astype(BF)[None]
        parts, wide_parts, small, grad_second = motion_back_plain(
            trained, motion, g_out, grad_out, second, vector_f, temporal_bias, to_frames
        )
        own_square, own_wide, small = sum_plain(parts, wide_parts, small)
        input_gradient = backward_plain(
            frozen, saved, x0, Q, grad_second, spatial_bias, cross_bias
        )[None]
    k = vectors.shape[1]
    own_vector = lax.dynamic_slice_in_dim(small[:13], clip_index * k, k, 1)
    own_bias = lax.dynamic_slice(
        small[13:17].reshape(-1, 128),
        (head_index * up_bias.shape[0], clip_index * up_bias.shape[1]),
        up_bias.shape,
    )

    square_parts = update(
        projections, projections_moment, projections_average, own_square, RATE_MATRIX
    )
    ffn_parts = update(feedforward, feedforward_moment, feedforward_average, own_wide, RATE_MATRIX)
    bias_parts = update(up_bias, up_bias_moment, up_bias_average, own_bias, RATE_VECTOR)
    vector_parts = update(vectors, vectors_moment, vectors_average, own_vector, RATE_VECTOR)
    return (output, input_gradient) + square_parts + ffn_parts + bias_parts + vector_parts


def solution(mesh):
    sizes = (mesh.shape["clip"], mesh.shape["head"])
    return jax.shard_map(
        functools.partial(per_device, sizes),
        mesh=mesh,
        in_specs=(
            P("clip", "head", None, None),
            P("clip", "head", None, None),
            P("clip"),
            P("clip"),
            P("clip", None, None),
            P(None, None, "head", None),
            P("head", None),
            P(),
            P(None, "head", None),
            P(None, "head", None),
            P(None, "head", None),
            P(None, "head"),
            P(None, "head", "clip"),
            P(None, "head", "clip"),
            P("head", "clip"),
            P(None, "clip"),
            P(None, "head", "clip"),
            P(None, "head", "clip"),
            P("head", "clip"),
            P(None, "clip"),
            P(None, "head", "clip"),
            P(None, "head", "clip"),
            P("head", "clip"),
            P(None, "clip"),
        ),
        out_specs=(
            P("clip", "head", None, None),
            P("clip", "head", None, None),
            P(None, "head", "clip"),
            P(None, "head", "clip"),
            P(None, "head", "clip"),
            P(None, "head", "clip"),
            P(None, "head", "clip"),
            P(None, "head", "clip"),
            P("head", "clip"),
            P("head", "clip"),
            P("head", "clip"),
            P(None, "clip"),
            P(None, "clip"),
            P(None, "clip"),
        ),
        check_vma=False,
    )
```

```python
import functools
import math

import jax
import jax.numpy as jnp
from jax import lax
from jax.experimental import pallas as pl
from jax.experimental.pallas import tpu as pltpu
from jax.sharding import PartitionSpec as P

C = 1280
HD = 160
HEADS = C // HD
GROUPS = 32
FMAX = 24
SIDE = 8
PIX = 64
TEXT_LEN = 77
BF = jnp.bfloat16
F32 = jnp.float32
MESH = pl.DeviceIdType.MESH

MOMENTUM = 0.9
RATE_MATRIX = 0.0002
RATE_VECTOR = 0.002
AVERAGE_DECAY = 0.7
GROUP_EPS = 1e-06
LAYER_EPS = 1e-05
MASK_FILL = -1e30


def place():
    c = lax.axis_index("clip")
    h = lax.axis_index("head")
    core, gx, gy = c % 2, (c // 2) % 2, c // 4
    partners = {
        "x": (c + 2 - 4 * gx, h),
        "y": (c + 4 - 8 * gy, h),
        "core": (c + 1 - 2 * core, h),
    }
    heads = [h, h + 1 - 2 * (h % 2), h + 2 - 4 * (h // 2), 3 - h]
    return c, h, core, gx, gy, partners, heads


def plane_of(core, gx, gy):
    plane = []
    for d in range(8):
        core_d, x_d, y_d = d % 2, d // 2 % 2, d // 4
        y, x = gy + y_d - 2 * gy * y_d, gx + x_d - 2 * gx * x_d
        plane.append((y, x, core + core_d - 2 * core * core_d))
    return plane


def plane_clips(plane):
    return [y * 4 + x * 2 + core for y, x, core in plane]


def greet(devices):
    barrier = pltpu.get_barrier_semaphore()
    for device in devices:
        pl.semaphore_signal(barrier, inc=1, device_id=device, device_id_type=MESH)
    pl.semaphore_wait(barrier, len(devices))


class Gather:

    def __init__(self, jobs, ins, outs, send, recv, load_sem, store_sem, hold):
        self.jobs = jobs
        self.sems = (send, recv, load_sem, store_sem)
        self.hold = hold
        c, h, core, gx, gy, partners, heads = place()
        self.c, self.h, self.core, self.gx, self.gy = c, h, core, gx, gy
        self.xp, self.yp, self.cp = partners["x"], partners["y"], partners["core"]
        self.heads = heads
        self.places = plane_of(core, gx, gy)
        self.plane = plane_clips(self.places)
        self.views = [self.view(job, ins, outs) for job in jobs]

    def peers(self):
        return [(self.plane[d], self.h) for d in range(1, 8)] + [
            (self.c, self.heads[j]) for j in (1, 2, 3)
        ]

    def copy(self, a, j, kind, src, dst, device):
        return pltpu.make_async_remote_copy(
            src_ref=src,
            dst_ref=dst,
            send_sem=self.sems[0].at[a, j, kind],
            recv_sem=self.sems[1].at[a, j, kind],
            device_id=device,
            device_id_type=MESH,
        )

    def view(self, job, ins, outs):
        kind, i_ref, o_ref, lo, at, n = job[0], ins[job[1]], outs[job[2]], job[3], job[4], job[5]
        core, gx, gy, h = self.core, self.gx, self.gy, self.h
        part, into = pl.ds(lo, n), pl.ds(at, n)
        if kind == "frozen":
            shard = i_ref.shape[-2]
            rows = shard // 4
            half = o_ref.shape[-1] // 2
            lanes = pl.ds(pl.multiple_of(core * half, 128), half)
            src = i_ref.at[part, pl.ds(pl.multiple_of((gy * 2 + gx) * rows, 16), rows), lanes]

            def slot(z, y, x, n0=0, nn=n, r0=0, rr=rows):
                first = pl.multiple_of(z * shard + (y * 2 + x) * rows + r0, 16)
                return o_ref.at[pl.ds(at + n0, nn), pl.ds(first, rr), lanes]

            def bundle(z):
                return [o_ref.at[into, pl.ds(pl.multiple_of(z * shard, 16), shard), lanes]]

            own = pl.ds(pl.multiple_of(h * shard, 16), shard)
            local = [(i_ref.at[lo + i], o_ref.at[at + i, own]) for i in range(n)]
        else:
            whole = i_ref.shape[-2]
            low, rows = job[6:] if len(job) > 6 else (0, whole)
            src = i_ref.at[part, pl.ds(low, rows)]

            def slot(z, y, x, n0=0, nn=n, r0=0, rr=rows):
                first = pl.multiple_of(((z * 2 + core) * 2 + x) * whole + low + r0, 16)
                return o_ref.at[pl.ds(at + n0, nn), y, pl.ds(first, rr)]

            def bundle(z):
                first = pl.multiple_of((z * 2 + core) * 2 * whole + low, 16)
                if rows == whole:
                    return [o_ref.at[into, :, pl.ds(first, 2 * rows)]]
                return [o_ref.at[into, :, pl.ds(first + x * whole, rows)] for x in (0, 1)]

            here = pl.ds(pl.multiple_of(((h * 2 + core) * 2 + gx) * whole + low, 16), rows)
            local = [
                (i_ref.at[lo + i, pl.ds(low, rows)], o_ref.at[at + i, gy, here]) for i in range(n)
            ]
        if n >= 4 or n == 2:
            first = dict(n0=0, nn=(n + 1) // 2)
            second = dict(n0=(n + 1) // 2, nn=n - (n + 1) // 2)
        else:
            top = (rows // 2 + 15) // 16 * 16
            first, second = dict(r0=0, rr=top), dict(r0=top, rr=rows - top)
        return kind, src, slot, bundle, local, first, second

    def local_copies(self, a):
        buf = self.hold.at[a % self.hold.shape[0]]
        triples = []
        for i, (src, dst) in enumerate(self.views[a][4]):
            rows, cols = src.shape
            triples.append((src, buf.at[pl.ds(i * rows, rows), pl.ds(0, cols)], dst))
        return triples

    def numbers(self, a):
        return (1, 2, 3) if self.views[a][0] == "frozen" else (0, 1, 2, 3)

    def fetch(self, a):
        src, slot = self.views[a][1:3]
        for j in (1, 2, 3):
            there = (self.c, self.heads[j])
            self.copy(a, j, 0, src, slot(self.h, self.gy, self.gx), there).start()

    def trade(self, a):
        src, slot = self.views[a][1:3]
        locals_ = self.local_copies(a)
        for k, (inp, mid, out) in enumerate(locals_):
            pltpu.make_async_copy(inp, mid, self.sems[2].at[a, k]).start()
        for j in self.numbers(a):
            here = slot(self.heads[j], self.gy, self.gx)
            if j:
                self.copy(a, j, 0, src, here, (self.c, self.heads[j])).wait_recv()
            give = here if j else src
            self.copy(a, j, 1, give, here, self.xp).start()
            self.copy(a, j, 2, give, here, self.yp).start()
        for k, (inp, mid, out) in enumerate(locals_):
            pltpu.make_async_copy(inp, mid, self.sems[2].at[a, k]).wait()
            pltpu.make_async_copy(mid, out, self.sems[3].at[a, k]).start()

    def forward(self, a):
        kind, src, slot, bundle, local, first, second = self.views[a]
        gx, gy, xp, yp = self.gx, self.gy, self.xp, self.yp
        for j in self.numbers(a):
            z = self.heads[j]
            from_x, from_y = slot(z, gy, 1 - gx), slot(z, 1 - gy, gx)
            self.copy(a, j, 1, from_x, from_x, xp).wait_recv()
            piece = slot(z, gy, 1 - gx, **first)
            self.copy(a, j, 3, piece, piece, yp).start()
            self.copy(a, j, 2, from_y, from_y, yp).wait_recv()
            piece = slot(z, 1 - gy, gx, **second)
            self.copy(a, j, 4, piece, piece, xp).start()
        for k, (inp, mid, out) in enumerate(self.local_copies(a)):
            pltpu.make_async_copy(mid, out, self.sems[3].at[a, k]).wait()

    def share(self, a):
        kind, src, slot, bundle, local, first, second = self.views[a]
        gx, gy, xp, yp = self.gx, self.gy, self.xp, self.yp
        for j in self.numbers(a):
            z = self.heads[j]
            piece = slot(z, 1 - gy, 1 - gx, **first)
            self.copy(a, j, 3, piece, piece, yp).wait_recv()
            piece = slot(z, 1 - gy, 1 - gx, **second)
            self.copy(a, j, 4, piece, piece, xp).wait_recv()
            for i, whole in enumerate(bundle(z)):
                self.copy(a, j, 5 + i, whole, whole, self.cp).start()

    def finish(self, a):
        kind, src, slot, bundle, local, first, second = self.views[a]
        gx, gy, xp, yp = self.gx, self.gy, self.xp, self.yp
        for j in self.numbers(a):
            z = self.heads[j]
            for i, whole in enumerate(bundle(z)):
                self.copy(a, j, 5 + i, whole, whole, self.cp).wait()
            here = slot(z, gy, gx)
            give = here if j else src
            if j:
                self.copy(a, j, 0, src, here, (self.c, z)).wait_send()
            self.copy(a, j, 1, give, here, xp).wait_send()
            self.copy(a, j, 2, give, here, yp).wait_send()
            piece = slot(z, gy, 1 - gx, **first)
            self.copy(a, j, 3, piece, piece, yp).wait_send()
            piece = slot(z, 1 - gy, gx, **second)
            self.copy(a, j, 4, piece, piece, xp).wait_send()

    def run(self, units, ahead=3):
        count = len(self.jobs)
        at, self.done = 0, 0

        def work(most):
            nonlocal at
            while at < len(units) and units[at][0] <= self.done and most > 0:
                units[at][1]()
                at += 1
                most -= 1

        for a in range(min(ahead, count)):
            self.fetch(a)
        work(2)
        for step in range(count + 3):
            if step < count:
                self.trade(step)
                work(1)
            if step + ahead < count:
                self.fetch(step + ahead)
            if 0 <= step - 1 < count:
                self.forward(step - 1)
                work(1)
            if 0 <= step - 2 < count:
                self.share(step - 2)
                work(1)
            if 0 <= step - 3 < count:
                self.finish(step - 3)
                self.done = step - 2
                work(1)
        work(len(units))


FROZEN = [(0, 0, 1), (1, 0, 9), (1, 9, 9), (2, 0, 1), (2, 1, 3), (2, 4, 1), (2, 5, 1)]
FROZEN += [(3, 0, 2), (2, 6, 1), (4, 0, 1), (4, 1, 1), (4, 2, 1), (2, 7, 1)]


def frozen_arrays(conv_weight, time_weight, spatial_square, cross_kv, spatial_ffn):
    return [
        time_weight[None],
        conv_weight.reshape((18,) + conv_weight.shape[2:]),
        spatial_square,
        cross_kv,
        spatial_ffn,
    ]


def gather_plain(arrays, small, projections, feedforward):
    small = lax.all_gather(lax.all_gather(small, "head", axis=0), "clip", axis=0)
    frozen = [
        lax.all_gather(arrays[i][lo : lo + n], "head", axis=1, tiled=True) for i, lo, n in FROZEN
    ]
    trained = [
        lax.all_gather(
            lax.all_gather(a.astype(BF), "clip", axis=2, tiled=True), "head", axis=1, tiled=True
        )
        for a in (projections, feedforward)
    ]
    return frozen, trained, small


TILE = 256


def stream(count, tiles, body, sem, slots):
    def begin(i):
        for p, (src, dst) in enumerate(tiles(i, i % slots)):
            pltpu.make_async_copy(src, dst, sem.at[i % slots, p]).start()

    for i in range(min(slots - 1, count)):
        begin(i)

    def step(i, carry):
        @pl.when(i + slots - 1 < count)
        def _():
            begin(i + slots - 1)

        for p, (src, dst) in enumerate(tiles(i, i % slots)):
            pltpu.make_async_copy(src, dst, sem.at[i % slots, p]).wait()
        body(i, i % slots)
        return carry

    lax.fori_loop(0, count, step, 0)


def tile_at(i):
    return pl.ds(pl.multiple_of(i * TILE, TILE), TILE)


class Weights:
    def __init__(self, buf, sem, there=lambda need: True):
        self.buf, self.sem, self.there = buf, sem, there
        self.items, self.begun = [], set()

    def add(self, ref, need=0, fresh=False):
        self.items.append((ref, need, fresh))
        return len(self.items) - 1

    def copy(self, i):
        ref = self.items[i][0]
        rows, cols = ref.shape
        dst = self.buf.at[i % 2, pl.ds(0, rows), pl.ds(0, cols)]
        return pltpu.make_async_copy(ref, dst, self.sem.at[i % 2])

    def begin(self, i):
        self.begun.add(i)
        self.copy(i).start()

    def use(self, i):
        if i not in self.begun:
            self.begin(i)
        after = i + 1
        if after < len(self.items):
            ref, need, fresh = self.items[after]
            if not fresh and self.there(need):
                self.begin(after)
        self.copy(i).wait()
        rows, cols = self.items[i][0].shape
        return self.buf[i % 2, pl.ds(0, rows), pl.ds(0, cols)]

    def through(self, x, i, sink):
        sink(pl.ds(0, C), dot_f32(x[...], self.use(i), ((1,), (0,))))

    def against(self, x, i, sink):
        sink(pl.ds(0, C), dot_f32(x[...], self.use(i), ((1,), (1,))))


def frame_rows(f):
    return pl.ds(pl.multiple_of(f * PIX, PIX), PIX)


def norm_rows(x, q, gain, out, codes=None):
    block = PIX if codes is None else x.shape[0] // FMAX

    def body(f, carry):
        rows = pl.ds(pl.multiple_of(f * block, block), block)
        v = x[rows, :]
        v = v - jnp.mean(v, axis=1, keepdims=True)
        scale = lax.rsqrt(jnp.mean(v * v, axis=1, keepdims=True) + LAYER_EPS)
        v = v * scale * q[gain : gain + 1] + q[gain + 1 : gain + 2]
        if codes is not None:
            v = v + codes[pl.ds(f, 1), :]
        out[rows, :] = v.astype(out.dtype)
        return carry

    lax.fori_loop(0, x.shape[0] // block, body, 0)


def dot_split(a, fold, dims):
    high = a.astype(BF)
    rest = a - high.astype(F32)
    middle = rest.astype(BF)
    last = (rest - middle.astype(F32)).astype(BF)
    out = dot_f32(jnp.concatenate([high, middle, last], axis=0), fold[...], dims)
    n = a.shape[0]
    return out[0:n] + out[n : 2 * n] + out[2 * n : 3 * n]


def group_spread(sums, fold):
    means = dot_split(sums, fold, ((1,), (0,))) * (1.0 / (C // GROUPS * PIX))
    return dot_split(means, fold, ((1,), (1,)))


def group_stats(x, fold, stat):
    frames = x.shape[0] // PIX
    stat[0] = jnp.zeros_like(stat[0])
    stat[1] = jnp.zeros_like(stat[1])
    for f in range(frames):
        block = x[f * PIX : (f + 1) * PIX, :].astype(F32)
        stat[0, f : f + 1] = jnp.sum(block, axis=0, keepdims=True)
    stat[0] = group_spread(stat[0], fold)
    for f in range(frames):
        block = x[f * PIX : (f + 1) * PIX, :].astype(F32) - stat[0, f : f + 1]
        stat[1, f : f + 1] = jnp.sum(block * block, axis=0, keepdims=True)
    stat[1] = lax.rsqrt(group_spread(stat[1], fold) + GROUP_EPS)


def group_apply(x, stat, q, gain, out, act):
    for f in range(x.shape[0] // PIX):
        rows = slice(f * PIX, (f + 1) * PIX)
        v = (x[rows, :].astype(F32) - stat[0, f : f + 1]) * stat[1, f : f + 1]
        out[rows, :] = act(v * q[gain : gain + 1] + q[gain + 1 : gain + 2]).astype(out.dtype)


def group_matrix():
    group = jnp.arange(C) // (C // GROUPS)
    return (group[:, None] == jnp.arange(128)[None, :]).astype(BF)


def make_windows(x, win, flipped):
    tokens = x.shape[0]

    def body(j, carry):
        lanes = pl.ds(pl.multiple_of(j * 128, 128), 128)
        v = x[:, lanes]
        row = lax.broadcasted_iota(jnp.int32, v.shape, 0)
        py, px = row // SIDE % SIDE, row % SIDE
        for tap in range(9):
            dy, dx = tap // 3 - 1, tap % 3 - 1
            if flipped:
                dy, dx = -dy, -dx
            shift = (-(dy * SIDE + dx)) % tokens
            moved = pltpu.roll(v, shift, 0) if shift else v
            ok = (py + dy >= 0) & (py + dy < SIDE) & (px + dx >= 0) & (px + dx < SIDE)
            win[tap, :, lanes] = jnp.where(ok, moved, 0.0).astype(win.dtype)
        return carry

    lax.fori_loop(0, C // 128, body, 0)


def silu(v):
    return v / (1.0 + jnp.exp(-v))


ORDER = (0, 3, 4, 5, 1, 7, 8, 9, 6, 2)
AT = tuple(ORDER.index(i) for i in range(10))


def forward_kernel(jobs, needs, n_saved, *refs):
    ins, refs = refs[:5], refs[5:]
    square_own, wide_own, cot, vec_own, up_own = refs[:5]
    lat, q, time_in, text, gate_bias, fold, codes, tbias = refs[5:13]
    outs, refs = refs[13:28], refs[28:]
    saved, refs = refs[:n_saved], refs[n_saved:]
    g_pixels, vf, text_k, text_v = refs[:4]
    (
        send, recv, load_sem, store_sem, hold,
        bias_send, bias_recv, bias_all, col_sem, row_sem, save_sem,
        plane_send, plane_recv, hop_send, hop_recv, keep_sem, in_sem,
        square_land, wide_land, vec_land, up_land, square_full, wide_full, up_mine, up_all,
        win, weight_buf, stage, acc, tmp, nrm, att, stat, extra,
        hid1, first, state0, state1, state2, second, self_q, self_k, self_v, cross_q,
    ) = refs[4:]
    (time_w, conv1, conv2, in_w, qkv_w, self_o, cross_w, text_w, cross_o, value_w, gate_w,
     down_w, out_w, square_w, wide_w) = outs
    value_out, gate_out, inner_out, normed_out = saved[10:14]
    comm = Gather(
        jobs, list(ins) + [square_full, wide_full], outs, send, recv, load_sem, store_sem, hold
    )
    ring = Weights(weight_buf, col_sem, lambda need: need <= comm.done)

    def part_of(slot, j):
        return weight_buf.at[slot, pl.ds(j * TILE, TILE)]

    greet(comm.peers())
    c, h, heads, plane = comm.c, comm.h, comm.heads, comm.plane
    share = lat.shape[0] // 4

    def bias_copy(j):
        return pltpu.make_async_remote_copy(
            src_ref=gate_bias,
            dst_ref=bias_all.at[comm.h],
            send_sem=bias_send.at[j],
            recv_sem=bias_recv.at[j],
            device_id=(comm.c, comm.heads[j]),
            device_id_type=MESH,
        )

    for j in (1, 2, 3):
        bias_copy(j).start()
    bias_all[comm.h] = gate_bias[...]

    def bias_in():
        for j in (1, 2, 3):
            bias_copy(j).wait()

    def trained_parts(d):
        y, x, core = comm.places[d]
        rows = core * 2 + x
        square_rows = pl.ds(pl.multiple_of(rows * 80, 16), 80)
        parts = []
        for k in range(5):
            one, other = ORDER[2 * k : 2 * k + 2]
            src = square_own.at[one + y * (other - one), square_rows]
            parts.append((src, square_land.at[c, k]))
        wide_rows = pl.ds(pl.multiple_of(rows * 320, 16), 320)
        return parts + [(wide_own.at[y, wide_rows], wide_land.at[c])]

    def plane_copies():
        copies = []
        for d in range(1, 8):
            parts = trained_parts(d) + [(vec_own, vec_land.at[c]), (up_own, up_land.at[c])]
            for i, (src, dst) in enumerate(parts):
                copies.append(
                    pltpu.make_async_remote_copy(
                        src_ref=src,
                        dst_ref=dst,
                        send_sem=plane_send.at[i, d],
                        recv_sem=plane_recv.at[i, d],
                        device_id=(plane[d], h),
                        device_id_type=MESH,
                    )
                )
        return copies

    def plane_own():
        return [
            pltpu.make_async_copy(src, dst, plane_send.at[i, 0])
            for i, (src, dst) in enumerate(trained_parts(0))
        ]

    for item in plane_copies() + plane_own():
        item.start()
    vec_land[c] = vec_own[...]
    up_land[c] = up_own[...]

    def up_copy(j):
        return pltpu.make_async_remote_copy(
            src_ref=up_mine,
            dst_ref=up_all.at[h],
            send_sem=hop_send.at[2, j],
            recv_sem=hop_recv.at[2, j],
            device_id=(c, heads[j]),
            device_id_type=MESH,
        )

    def assemble_unit():
        for item in plane_copies() + plane_own():
            item.wait()
        for i in range(8):
            lanes = slice(i * HD, (i + 1) * HD)
            square_full[:, :, lanes] = square_land[i]
            wide_full[0, :, lanes] = wide_land[i]
            vf[:, lanes] = vec_land[i].astype(BF).astype(F32)
            up_mine[:, i * 16 : (i + 1) * 16] = up_land[i].astype(BF).astype(F32)
        for j in (1, 2, 3):
            up_copy(j).start()
        up_all[h] = up_mine[...]

    def cot_copies():
        at = g_pixels.at[pl.ds(h * cot.shape[0], cot.shape[0])]
        return [
            pltpu.make_async_remote_copy(
                src_ref=cot.at[:, heads[j]],
                dst_ref=at,
                send_sem=hop_send.at[0, j],
                recv_sem=hop_recv.at[0, j],
                device_id=(c, heads[j]),
                device_id_type=MESH,
            )
            for j in (1, 2, 3)
        ]

    def cot_own():
        at = g_pixels.at[pl.ds(h * cot.shape[0], cot.shape[0])]
        return pltpu.make_async_copy(cot.at[:, h], at, hop_send.at[0, 0])

    for item in cot_copies() + [cot_own()]:
        item.start()

    def keep(i, src):
        pltpu.make_async_copy(src, saved[i], keep_sem.at[i]).start()

    def kept(*pairs):
        for i, src in pairs:
            pltpu.make_async_copy(src, saved[i], keep_sem.at[i]).wait()

    def time_unit(w):
        def sink(lanes, tile):
            extra[:, lanes] = tile + q[2:3, lanes] + q[3:4, lanes]

        ring.through(time_in, w, sink)

    def act1_unit():
        group_stats(lat, fold, stat)
        group_apply(lat, stat, q, 0, tmp, silu)

    def windows_unit():
        make_windows(tmp, win, False)

    def conv_unit(w, tap):
        def sink(lanes, tile):
            if tap == 0:
                acc[:, lanes] = tile
            else:
                acc[:, lanes] += tile

        ring.through(win.at[tap], w, sink)

    def act2_unit():
        hid1[...] = acc[...] + extra[0:1]
        keep(0, hid1)
        group_stats(hid1, fold, stat)
        group_apply(hid1, stat, q, 4, tmp, silu)

    def first_unit():
        first[...] = lat[...].astype(F32) + acc[...] + q[6:7]
        keep(1, first)
        group_stats(first, fold, stat)
        group_apply(first, stat, q, 7, nrm, lambda v: v)

    def add_unit(w, x, base, bias, out, norm, at):
        def sink(lanes, tile):
            total = tile + q[bias : bias + 1, lanes]
            out[:, lanes] = total if base is None else total + base[:, lanes]

        ring.through(x, w, sink)
        keep(at, out)
        if norm is not None:
            norm_rows(out, q, norm, nrm)

    def project_unit(x, w, out, at=None):
        def sink(lanes, tile):
            out[:, lanes] = tile.astype(BF)

        ring.against(x, w, sink)
        if at is not None:
            keep(at, out)

    def project_first(w, x, out, at=None):
        project_unit(x, w, out, at)

    def attend_unit(qr, kr, vr, bias):
        attend_body(qr, kr, vr, bias, att, tmp)

    def save(i, k):
        dst = (value_out, gate_out)[k].at[:, tile_at(i)]
        return pltpu.make_async_copy(stage.at[i % 2, k], dst, save_sem.at[i % 2, k])

    def ffn_unit(part, parts):
        per = value_w.shape[1] // TILE // parts
        start = part * per

        def tiles(i, slot):
            rows = tile_at(start + i)
            return [
                (value_w.at[0, rows], part_of(slot, 0)),
                (gate_w.at[0, rows], part_of(slot, 1)),
                (down_w.at[0, rows], part_of(slot, 2)),
            ]

        def body(i, slot):
            tile = start + i
            lanes = tile_at(tile % 5)
            z = tile // 5
            x = nrm[...]
            value = dot_f32(x, part_of(slot, 0)[...], ((1,), (1,))) + bias_all[z, 0:1, lanes]
            gate = dot_f32(x, part_of(slot, 1)[...], ((1,), (1,))) + bias_all[z, 1:2, lanes]
            mixed = (value * gelu_erf(gate)).astype(BF)

            @pl.when(tile >= 2)
            def _():
                save(tile - 2, 0).wait()
                save(tile - 2, 1).wait()

            stage[tile % 2, 0] = value.astype(BF)
            stage[tile % 2, 1] = gate.astype(BF)
            save(tile, 0).start()
            save(tile, 1).start()
            acc[...] += dot_f32(mixed, part_of(slot, 2)[...], ((1,), (0,)))

        if part == 0:
            acc[...] = state2[...] + q[18:19]
        stream(per, tiles, body, row_sem, 2)
        if part == parts - 1:
            for tile in (value_w.shape[1] // TILE - 2, value_w.shape[1] // TILE - 1):
                save(tile, 0).wait()
                save(tile, 1).wait()
            nrm[...] = acc[...].astype(BF)

    def gone_unit():
        group_stats(second, fold, stat)
        per = PIX // 4
        for f in range(second.shape[0] // PIX):
            v = second[f * PIX : (f + 1) * PIX, :]
            v = (v - stat[0, f : f + 1]) * stat[1, f : f + 1]
            v = (v * vf[0:1] + vf[1:2]).astype(BF)
            for z in range(4):
                win[8, pl.ds(z * share + f * per, per), :] = v[z * per : (z + 1) * per]
        for item in hop_copies() + [hop_own()]:
            item.start()

    def hop_rows(z):
        return pl.ds(pl.multiple_of(z * share, 16), share)

    def hop_copies():
        return [
            pltpu.make_async_remote_copy(
                src_ref=win.at[8, hop_rows(heads[j])],
                dst_ref=normed_out.at[hop_rows(h)],
                send_sem=hop_send.at[1, j],
                recv_sem=hop_recv.at[1, j],
                device_id=(c, heads[j]),
                device_id_type=MESH,
            )
            for j in (1, 2, 3)
        ]

    def hop_own():
        src = win.at[8, hop_rows(h)]
        return pltpu.make_async_copy(src, normed_out.at[hop_rows(h)], hop_send.at[1, 0])

    def arrive_unit():
        for item in hop_copies() + [hop_own()]:
            item.wait()
        item = pltpu.make_async_copy(normed_out, nrm, in_sem.at[0])
        item.start()
        item.wait()
        for item in cot_copies() + [cot_own()]:
            item.wait()
        for j in (1, 2, 3):
            up_copy(j).wait()
        kept((0, hid1), (2, state0), (3, state1))
        kept((6, self_q), (7, self_k), (8, self_v), (9, cross_q))

    def motion_add_unit(x, w, base, bias, out, norm, at, tat, code, before):
        def sink(lanes, tile):
            total = tile + vf[bias : bias + 1, lanes]
            out[:, lanes] = total if base is None else total + base[:, lanes]

        ring.through(x, w, sink)
        keep(at, out)
        kept(*before)
        norm_rows(out, vf, norm, nrm, codes if code else None)
        keep(tat, nrm)

    def motion_first(w, x, *rest):
        motion_add_unit(x, w, *rest)

    def motion_project_unit(w, out, at, before):
        kept(*before)
        project_unit(nrm, w, out, at)

    def motion_attend_unit(at, before):
        kept(*before)
        attend_body(self_q, self_k, self_v, tbias, att, tmp)
        keep(at, att)

    def inner_copy(i):
        src = stage.at[i % 2, 0]
        return pltpu.make_async_copy(src, inner_out.at[:, tile_at(i)], save_sem.at[i % 2, 0])

    def wide_unit(part, parts):
        count = wide_w.shape[2] // TILE
        per = count // parts
        start = part * per

        def tiles(i, slot):
            rows = tile_at(start + i)
            return [
                (wide_w.at[0, 0, rows], part_of(slot, 0)),
                (wide_w.at[0, 1, rows], part_of(slot, 1)),
            ]

        def body(i, slot):
            tile = start + i
            z, row = tile // 5, tile % 5 * 2
            bias = [up_all[z, pl.ds(row + k, 1), :] for k in (0, 1)]
            inner = dot_f32(nrm[...], part_of(slot, 0)[...], ((1,), (1,)))
            inner = inner + jnp.concatenate(bias, axis=1)

            @pl.when(tile >= 2)
            def _():
                inner_copy(tile - 2).wait()

            stage[tile % 2, 0] = inner.astype(BF)
            inner_copy(tile).start()
            acc[...] += dot_f32(gelu_tanh(inner).astype(BF), part_of(slot, 1)[...], ((1,), (0,)))

        if part == 0:
            acc[...] = state1[...] + vf[11:12]
        stream(per, tiles, body, row_sem, 2)
        if part == parts - 1:
            for tile in (count - 2, count - 1):
                inner_copy(tile).wait()
            kept((19, nrm))
            nrm[...] = acc[...].astype(BF)
            keep(22, nrm)

    def nothing():
        pass

    P_ = functools.partial
    units = [(0, act1_unit), (0, windows_unit), (0, assemble_unit)]

    def with_weight(key, ref, unit, *rest, fresh=False):
        return needs[key], P_(unit, ring.add(ref, needs[key], fresh), *rest)

    def square(i):
        return square_w.at[AT[i] // 2, AT[i] % 2]

    units += [with_weight("time", time_w.at[0], time_unit)]
    units += [with_weight(("conv1", t), conv1.at[t], conv_unit, t) for t in range(9)]
    units += [(0, act2_unit), (0, windows_unit)]
    units += [with_weight(("conv2", t), conv2.at[t], conv_unit, t) for t in range(9)]
    units += [(0, first_unit)]
    units += [with_weight("in", in_w.at[0], add_unit, nrm, None, 9, state0, 10, 2)]
    units += [
        with_weight("qkv", qkv_w.at[i], project_first, nrm, o, 6 + i)
        for i, o in enumerate((self_q, self_k, self_v))
    ]
    units += [(0, P_(attend_unit, self_q, self_k, self_v, spatial_mask))]
    units += [with_weight("self_o", self_o.at[0], add_unit, att, state0, 12, state1, 13, 3)]
    units += [with_weight("cross", cross_w.at[0], project_first, nrm, cross_q, 9)]
    units += [with_weight("text", text_w.at[0], project_first, text, text_k)]
    units += [with_weight("text", text_w.at[1], project_first, text, text_v)]
    units += [(0, P_(attend_unit, cross_q, text_k, text_v, text_mask))]
    units += [with_weight("cross_o", cross_o.at[0], add_unit, att, state1, 15, state2, 16, 4)]
    units += [(0, bias_in)]
    units += [(needs["ffn"], P_(ffn_unit, i, 5)) for i in range(5)]
    units += [
        with_weight("out", out_w.at[0], add_unit, nrm, first, 19, second, None, 5, fresh=True)
    ]
    entered, block1, block2 = hid1, state0, state1
    qkv = (self_q, self_k, self_v)
    units += [(0, gone_unit), (0, nothing), (0, nothing), (0, nothing), (0, arrive_unit)]
    units += [
        with_weight(
            ("square", 0), square(0), motion_first, nrm, None, 2, entered, 3, 14, 17, True, ()
        )
    ]
    units += [
        with_weight(("square", 3 + i), square(3 + i), motion_project_unit, o, 23 + i, ())
        for i, o in enumerate(qkv)
    ]
    units += [(0, P_(motion_attend_unit, 20, ()))]
    units += [
        with_weight(
            ("square", 1),
            square(1),
            motion_first,
            att, entered, 5, block1, 6, 15, 18, True, ((17, nrm),),
        )
    ]
    units += [
        with_weight(
            ("square", 7 + i), square(7 + i), motion_project_unit, o, 26 + i, ((23 + i, o),)
        )
        for i, o in enumerate(qkv)
    ]
    units += [(0, P_(motion_attend_unit, 21, ((20, att),)))]
    units += [
        with_weight(
            ("square", 6),
            square(6),
            motion_first,
            att, block1, 8, block2, 9, 16, 19, False, ((18, nrm),),
        )
    ]
    units += [(needs["wide"], P_(wide_unit, i, 5)) for i in range(5)]
    comm.run(units)
    kept((1, first), (4, state2), (5, second), (14, entered), (15, block1), (16, block2))
    kept((21, att), (22, nrm))
    kept(*[(26 + i, o) for i, o in enumerate(qkv)])


def forward_fused(
    arrays, projections, feedforward, vectors, up_bias, lat, cot, q, time_in, text, gate_bias, tbias
):
    tokens = lat.shape[0]
    ins = list(arrays)
    shapes, jobs, needs = [], [], {}
    names = ["time", "conv1", "conv2", "in", "qkv", "self_o", "cross", "text", "cross_o"]
    names += ["value", "gate", "ffn", "out"]
    for o, (i, lo, n) in enumerate(FROZEN):
        rows, cols = ins[i].shape[1:]
        shapes.append((n, 4 * rows, cols))
        step = 3 if n == 9 else n
        for at in range(0, n, step):
            jobs.append(("frozen", i, o, lo + at, at, step))
            if n == 9:
                for t in range(at, at + step):
                    needs[names[o], t] = len(jobs)
        needs[names[o]] = len(jobs)
    shapes += [(5, 2, C, C), (1, 2, 4 * C, C)]
    for k in range(5):
        jobs.append(("own", 5, 13, k, k, 1))
        for i in ORDER[2 * k : 2 * k + 2]:
            needs["square", i] = len(jobs)
    jobs += [("own", 6, 14, 0, 0, 1, low, 80) for low in range(0, 320, 80)]
    needs["wide"] = len(jobs)
    count = len(jobs)
    most = max(j[5] * ins[j[1]].shape[1] for j in jobs if j[0] == "frozen")
    any_spec, vmem = pl.BlockSpec(memory_space=pl.ANY), pl.BlockSpec(memory_space=pltpu.VMEM)
    dma = pltpu.SemaphoreType.DMA

    def array(shape, dtype=BF):
        return jax.ShapeDtypeStruct(shape, dtype)

    f32, low, hidden = array((tokens, C), F32), array((tokens, C)), array((tokens, 4 * C))
    saved = [f32] * 6 + [low] * 4 + [hidden] * 3 + [low] + [f32] * 3 + [low] * 12
    outs = pl.pallas_call(
        functools.partial(forward_kernel, jobs, needs, len(saved)),
        out_shape=tuple(array(shape) for shape in shapes)
        + tuple(saved)
        + (
            array((FMAX, tokens // FMAX, C)),
            array((16, C), F32),
            array((text.shape[0], C)),
            array((text.shape[0], C)),
        ),
        in_specs=[any_spec] * 8 + [vmem] * 10,
        out_specs=(any_spec,) * (len(shapes) + len(saved) + 1) + (vmem,) * 3,
        scratch_shapes=[
            dma((count, 4, 7)),
            dma((count, 4, 7)),
            dma((count, 4)),
            dma((count, 4)),
            pltpu.VMEM((2, most, C), BF),
            dma((4,)),
            dma((4,)),
            pltpu.VMEM((4, 8, C), F32),
            dma((2,)),
            dma((2, 3)),
            dma((2, 2)),
            dma((8, 8)),
            dma((8, 8)),
            dma((3, 4)),
            dma((3, 4)),
            dma((len(saved),)),
            dma((1,)),
            pltpu.VMEM((8, 5, 80, HD), BF),
            pltpu.VMEM((8, 320, HD), BF),
            pltpu.VMEM((8, 16, HD), F32),
            pltpu.VMEM((8, 16, 16), F32),
            pltpu.VMEM((5, 80, C), BF),
            pltpu.VMEM((1, 320, C), BF),
            pltpu.VMEM((16, 128), F32),
            pltpu.VMEM((4, 16, 128), F32),
            pltpu.VMEM((9, tokens, C), BF),
            pltpu.VMEM((2, C, C), BF),
            pltpu.VMEM((2, 2, tokens, TILE), BF),
            pltpu.VMEM((tokens, C), F32),
            pltpu.VMEM((tokens, C), F32),
            pltpu.VMEM((tokens, C), BF),
            pltpu.VMEM((tokens, C), BF),
            pltpu.VMEM((2, 8, C), F32),
            pltpu.VMEM((16, C), F32),
        ]
        + [pltpu.VMEM((tokens, C), F32)] * 6
        + [pltpu.VMEM((tokens, C), BF)] * 4,
        compiler_params=pltpu.CompilerParams(
            collective_id=1, has_side_effects=True, vmem_limit_bytes=60 << 20
        ),
    )(
        *ins,
        projections.astype(BF),
        feedforward.astype(BF),
        cot.reshape(tokens // PIX, 4, PIX // 4, C),
        jnp.pad(vectors, ((0, 3), (0, 0))),
        jnp.pad(up_bias, ((0, 6), (0, 0))),
        lat,
        jnp.pad(q, ((0, 4), (0, 0))),
        jnp.pad(time_in, ((0, 15), (0, 0))),
        text,
        jnp.pad(gate_bias, ((0, 6), (0, 0))),
        group_matrix(),
        frame_table(),
        tbias,
    )
    frozen, trained, kept = outs[:13], (outs[13].reshape(10, C, C), outs[14][0]), outs[15:44]
    g_pixels, vf, text_k, text_v = outs[44:]
    states = tuple(kept[:10]) + (text_k, text_v) + tuple(kept[10:12])
    motion = (kept[13],) + tuple(kept[14:22]) + (kept[12],) + tuple(kept[22:29])
    return frozen, trained, states, motion, g_pixels.reshape(tokens, C), vf


def pack_small(vectors, up_bias):
    flat = jnp.concatenate([a.astype(BF).reshape(-1) for a in (vectors, up_bias)])
    return jnp.pad(flat, (0, 32 * C - flat.shape[0])).reshape(32, C)


def unpack_small(sizes, packed, vectors, up_bias):
    packed = packed.reshape(sizes[0], sizes[1], -1).astype(F32)
    vector = packed[:, 0, : vectors.size].reshape((sizes[0],) + vectors.shape)
    bias = packed[:, :, vectors.size : vectors.size + up_bias.size]
    bias = bias.reshape(sizes + up_bias.shape).transpose(1, 2, 0, 3)
    return vector.transpose(1, 0, 2).reshape(vectors.shape[0], C), bias.reshape(1, -1)


def sum_plain(parts, wide_parts, small):
    sums = [
        jnp.stack(
            [
                lax.psum_scatter(
                    lax.psum_scatter(g, "head", scatter_dimension=0, tiled=True),
                    "clip",
                    scatter_dimension=1,
                    tiled=True,
                ).astype(F32)
                for g in a
            ]
        )
        for a in (parts, wide_parts)
    ]
    return sums + [lax.psum(small, ("clip", "head"))]


def head_window(head):
    start = head * HD // 128 * 128
    return start, head * HD - start


def lane_mask(shape, low):
    lane = lax.broadcasted_iota(jnp.int32, shape, 1)
    return (lane >= low) & (lane < low + HD)


def dot_f32(a, b, dims):
    return lax.dot_general(a, b, (dims, ((), ())), preferred_element_type=F32)


def spatial_mask(shape):
    row = lax.broadcasted_iota(jnp.int32, shape, 0)
    return row // PIX == lax.broadcasted_iota(jnp.int32, shape, 1) // PIX


def text_mask(shape):
    return lax.broadcasted_iota(jnp.int32, shape, 1) < TEXT_LEN


def head_probs(q, k, bias):
    scores = dot_f32(q, k, ((1,), (1,))) * HD ** (-0.5)
    if callable(bias):
        scores = jnp.where(bias(scores.shape), scores, MASK_FILL)
    else:
        scores = scores + bias[...]
    top = jnp.max(scores, axis=1, keepdims=True)
    weights = jnp.exp(scores - top)
    return weights / jnp.sum(weights, axis=1, keepdims=True)


def attend_body(q_ref, k_ref, v_ref, bias_ref, o_ref, acc):
    acc[...] = jnp.zeros_like(acc)
    for head in range(HEADS):
        start, low = head_window(head)
        win = pl.ds(start, 256)
        q = q_ref[:, win]
        mask = lane_mask(q.shape, low)
        q = jnp.where(mask, q, jnp.zeros_like(q))
        probs = head_probs(q, k_ref[:, win], bias_ref)
        out = dot_f32(probs.astype(BF), v_ref[:, win], ((1,), (0,)))
        acc[:, win] += jnp.where(mask, out, 0.0)
    o_ref[...] = acc[...].astype(BF)


def attend(q, k, v, bias):
    return pl.pallas_call(
        attend_body,
        out_shape=jax.ShapeDtypeStruct(q.shape, BF),
        scratch_shapes=[pltpu.VMEM(q.shape, F32)],
        compiler_params=pltpu.CompilerParams(vmem_limit_bytes=40 << 20),
    )(q, k, v, bias)


def attend_back_body(with_keys, q_ref, k_ref, v_ref, bias_ref, g_ref, *refs):
    if with_keys:
        dq_ref, dk_ref, dv_ref, dq, dk, dv = refs
        dk[...] = jnp.zeros_like(dk)
        dv[...] = jnp.zeros_like(dv)
    else:
        dq_ref, dq = refs
    dq[...] = jnp.zeros_like(dq)
    for head in range(HEADS):
        start, low = head_window(head)
        win = pl.ds(start, 256)
        q, k, v, g = q_ref[:, win], k_ref[:, win], v_ref[:, win], g_ref[:, win]
        mask = lane_mask(q.shape, low)
        q = jnp.where(mask, q, jnp.zeros_like(q))
        g = jnp.where(mask, g, jnp.zeros_like(g))
        probs = head_probs(q, k, bias_ref)
        dp = dot_f32(g, v, ((1,), (1,)))
        ds = probs * (dp - jnp.sum(dp * probs, axis=1, keepdims=True)) * HD ** (-0.5)
        ds = ds.astype(BF)
        dq[:, win] += jnp.where(mask, dot_f32(ds, k, ((1,), (0,))), 0.0)
        if with_keys:
            dk[:, win] += dot_f32(ds, q, ((0,), (0,)))
            dv[:, win] += dot_f32(probs.astype(BF), g, ((0,), (0,)))
    dq_ref[...] = dq[...].astype(BF)
    if with_keys:
        dk_ref[...] = dk[...].astype(BF)
        dv_ref[...] = dv[...].astype(BF)


def attend_back(q, k, v, bias, g, with_keys=True):
    count = 3 if with_keys else 1
    return pl.pallas_call(
        functools.partial(attend_back_body, with_keys),
        out_shape=(jax.ShapeDtypeStruct(q.shape, BF),) * count,
        scratch_shapes=[pltpu.VMEM(q.shape, F32)] * count,
        compiler_params=pltpu.CompilerParams(vmem_limit_bytes=48 << 20),
    )(q, k, v, bias, g)


def group_mean(per_channel):
    width = C // GROUPS
    means = jnp.mean(per_channel.reshape(-1, GROUPS, width), axis=-1) / PIX
    return jnp.repeat(means, width, axis=1)[:, None, :]


def gn_stats(x):
    center = group_mean(jnp.sum(x, axis=1))
    centered = x - center
    variance = group_mean(jnp.sum(centered * centered, axis=1))
    return center, lax.rsqrt(variance + GROUP_EPS)


def gn(x, stats, gain, shift):
    return (x - stats[0]) * stats[1] * gain + shift


def gn_back(dy, x, stats, gain):
    z = (x - stats[0]) * stats[1]
    gd = dy * gain
    mean_gd = group_mean(jnp.sum(gd, axis=1))
    mean_gz = group_mean(jnp.sum(gd * z, axis=1))
    return (gd - mean_gd - z * mean_gz) * stats[1]


def ln_stats(x):
    center = jnp.mean(x, axis=-1, keepdims=True)
    centered = x - center
    variance = jnp.mean(centered * centered, axis=-1, keepdims=True)
    return center, lax.rsqrt(variance + LAYER_EPS)


def ln(x, stats, gain, shift):
    return (x - stats[0]) * stats[1] * gain + shift


def ln_back(dy, x, stats, gain):
    z = (x - stats[0]) * stats[1]
    gd = dy * gain
    mean_gd = jnp.mean(gd, axis=-1, keepdims=True)
    mean_gz = jnp.mean(gd * z, axis=-1, keepdims=True)
    return (gd - mean_gd - z * mean_gz) * stats[1]


def ln_param_grads(dy, x, stats):
    z = (x - stats[0]) * stats[1]
    return jnp.sum(dy * z, axis=0), jnp.sum(dy, axis=0)


def silu_back(dy, v):
    gate = jax.nn.sigmoid(v)
    return dy * gate * (1.0 + v * (1.0 - gate))


def gelu_exact(v):
    return jax.nn.gelu(v, approximate=False)


def gelu_erf(v):
    return 0.5 * v * (1.0 + lax.erf(v * math.sqrt(0.5)))


def gelu_exact_slope(v):
    density = jnp.exp(-0.5 * v * v) * (1.0 / math.sqrt(2.0 * math.pi))
    return 0.5 * (1.0 + lax.erf(v * math.sqrt(0.5))) + v * density


def gelu_tanh(v):
    return jax.nn.gelu(v, approximate=True)


def gelu_tanh_slope(v):
    k = math.sqrt(2.0 / math.pi)
    t = jnp.tanh(k * (v + 0.044715 * v * v * v))
    return 0.5 * (1.0 + t) + 0.5 * v * (1.0 - t * t) * k * (1.0 + 3.0 * 0.044715 * v * v)


def frame_table():
    frame_pos = jnp.arange(FMAX, dtype=F32)[:, None]
    channel = jnp.arange(C)
    frequency = jnp.exp((channel - channel % 2).astype(F32) * (-math.log(10000.0) / C))
    angles = frame_pos * frequency[None, :]
    return jnp.where(channel[None, :] % 2 == 0, jnp.sin(angles), jnp.cos(angles))


def time_table(timesteps):
    half_width = C // 2
    frequency = jnp.exp(jnp.arange(half_width, dtype=F32) * (-math.log(10000.0) / half_width))
    angles = timesteps.astype(F32)[:, None] * frequency[None, :]
    return jnp.concatenate([jnp.cos(angles), jnp.sin(angles)], axis=1)


def through(x, w):
    return dot_f32(x, w, ((1,), (0,)))


def against(x, w):
    return dot_f32(x, w, ((1,), (1,)))


def outer(a, b):
    return dot_f32(a, b, ((0,), (0,))).astype(BF)


def windows(x, flipped):
    frames = x.shape[0]
    padded = jnp.pad(x.reshape(frames, SIDE, SIDE, C), ((0, 0), (1, 1), (1, 1), (0, 0)))
    pieces = []
    for tap in range(9):
        dy, dx = tap // 3, tap % 3
        if flipped:
            dy, dx = 2 - dy, 2 - dx
        pieces.append(padded[:, dy : dy + SIDE, dx : dx + SIDE].reshape(frames * PIX, C))
    return pieces


def conv(x, w):
    return through(jnp.concatenate(windows(x, False), axis=1), w.reshape(9 * C, C))


def conv_back(g, w):
    stacked = jnp.stack(windows(g, True), axis=1)
    return lax.dot_general(
        stacked, w, (((1, 2), (0, 2)), ((), ())), preferred_element_type=F32
    )


def update(weight, moment, average, gradient, step_rate):
    moment_new = MOMENTUM * moment + gradient
    weight_new = weight - step_rate * (gradient + MOMENTUM * moment_new)
    average_new = AVERAGE_DECAY * average + (1.0 - AVERAGE_DECAY) * weight_new
    return (moment_new, average_new, weight_new)


PAIRS = ((2, 6), (7, 8), (9, 1), (3, 4), (5, 0))
CHUNKS = 4 + len(PAIRS)
LANDED = 2


class GradientSum:
    def __init__(self, grads, landed, columns, bufs, sems, frees):
        self.grads, self.landed, self.columns = grads, landed, columns
        self.total, self.own, self.got_x, self.got_y, self.got2, self.got3, self.deal = bufs
        self.send, self.recv, self.load_sem = sems
        self.free_x, self.free_y, self.free2_x, self.free2_y, self.free3, self.free_core = frees
        c, h, core, gx, gy, partners, heads = place()
        self.c, self.h, self.core, self.gx, self.gy = c, h, core, gx, gy
        self.xp, self.yp, self.cp = partners["x"], partners["y"], partners["core"]
        self.heads = heads
        self.plane = plane_clips(plane_of(core, gx, gy))

    def peers(self):
        return [(self.plane[d], self.h) for d in range(1, 8)] + [
            (self.c, self.heads[j]) for j in (1, 2, 3)
        ]

    def block(self, k, y, z, core):
        if k < 4:
            ref, base = self.grads[10 + y], z * C + k * 320
        else:
            ref, base = self.grads[PAIRS[k - 4][y]], z * 320
        return ref.at[pl.ds(pl.multiple_of(base + core * 160, 16), 160)]

    def x_rows(self, x):
        return pl.ds(pl.multiple_of(x * 80, 16), 80)

    def copy(self, k, kind, src, dst, device):
        return pltpu.make_async_remote_copy(
            src_ref=src,
            dst_ref=dst,
            send_sem=self.send.at[k, kind],
            recv_sem=self.recv.at[k, kind],
            device_id=device,
            device_id_type=MESH,
        )

    def core_copies(self, k):
        return [
            self.copy(
                k,
                y * 4 + z,
                self.block(k, y, z, 1 - self.core),
                self.landed.at[k % LANDED, y, z],
                self.cp,
            )
            for y in (0, 1)
            for z in range(4)
        ]

    def landed_copy(self, k):
        slot = self.total.at[k % self.total.shape[0]]
        return pltpu.make_async_copy(self.landed.at[k % LANDED], slot, self.load_sem.at[k, 0])

    def own_copies(self, k):
        return [
            pltpu.make_async_copy(
                self.block(k, y, z, self.core),
                self.own.at[y, z],
                self.load_sem.at[k, 1 + y * 4 + z],
            )
            for y in (0, 1)
            for z in range(4)
        ]

    def first_copy(self, k):
        held = self.total.at[k % self.total.shape[0]]
        at = k // 2 % 2
        if k % 2 == 0:
            src = held.at[:, :, self.x_rows(1 - self.gx)]
            return self.copy(k, 8, src, self.got_x.at[at], self.xp)
        return self.copy(k, 8, held.at[1 - self.gy], self.got_y.at[at], self.yp)

    def second_copy(self, k):
        at = k // 2 % 2
        if k % 2 == 0:
            return self.copy(k, 9, self.got_x.at[at, 1 - self.gy], self.got2.at[k % 4], self.yp)
        src = self.got_y.at[at, :, self.x_rows(1 - self.gx)]
        return self.copy(k, 9, src, self.got2.at[k % 4], self.xp)

    def last_copies(self, k):
        return [
            self.copy(
                k,
                9 + j,
                self.got2.at[k % 4, self.heads[j]],
                self.got3.at[k % 2, j - 1],
                (self.c, self.heads[j]),
            )
            for j in (1, 2, 3)
        ]

    def deal_place(self, k):
        rows = self.core * 160 + self.gx * 80
        if k < 4:
            return self.columns[1].at[self.gy, pl.ds(pl.multiple_of(k * 320 + rows, 16), 80)]
        one, other = PAIRS[k - 4]
        at = one + self.gy * (other - one)
        return self.columns[0].at[at, pl.ds(pl.multiple_of(rows, 16), 80)]

    def deal_copies(self, k):
        at = self.deal_place(k)
        return [
            self.copy(k, 12 + d, self.deal.at[k % 2, self.plane[d]], at, (self.plane[d], self.h))
            for d in range(1, 8)
        ]

    def deal_own(self, k):
        src = self.deal.at[k % 2, self.c]
        return pltpu.make_async_copy(src, self.deal_place(k), self.load_sem.at[k, 9])

    def signal(self, sem, device):
        pl.semaphore_signal(sem, inc=1, device_id=device, device_id_type=MESH)

    def exchange(self, k):
        if k >= LANDED:
            pl.semaphore_wait(self.free_core, 1)
        for item in self.core_copies(k):
            item.start()

    def load(self, k):
        for item in self.core_copies(k):
            item.wait_recv()
        if k >= self.total.shape[0]:
            self.first_copy(k - self.total.shape[0]).wait_send()
        self.landed_copy(k).start()

    def load_own(self, k):
        for item in self.own_copies(k):
            item.start()

    def add_core(self, k):
        self.landed_copy(k).wait()
        if k + LANDED < CHUNKS:
            self.signal(self.free_core, self.cp)
        for item in self.own_copies(k):
            item.wait()
        slot = k % self.total.shape[0]
        total, own = self.total, self.own

        def body(i, carry):
            y, z = i // 4, i % 4
            total[slot, y, z] = total[slot, y, z] + own[y, z]
            return carry

        lax.fori_loop(0, 8, body, 0)
        if k >= 4:
            pl.semaphore_wait(self.free_x if k % 2 == 0 else self.free_y, 1)
        self.first_copy(k).start()

    def add_first(self, k):
        self.first_copy(k).wait_recv()
        slot, at = k % self.total.shape[0], k // 2 % 2
        total, got_x, got_y = self.total, self.got_x, self.got_y
        gy, mine = self.gy, self.x_rows(self.gx)

        def body(i, carry):
            if k % 2 == 0:
                y, z = i // 4, i % 4
                got_x[at, y, z] = got_x[at, y, z] + total[slot, y, z, mine, :]
            else:
                z = i // 2
                half = self.x_rows(i % 2)
                got_y[at, z, half, :] = got_y[at, z, half, :] + total[slot, gy, z, half, :]
            return carry

        lax.fori_loop(0, 8, body, 0)
        if k >= 4:
            pl.semaphore_wait(self.free2_y if k % 2 == 0 else self.free2_x, 1)
        self.second_copy(k).start()

    def add_second(self, k):
        self.second_copy(k).wait_recv()
        at = k // 2 % 2
        got_x, got_y, got2 = self.got_x, self.got_y, self.got2
        mine = self.x_rows(self.gx)

        def body(z, carry):
            if k % 2 == 0:
                got2[k % 4, z] = got2[k % 4, z] + got_x[at, self.gy, z]
            else:
                got2[k % 4, z] = got2[k % 4, z] + got_y[at, z, mine, :]
            return carry

        lax.fori_loop(0, 4, body, 0)
        self.second_copy(k).wait_send()
        if k + 4 < CHUNKS:
            if k % 2 == 0:
                self.signal(self.free_x, self.xp)
            else:
                self.signal(self.free_y, self.yp)
        for j, item in enumerate(self.last_copies(k)):
            if k >= 2:
                pl.semaphore_wait(self.free3.at[j], 1)
            item.start()

    def add_last(self, k):
        for item in self.last_copies(k):
            item.wait()
        got3, at = self.got3, k % 2
        rest = got3[at, 0].astype(F32) + got3[at, 1].astype(F32) + got3[at, 2].astype(F32)
        result = (self.got2[k % 4, self.h].astype(F32) + rest).astype(BF)
        if k + 4 < CHUNKS:
            if k % 2 == 0:
                self.signal(self.free2_y, self.yp)
            else:
                self.signal(self.free2_x, self.xp)
        if k + 2 < CHUNKS:
            for j in (1, 2, 3):
                self.signal(self.free3.at[j - 1], (self.c, self.heads[j]))
        if k >= 2:
            self.deal_done(k - 2)
        for d in range(8):
            self.deal[k % 2, d] = result[:, d * HD : (d + 1) * HD]
        for item in self.deal_copies(k):
            item.start()
        self.deal_own(k).start()

    def deal_done(self, k):
        for item in self.deal_copies(k):
            item.wait_send()
        self.deal_own(k).wait()

    def run(self, units, ready):
        at, sent, added = 0, 0, 0

        def flush():
            nonlocal sent
            while sent < CHUNKS and ready[sent] <= at and sent < added + LANDED:
                self.exchange(sent)
                sent += 1

        def work(most):
            nonlocal at
            for unit in units[at : at + most]:
                unit()
                at += 1
                flush()

        def until(k):
            if sent <= k:
                work(ready[k] - at)

        until(0)
        self.load(0)
        self.load_own(0)
        for step in range(CHUNKS + 4):
            if step < CHUNKS:
                self.add_core(step)
                added += 1
                flush()
                work(2)
            if 0 <= step - 2 < CHUNKS:
                self.add_first(step - 2)
                work(2)
            if step + 1 < CHUNKS:
                until(step + 1)
                self.load(step + 1)
                self.load_own(step + 1)
            if 0 <= step - 3 < CHUNKS:
                self.add_second(step - 3)
                work(2)
            if 0 <= step - 4 < CHUNKS:
                self.add_last(step - 4)
                work(2)
        work(len(units))
        for k in range(CHUNKS):
            for item in self.core_copies(k):
                item.wait_send()
            if k >= CHUNKS - self.total.shape[0]:
                self.first_copy(k).wait_send()
            for item in self.deal_copies(k):
                item.wait_recv()
        for k in (CHUNKS - 2, CHUNKS - 1):
            self.deal_done(k)


SMALL_ROWS = 24


class SmallSum:
    def __init__(self, total, small, out, land, room, send, recv, sem):
        self.t, self.small, self.out, self.land, self.room = total, small, out, land, room
        self.send, self.recv, self.sem = send, recv, sem

    def rows(self, i):
        return pl.ds(pl.multiple_of(i * SMALL_ROWS, 8), SMALL_ROWS)

    def copy(self, i, src, dst, device):
        return pltpu.make_async_remote_copy(
            src_ref=src,
            dst_ref=dst,
            send_sem=self.send.at[i],
            recv_sem=self.recv.at[i],
            device_id=device,
            device_id_type=MESH,
        )

    def plane_copies(self):
        t = self.t
        at = self.land.at[self.rows(t.c)]
        return [self.copy(d, self.small, at, (t.plane[d], t.h)) for d in range(1, 8)]

    def head_copies(self):
        t = self.t
        return [
            self.copy(7 + j, self.out, self.land.at[self.rows(7 + j)], (t.c, t.heads[j]))
            for j in (1, 2, 3)
        ]

    def gather(self, places):
        copies = [
            pltpu.make_async_copy(
                self.land.at[self.rows(p)], self.room.at[self.rows(i)], self.sem.at[i]
            )
            for i, p in enumerate(places)
        ]
        for item in copies:
            item.start()
        for item in copies:
            item.wait()
        for i in range(len(places)):
            self.out[...] += self.room[self.rows(i), :]

    def first(self):
        for item in self.plane_copies():
            item.start()

    def second(self):
        for item in self.plane_copies():
            item.wait()
        self.out[...] = self.small[...]
        self.gather([self.t.plane[d] for d in range(1, 8)])
        for item in self.head_copies():
            item.start()

    def last(self):
        for item in self.head_copies():
            item.wait()
        self.gather([8, 9, 10])


def column_sum(x, rows=PIX):
    total = jnp.sum(x[0:rows, :].astype(F32), axis=0, keepdims=True)
    for f in range(1, x.shape[0] // rows):
        total += jnp.sum(x[f * rows : (f + 1) * rows, :].astype(F32), axis=0, keepdims=True)
    return total


def norm_back_rows(dy, x, q, gain, out, vec=None):
    def body(f, carry):
        rows = frame_rows(f)
        v = x[rows, :]
        v = v - jnp.mean(v, axis=1, keepdims=True)
        scale = lax.rsqrt(jnp.mean(v * v, axis=1, keepdims=True) + LAYER_EPS)
        z = v * scale
        g = dy[rows, :]
        if vec is not None:
            vec[gain : gain + 1] += jnp.sum(g * z, axis=0, keepdims=True)
            vec[gain + 1 : gain + 2] += jnp.sum(g, axis=0, keepdims=True)
        gd = g * q[gain : gain + 1]
        m1 = jnp.mean(gd, axis=1, keepdims=True)
        m2 = jnp.mean(gd * z, axis=1, keepdims=True)
        out[rows, :] = out[rows, :] + (gd - m1 - z * m2) * scale
        return carry

    lax.fori_loop(0, x.shape[0] // PIX, body, 0)


def group_back(dy, x, q, gain, with_silu, fold, stat, sums, sink, vec=None):
    group_stats(x, fold, stat)
    frames = x.shape[0] // PIX
    sums[0] = jnp.zeros_like(sums[0])
    sums[1] = jnp.zeros_like(sums[1])

    def normal(f):
        block = x[f * PIX : (f + 1) * PIX, :].astype(F32)
        return (block - stat[0, f : f + 1]) * stat[1, f : f + 1]

    for f in range(frames):
        rows = slice(f * PIX, (f + 1) * PIX)
        z = normal(f)
        g = dy[rows, :]
        if with_silu:
            v = z * q[gain : gain + 1] + q[gain + 1 : gain + 2]
            gate = 1.0 / (1.0 + jnp.exp(-v))
            g = g * gate * (1.0 + v * (1.0 - gate))
        if vec is not None:
            vec[gain : gain + 1] += jnp.sum(g * z, axis=0, keepdims=True)
            vec[gain + 1 : gain + 2] += jnp.sum(g, axis=0, keepdims=True)
        gd = g * q[gain : gain + 1]
        dy[rows, :] = gd
        sums[0, f : f + 1] = jnp.sum(gd, axis=0, keepdims=True)
        sums[1, f : f + 1] = jnp.sum(gd * z, axis=0, keepdims=True)
    sums[0] = group_spread(sums[0], fold)
    sums[1] = group_spread(sums[1], fold)
    for f in range(frames):
        rows = slice(f * PIX, (f + 1) * PIX)
        dx = dy[rows, :] - sums[0, f : f + 1] - normal(f) * sums[1, f : f + 1]
        sink(rows, dx * stat[1, f : f + 1])


def backward_kernel(n_weights, *refs):
    weights, refs = refs[:n_weights], refs[n_weights:]
    conv1, conv2, in_w, qkv_w, self_o, cross_w, cross_o, value_w, gate_w, down_w, out_w = weights[:11]
    square_w, wide_w = weights[11:]
    hid1, first, state0, state1, state2, second, lat, value_in, gate_in = refs[:9]
    self_q, self_k, self_v, cross_q, text_k, text_v = refs[9:15]
    normed, entered, block1, block2, t1, t2, t3, att1, att2, inner, stream_in = refs[15:26]
    qkv1, qkv2, g_pixels, g_frames = refs[26:29], refs[29:32], refs[32], refs[33]
    q, vf, fold, tbias, alive = refs[34:39]
    columns, grad_in, output, small_out = refs[39:41], refs[41], refs[42], refs[43]
    landed, hop_land, small_land, g_second = refs[44:48]
    grads, refs = refs[48:60], refs[60:]
    (
        total, own, got_x, got_y, got2, got3, deal,
        send, recv, load_sem, free_x, free_y, free2_x, free2_y, free3, free_core,
        hop_send, hop_recv, small_send, small_recv, small_sem,
        col_sem, pair_sem, in_sem, out_sem, fetch_sem,
        win, weight_buf, pair, gs, acc, tmp, xb, low, stat, sums, vec,
    ) = refs
    comm = GradientSum(
        grads,
        landed,
        columns,
        (total, own, got_x, got_y, got2, got3, deal),
        (send, recv, load_sem),
        (free_x, free_y, free2_x, free2_y, free3, free_core),
    )
    tiny = SmallSum(comm, vec, small_out, small_land, tmp, small_send, small_recv, small_sem)
    greet(comm.peers())
    ring = Weights(weight_buf, col_sem)

    def part_of(slot, j):
        return weight_buf.at[slot, pl.ds(j * TILE, TILE)]

    frames = gs.shape[0] // PIX
    share = gs.shape[0] // 4

    def bring(pairs):
        copies = [
            pltpu.make_async_copy(src, dst, in_sem.at[i]) for i, (src, dst) in enumerate(pairs)
        ]
        for item in copies:
            item.start()
        for item in copies:
            item.wait()

    fetches = {}

    def fetch(key, *pairs):
        row = len(fetches)
        fetches[key] = [
            pltpu.make_async_copy(src, dst, fetch_sem.at[row, i])
            for i, (src, dst) in enumerate(pairs)
        ]
        for item in fetches[key]:
            item.start()

    def fetched(key):
        for item in fetches[key]:
            item.wait()

    def hop_rows(z):
        return pl.ds(pl.multiple_of(z * share, 16), share)

    def hop_copies(i):
        return [
            pltpu.make_async_remote_copy(
                src_ref=win.at[2, hop_rows(comm.heads[j])],
                dst_ref=hop_land.at[i, comm.h],
                send_sem=hop_send.at[i, j],
                recv_sem=hop_recv.at[i, j],
                device_id=(comm.c, comm.heads[j]),
                device_id_type=MESH,
            )
            for j in (1, 2, 3)
        ]

    def hop_own(i):
        src = win.at[2, hop_rows(comm.h)]
        return pltpu.make_async_copy(src, hop_land.at[i, comm.h], hop_send.at[i, 0])

    def hop_start(i):
        for item in hop_copies(i):
            item.start()
        hop_own(i).start()

    def hop_end(i, sink):
        for item in hop_copies(i):
            item.wait()
        hop_own(i).wait()
        bring([(hop_land.at[i, z], win.at[2, pl.ds(z * share, share)]) for z in range(4)])
        per = share // frames
        for f in range(frames):
            parts = [win[2, pl.ds(z * share + f * per, per), :] for z in range(4)]
            sink(f, slice(f * PIX, (f + 1) * PIX), jnp.concatenate(parts, axis=0).astype(F32))

    def stage_copy(i, slot, g):
        src = win.at[7 + slot, pl.ds(0, TILE)]
        return pltpu.make_async_copy(src, g.at[tile_at(i)], out_sem.at[slot])

    def outer_unit(a, b, g):
        count = g.shape[0] // TILE

        def body(i, carry):
            slot = i % 2

            @pl.when(i >= 2)
            def _():
                stage_copy(i - 2, slot, g).wait()

            tile = dot_f32(a[:, tile_at(i)], b[...], ((0,), (0,)))
            win[7 + slot, pl.ds(0, TILE), :] = tile.astype(BF)
            stage_copy(i, slot, g).start()
            return carry

        lax.fori_loop(0, count, body, 0)
        for i in (count - 2, count - 1):
            stage_copy(i, i % 2, g).wait()

    def leave_unit(w):
        vec[...] = jnp.zeros_like(vec)
        bring([(stream_in, win.at[0]), (g_pixels, win.at[1]), (t3, win.at[3])])
        fetch("output", (second, tmp))
        fetch("block2", (block2, xb))

        def sink(lanes, tile):
            win[2, :, lanes] = tile.astype(BF)

        ring.through(win.at[0], w, sink)
        hop_start(0)
        vec[12:13] = column_sum(win.at[1])

    def stream_unit(w):
        against_unit(win.at[1], w, gs)
        low[...] = gs[...].astype(BF)
        vec[11:12] = column_sum(low)
        acc[...] = jnp.zeros_like(acc)

    def wide_copy(i, slot, j):
        src = win.at[5 + 2 * slot + j, pl.ds(0, TILE)]
        return pltpu.make_async_copy(src, grads[10 + j].at[tile_at(i)], out_sem.at[2 * slot + j])

    def wide_unit(part, parts):
        count = wide_w.shape[1] // TILE
        per = count // parts
        start = part * per

        def tiles(i, slot):
            rows = tile_at(start + i)
            return [
                (wide_w.at[0, rows], part_of(slot, 0)),
                (wide_w.at[1, rows], part_of(slot, 1)),
                (inner.at[:, rows], pair.at[slot, 0]),
            ]

        def body(i, slot):
            tile = start + i
            to = tile % 2
            g = dot_f32(low[...], part_of(slot, 1)[...], ((1,), (1,)))
            inner_tile = pair[slot, 0].astype(F32)
            g = gelu_tanh_slope(inner_tile) * g
            g_low = g.astype(BF)
            rows = pl.ds(13 + tile // 5, 1)
            vec[rows, tile_at(tile % 5)] = jnp.sum(g_low.astype(F32), axis=0, keepdims=True)
            acc[...] += dot_f32(g_low, part_of(slot, 0)[...], ((1,), (0,)))

            @pl.when(tile >= 2)
            def _():
                wide_copy(tile - 2, to, 0).wait()
                wide_copy(tile - 2, to, 1).wait()

            up = dot_f32(g_low, win[3], ((0,), (0,)))
            win[5 + 2 * to, pl.ds(0, TILE), :] = up.astype(BF)
            wide_copy(tile, to, 0).start()
            down = dot_f32(gelu_tanh(inner_tile).astype(BF), low[...], ((0,), (0,)))
            win[6 + 2 * to, pl.ds(0, TILE), :] = down.astype(BF)
            wide_copy(tile, to, 1).start()

        stream(per, tiles, body, pair_sem, 2)
        if part == parts - 1:
            for tile in (count - 2, count - 1):
                wide_copy(tile, tile % 2, 0).wait()
                wide_copy(tile, tile % 2, 1).wait()

    def output_unit():
        fetched("output")

        def sink(f, rows, moved):
            result = alive[f : f + 1, 0:1] * (tmp[rows, :] + moved + vf[12:13])
            win[4, rows, :] = result.astype(BF)

        hop_end(0, sink)
        fetch("result", (win.at[4], output))
        fetch("att2", (att2, win.at[3]))
        fetch_heads("qkv2", qkv2)

    def fetch_heads(key, parts):
        fetch(key, *[(part, win.at[i]) for i, part in enumerate(parts)])

    def motion_norm_unit(state, gain, bias):
        if state == "block1":
            fetch("att1", (att1, win.at[3]))
        fetched(state)
        norm_back_rows(acc, xb, vf, gain, gs, vec)
        low[...] = gs[...].astype(BF)
        vec[bias : bias + 1] = column_sum(low)

    def motion_out_unit(att, wo, w):
        fetched(att)
        outer_unit(win.at[3], low, grads[wo])
        against_unit(low, w, win.at[6])

    def motion_attend_unit(qkv, t, state):
        fetched(qkv)
        if qkv == "qkv2":
            fetched("result")
        attend_back_body(
            True,
            win.at[0],
            win.at[1],
            win.at[2],
            tbias,
            win.at[6],
            win.at[3],
            win.at[4],
            win.at[5],
            tmp,
            acc,
            xb,
        )
        fetch(t, ({"t1": t1, "t2": t2}[t], win.at[6]))
        fetch(state, ({"block1": block1, "entered": entered}[state], xb))
        if qkv == "qkv2":
            fetch_heads("qkv1", qkv1)
        else:
            fetch("normed", (normed, win.at[0]))

    def motion_outer_unit(t, i, g):
        if i == 0:
            fetched(t)
        outer_unit(win.at[3 + i], win.at[6], g)

    def entry_unit():
        fetch("second", (second, xb))
        fetched("normed")
        outer_unit(win.at[0], low, grads[0])

    def entry_back_unit(w):
        against_unit(low, w, win.at[2])
        hop_start(1)
        fetch("frames", (g_frames, low))

    def second_unit():
        def sink(f, rows, moved):
            acc[rows, :] = moved

        hop_end(1, sink)
        fetched("second")
        fetched("frames")

        def put(rows, dx):
            gs[rows, :] = low[rows, :].astype(F32) + dx

        group_back(acc, xb, vf, 0, False, fold, stat, sums, put, vec)
        low[...] = gs[...].astype(BF)
        fetch("kept", (gs, g_second))
        tiny.first()

    def against_unit(x, w, out):
        def sink(lanes, tile):
            out[:, lanes] = tile.astype(out.dtype)

        ring.against(x, w, sink)

    def start_unit(w):
        fetch("state2", (state2, xb))
        rows = pl.ds(0, text_k.shape[0])
        fetch(
            "cross",
            (cross_q, win.at[0]),
            (text_k, win.at[1, rows]),
            (text_v, win.at[2, rows]),
        )
        fetched("kept")
        against_unit(low, w, gs)
        low[...] = gs[...].astype(BF)
        acc[...] = jnp.zeros_like(acc)

    def ffn_unit(part, parts):
        per = value_w.shape[1] // TILE // parts
        start = part * per

        def tiles(i, slot):
            rows = tile_at(start + i)
            return [
                (value_w.at[0, rows], part_of(slot, 0)),
                (gate_w.at[0, rows], part_of(slot, 1)),
                (down_w.at[0, rows], part_of(slot, 2)),
                (value_in.at[:, rows], pair.at[slot, 0]),
                (gate_in.at[:, rows], pair.at[slot, 1]),
            ]

        def body(i, slot):
            g = dot_f32(low[...], part_of(slot, 2)[...], ((1,), (1,)))
            value, gate = pair[slot, 0].astype(F32), pair[slot, 1].astype(F32)
            phi = 0.5 * (1.0 + lax.erf(gate * math.sqrt(0.5)))
            density = jnp.exp(-0.5 * gate * gate) * (1.0 / math.sqrt(2.0 * math.pi))
            g_value = (gate * phi * g).astype(BF)
            g_gate = (value * (phi + gate * density) * g).astype(BF)
            acc[...] += dot_f32(g_value, part_of(slot, 0)[...], ((1,), (0,)))
            acc[...] += dot_f32(g_gate, part_of(slot, 1)[...], ((1,), (0,)))

        stream(per, tiles, body, pair_sem, 2)

    def norm_unit(state, gain):
        fetched(state)
        norm_back_rows(acc, xb, q, gain, gs)
        low[...] = gs[...].astype(BF)
        if state == "state2":
            fetch("state1", (state1, xb))
        if state == "state0":
            fetch("first", (first, xb), (g_second, gs))

    def cross_unit():
        rows = text_k.shape[0]
        keys, values = win.at[1, pl.ds(0, rows)], win.at[2, pl.ds(0, rows)]
        fetched("cross")
        attend_back_body(False, win.at[0], keys, values, text_mask, win.at[6], win.at[3], tmp)
        fetch_heads("self", (self_q, self_k, self_v))

    def self_unit():
        fetched("self")
        attend_back_body(
            True,
            win.at[0],
            win.at[1],
            win.at[2],
            spatial_mask,
            win.at[6],
            win.at[3],
            win.at[4],
            win.at[5],
            tmp,
            acc,
            xb,
        )
        fetch("state0", (state0, xb))

    def through_unit(x, w, fresh):
        def sink(lanes, tile):
            if fresh:
                acc[:, lanes] = tile
            else:
                acc[:, lanes] += tile

        ring.through(x, w, sink)

    def first_unit():
        fetched("first")

        def sink(rows, dx):
            gs[rows, :] = gs[rows, :] + dx

        group_back(acc, xb, q, 7, False, fold, stat, sums, sink)
        fetch("hid1", (hid1, xb))
        fetch("lat", (lat, low))

    def hid_unit():
        fetched("hid1")

        def sink(rows, dx):
            tmp[rows, :] = dx

        group_back(acc, xb, q, 4, True, fold, stat, sums, sink)

    def last_unit():
        fetched("lat")

        def sink(rows, dx):
            low[rows, :] = (gs[rows, :] + dx).astype(BF)

        group_back(acc, low, q, 0, True, fold, stat, sums, sink)
        bring([(low, grad_in)])

    def windows_unit(x):
        make_windows(x, win, True)

    def conv_unit(w, tap):
        def sink(lanes, tile):
            if tap == 0:
                acc[:, lanes] = tile
            else:
                acc[:, lanes] += tile

        ring.against(win.at[tap], w, sink)

    P_ = functools.partial
    def nothing():
        pass

    ready = [0] * CHUNKS
    def square(i):
        return ring.add(square_w.at[AT[i]])

    units = [P_(leave_unit, square(2)), P_(outer_unit, win.at[0], win.at[1], grads[2])]
    units += [P_(stream_unit, square(2))]
    units += [P_(wide_unit, i, 10) for i in range(10)]
    ready[0:4] = [len(units)] * 4
    after_wide = ring.add(square_w.at[AT[6]], fresh=True)
    units += [P_(ring.begin, after_wide), output_unit, P_(motion_norm_unit, "block2", 9, 8)]
    done = {2: 0}
    for state, t, qkv, att, wo, wq, gain, bias in (
        ("block1", "t2", "qkv2", "att2", 6, 7, 6, 5),
        ("entered", "t1", "qkv1", "att1", 1, 3, 3, 2),
    ):
        units += [P_(motion_out_unit, att, wo, after_wide if wo == 6 else square(wo))]
        done[wo] = len(units)
        units += [P_(motion_attend_unit, qkv, t, state)]
        units += [P_(through_unit, win.at[3 + i], square(wq + i), i == 0) for i in range(3)]
        for i in range(3):
            units += [P_(motion_outer_unit, t, i, grads[wq + i])]
            done[wq + i] = len(units)
        units += [P_(motion_norm_unit, state, gain, bias)]
    units += [entry_unit]
    done[0] = len(units)
    for k, (one, other) in enumerate(PAIRS):
        ready[4 + k] = max(done[one], done[other])
    units += [P_(entry_back_unit, square(0)), nothing, nothing, nothing, nothing, second_unit]
    units += [P_(start_unit, ring.add(out_w.at[0]))]
    units += [P_(ffn_unit, i, 10) for i in range(10)]
    after_ffn = ring.add(cross_o.at[0], fresh=True)
    units += [P_(ring.begin, after_ffn), tiny.second, P_(norm_unit, "state2", 16)]
    units += [P_(against_unit, low, after_ffn, win.at[6]), cross_unit]
    units += [P_(through_unit, win.at[3], ring.add(cross_w.at[0]), True)]
    units += [P_(norm_unit, "state1", 13), tiny.last]
    units += [P_(against_unit, low, ring.add(self_o.at[0]), win.at[6]), self_unit]
    units += [P_(through_unit, win.at[3 + i], ring.add(qkv_w.at[i]), i == 0) for i in range(3)]
    units += [P_(norm_unit, "state0", 10)]
    units += [P_(against_unit, low, ring.add(in_w.at[0]), acc), first_unit]
    units += [P_(windows_unit, gs)]
    units += [P_(conv_unit, ring.add(conv2.at[t]), t) for t in range(9)]
    units += [hid_unit, P_(windows_unit, tmp)]
    units += [P_(conv_unit, ring.add(conv1.at[t]), t) for t in range(9)]
    units += [last_unit]
    comm.run(units, ready)


def backward_fused(frozen, trained, saved, motion, lat, g_pixels, g_frames, q, vf, tbias, alive):
    tokens = lat.shape[0]
    weights = [frozen[i] for i in (1, 2, 3, 4, 5, 6, 8, 9, 10, 11, 12)] + list(trained)
    kept = list(saved[:6]) + [lat, saved[12], saved[13]] + list(saved[6:12])
    kept += list(motion) + [g_pixels, g_frames]
    fold = group_matrix()
    any_spec, vmem = pl.BlockSpec(memory_space=pl.ANY), pl.BlockSpec(memory_space=pltpu.VMEM)
    dma, count = pltpu.SemaphoreType.DMA, pltpu.SemaphoreType.REGULAR

    def array(shape, dtype=BF):
        return jax.ShapeDtypeStruct(shape, dtype)

    outs = pl.pallas_call(
        functools.partial(backward_kernel, len(weights)),
        out_shape=(
            array((10, 320, HD)),
            array((2, C, HD)),
            array((tokens, C)),
            array((tokens, C)),
            array((SMALL_ROWS, C), F32),
            array((LANDED, 2, 4, 160, C)),
            array((2, 4, tokens // 4, C)),
            array((11 * SMALL_ROWS, C), F32),
            array((tokens, C), F32),
        )
        + (array((C, C)),) * 10
        + (array((4 * C, C)),) * 2,
        in_specs=[any_spec] * (len(weights) + len(kept)) + [vmem] * 5,
        out_specs=(any_spec,) * 4 + (vmem,) + (any_spec,) * 16,
        scratch_shapes=[
            pltpu.VMEM((3, 2, 4, 160, C), BF),
            pltpu.VMEM((2, 4, 160, C), BF),
            pltpu.VMEM((2, 2, 4, 80, C), BF),
            pltpu.VMEM((2, 4, 160, C), BF),
            pltpu.VMEM((4, 4, 80, C), BF),
            pltpu.VMEM((2, 3, 80, C), BF),
            pltpu.VMEM((2, 8, 80, HD), BF),
            dma((CHUNKS, 20)),
            dma((CHUNKS, 20)),
            dma((CHUNKS, 10)),
            count,
            count,
            count,
            count,
            count((3,)),
            count,
            dma((2, 4)),
            dma((2, 4)),
            dma((11,)),
            dma((11,)),
            dma((7,)),
            dma((2,)),
            dma((2, 5)),
            dma((4,)),
            dma((4,)),
            dma((32, 3)),
            pltpu.VMEM((9, tokens, C), BF),
            pltpu.VMEM((2, C, C), BF),
            pltpu.VMEM((2, 2, tokens, TILE), BF),
            pltpu.VMEM((tokens, C), F32),
            pltpu.VMEM((tokens, C), F32),
            pltpu.VMEM((tokens, C), F32),
            pltpu.VMEM((tokens, C), F32),
            pltpu.VMEM((tokens, C), BF),
            pltpu.VMEM((2, 8, C), F32),
            pltpu.VMEM((2, 8, C), F32),
            pltpu.VMEM((SMALL_ROWS, C), F32),
        ],
        compiler_params=pltpu.CompilerParams(
            collective_id=3, has_side_effects=True, vmem_limit_bytes=62 << 20
        ),
    )(*weights, *kept, jnp.pad(q, ((0, 4), (0, 0))), vf, fold, tbias, alive)
    square, wide, grad_in, output, small = outs[:5]
    return output, grad_in, square.astype(F32), wide.astype(F32), small


def forward_plain(frozen, x0, Q, time_in, text, geglu_bias, spatial_bias, cross_bias):
    time_w, conv1_w, conv2_w, in_w, self_w, self_o, cross_qw, cross_w, cross_o = frozen[:9]
    ffn_value, ffn_gate, ffn_down, out_w = frozen[9:]
    geglu_f = lax.all_gather(geglu_bias, "head", axis=1, tiled=True)

    def flat(x):
        return x.reshape(-1, C)

    act1 = silu(gn(x0, gn_stats(x0), Q[0], Q[1])).astype(BF)
    hid1 = (conv(act1, conv1_w) + through(time_in, time_w[0]) + Q[2] + Q[3]).reshape(x0.shape)
    act2 = silu(gn(hid1, gn_stats(hid1), Q[4], Q[5])).astype(BF)
    first = x0 + conv(act2, conv2_w).reshape(x0.shape) + Q[6]
    spatial_in = flat(gn(first, gn_stats(first), Q[7], Q[8]).astype(BF))
    state0 = through(spatial_in, in_w[0]) + Q[9]
    norm1 = ln(state0, ln_stats(state0), Q[10], Q[11]).astype(BF)
    self_q, self_k, self_v = (against(norm1, self_w[i]).astype(BF) for i in range(3))
    self_att = attend(self_q, self_k, self_v, spatial_bias)
    state1 = state0 + through(self_att, self_o[0]) + Q[12]
    norm2 = ln(state1, ln_stats(state1), Q[13], Q[14]).astype(BF)
    cross_q = against(norm2, cross_qw[0]).astype(BF)
    text_k, text_v = (against(text, cross_w[i]).astype(BF) for i in (0, 1))
    cross_att = attend(cross_q, text_k, text_v, cross_bias)
    state2 = state1 + through(cross_att, cross_o[0]) + Q[15]
    norm3 = ln(state2, ln_stats(state2), Q[16], Q[17]).astype(BF)
    value_in = (against(norm3, ffn_value[0]) + geglu_f[0]).astype(BF)
    gate_in = (against(norm3, ffn_gate[0]) + geglu_f[1]).astype(BF)
    mixed = (value_in.astype(F32) * gelu_erf(gate_in.astype(F32))).astype(BF)
    state3 = (state2 + through(mixed, ffn_down[0]) + Q[18]).astype(BF)
    second = flat(first) + through(state3, out_w[0]) + Q[19]
    states = (flat(hid1), flat(first), state0, state1, state2, second)
    return states + (self_q, self_k, self_v, cross_q, text_k, text_v, value_in, gate_in)


def motion_plain(trained, second, vector_f, bias_f, codes, temporal_bias, to_pixels):
    square_w, ffn_w = trained
    normed = to_pixels(gn(second, gn_stats(second), vector_f[0], vector_f[1]).astype(BF))
    entered = through(normed, square_w[0]) + vector_f[2]

    def temporal_in(x, gain_row, wq):
        t = ln(x, ln_stats(x), vector_f[gain_row], vector_f[gain_row + 1]) + codes
        t = t.astype(BF)
        return t, [against(t, square_w[wq + i]).astype(BF) for i in range(3)]

    t1, qkv1 = temporal_in(entered, 3, 3)
    att1 = attend(*qkv1, temporal_bias)
    block1 = entered + through(att1, square_w[1]) + vector_f[5]
    t2, qkv2 = temporal_in(block1, 6, 7)
    att2 = attend(*qkv2, temporal_bias)
    block2 = block1 + through(att2, square_w[6]) + vector_f[8]
    t3 = ln(block2, ln_stats(block2), vector_f[9], vector_f[10]).astype(BF)
    inner = against(t3, ffn_w[0]) + bias_f
    spread = gelu_tanh(inner).astype(BF)
    stream = (block2 + through(spread, ffn_w[1]) + vector_f[11]).astype(BF)
    motion = (normed, entered, block1, block2, t1, t2, t3, att1, att2, inner.astype(BF), stream)
    return motion + tuple(qkv1) + tuple(qkv2)


def motion_back_plain(
    trained, motion, g_out, grad_out, second, vector_f, temporal_bias, to_frames
):
    square_w, ffn_w = trained
    normed, entered, block1, block2, t1, t2, t3, att1, att2, inner, stream = motion[:11]
    qkv1, qkv2 = motion[11:14], motion[14:17]
    spread = gelu_tanh(inner.astype(F32)).astype(BF)
    tl1, tl2, tl3 = ln_stats(entered), ln_stats(block1), ln_stats(block2)
    stats3 = gn_stats(second)
    col = lambda v: jnp.sum(v.astype(F32), axis=0)
    G = {}
    G[2] = outer(stream, g_out)
    grad_stream = against(g_out, square_w[2])
    g_ffn = grad_stream.astype(BF)
    grad_down = outer(spread, g_ffn)
    g_inner = (gelu_tanh_slope(inner.astype(F32)) * against(g_ffn, ffn_w[1])).astype(BF)
    grad_up = outer(g_inner, t3)
    grad_t3 = through(g_inner, ffn_w[0])
    grad_b2 = grad_stream + ln_back(grad_t3, block2, tl3, vector_f[9])
    dgain3, dshift3 = ln_param_grads(grad_t3, block2, tl3)

    def temporal_back(grad, x, stats, t, qkv, att, gain_row, wo, wq):
        low = grad.astype(BF)
        G[wo] = outer(att, low)
        dqkv = attend_back(*qkv, temporal_bias, against(low, square_w[wo]).astype(BF))
        for i in range(3):
            G[wq + i] = outer(dqkv[i], t)
        grad_t = sum(through(dqkv[i], square_w[wq + i]) for i in range(3))
        grad_x = grad + ln_back(grad_t, x, stats, vector_f[gain_row])
        return grad_x, ln_param_grads(grad_t, x, stats), col(low)

    grad_b1, (dgain2, dshift2), dbias2 = temporal_back(
        grad_b2, block1, tl2, t2, qkv2, att2, 6, 6, 7
    )
    grad_e, (dgain1, dshift1), dbias1 = temporal_back(
        grad_b1, entered, tl1, t1, qkv1, att1, 3, 1, 3
    )
    g_entry = grad_e.astype(BF)
    G[0] = outer(normed, g_entry)
    grad_normed = to_frames(against(g_entry, square_w[0]).astype(BF)).astype(F32).reshape(second.shape)
    z = (second - stats3[0]) * stats3[1]
    dgain0 = jnp.sum(grad_normed * z, axis=(0, 1))
    dshift0 = jnp.sum(grad_normed, axis=(0, 1))
    grad_second = grad_out + gn_back(grad_normed, second, stats3, vector_f[0])

    grad_vector = jnp.stack(
        [
            dgain0,
            dshift0,
            col(g_entry),
            dgain1,
            dshift1,
            dbias1,
            dgain2,
            dshift2,
            dbias2,
            dgain3,
            dshift3,
            col(g_ffn),
            col(g_out),
        ]
    )
    fill = jnp.zeros((SMALL_ROWS - 17, C), F32)
    small = jnp.concatenate([grad_vector, col(g_inner).reshape(4, C), fill])
    return [G[i] for i in range(10)], [grad_up, grad_down], small, grad_second


def backward_plain(frozen, saved, x0, Q, grad_second, spatial_bias, cross_bias):
    time_w, conv1_w, conv2_w, in_w, self_w, self_o, cross_qw, cross_w, cross_o = frozen[:9]
    ffn_value, ffn_gate, ffn_down, out_w = frozen[9:]
    hid1, first, state0, state1, state2 = saved[:5]
    self_q, self_k, self_v, cross_q, text_k, text_v, value_in, gate_in = saved[6:]
    hid1, first = hid1.reshape(x0.shape), first.reshape(x0.shape)
    value_in, gate_in = value_in.astype(F32), gate_in.astype(F32)

    def flat(x):
        return x.reshape(-1, C)

    def framed(x):
        return x.reshape(x0.shape)

    stats0, stats1, stats2 = gn_stats(x0), gn_stats(hid1), gn_stats(first)
    sl1, sl2, sl3 = ln_stats(state0), ln_stats(state1), ln_stats(state2)
    g_po = flat(grad_second).astype(BF)
    grad_s3 = against(g_po, out_w[0])
    g_fb = grad_s3.astype(BF)
    grad_mixed = against(g_fb, ffn_down[0])
    g_value = (gelu_exact(gate_in) * grad_mixed).astype(BF)
    g_gate = (value_in * gelu_exact_slope(gate_in) * grad_mixed).astype(BF)
    grad_n3 = through(g_value, ffn_value[0]) + through(g_gate, ffn_gate[0])
    grad_s2 = grad_s3 + ln_back(grad_n3, state2, sl3, Q[16])
    g_cb = grad_s2.astype(BF)
    (g_cq,) = attend_back(
        cross_q, text_k, text_v, cross_bias, against(g_cb, cross_o[0]).astype(BF), False
    )
    grad_s1 = grad_s2 + ln_back(through(g_cq, cross_qw[0]), state1, sl2, Q[13])
    g_sb = grad_s1.astype(BF)
    dself = attend_back(
        self_q, self_k, self_v, spatial_bias, against(g_sb, self_o[0]).astype(BF)
    )
    grad_n1 = sum(through(dself[i], self_w[i]) for i in range(3))
    grad_s0 = grad_s1 + ln_back(grad_n1, state0, sl1, Q[10])
    g_pi = grad_s0.astype(BF)
    grad_gn = framed(against(g_pi, in_w[0]))
    grad_first = grad_second + gn_back(grad_gn, first, stats2, Q[7])

    grad_act2 = framed(conv_back(grad_first.astype(BF), conv2_w))
    grad_n = silu_back(grad_act2, gn(hid1, stats1, Q[4], Q[5]))
    grad_hid1 = gn_back(grad_n, hid1, stats1, Q[4])
    grad_act1 = framed(conv_back(grad_hid1.astype(BF), conv1_w))
    grad_n = silu_back(grad_act1, gn(x0, stats0, Q[0], Q[1]))
    return (grad_first + gn_back(grad_n, x0, stats0, Q[0])).astype(BF)


def update_kernel(step_rate, weight, moment, average, gradient, *outs):
    parts = update(weight[...], moment[...], average[...], gradient[...].astype(F32), step_rate)
    for out, part in zip(outs, parts):
        out[...] = part


def update_turned(weight, moment, average, gradient, step_rate):
    n, r, k = weight.shape
    block = min(r, 640)
    spec = pl.BlockSpec((1, k, block), lambda i, j: (i, 0, j))
    turned = [jnp.swapaxes(a, 1, 2) for a in (weight, moment, average, gradient.astype(BF))]
    parts = pl.pallas_call(
        functools.partial(update_kernel, step_rate),
        grid=(n, r // block),
        out_shape=(jax.ShapeDtypeStruct((n, k, r), F32),) * 3,
        in_specs=[spec] * 4,
        out_specs=(spec,) * 3,
        compiler_params=pltpu.CompilerParams(vmem_limit_bytes=40 << 20),
    )(*turned)
    return tuple(jnp.swapaxes(part, 1, 2) for part in parts)


def per_device(
    sizes,
    latents,
    cotangent,
    frames,
    timesteps,
    text,
    conv_weight,
    time_weight,
    frozen_params,
    spatial_square,
    cross_kv,
    spatial_ffn,
    geglu_bias,
    projections,
    feedforward,
    up_bias,
    vectors,
    projections_moment,
    feedforward_moment,
    up_bias_moment,
    vectors_moment,
    projections_average,
    feedforward_average,
    up_bias_average,
    vectors_average,
):
    Q = frozen_params
    n_head = sizes[1]
    head_index = lax.axis_index("head")
    clip_index = lax.axis_index("clip")
    own_frames = latents.shape[1]
    tokens = own_frames * PIX
    own_pixels = PIX // n_head
    columns = FMAX * own_pixels

    def framed(x):
        return x.reshape(own_frames, PIX, C)

    def flat(x):
        return x.reshape(tokens, C)

    def to_pixels(x):
        x = lax.all_to_all(framed(x), "head", 1, 0, tiled=True)
        return x.reshape(columns, C)

    def to_frames(x):
        x = lax.all_to_all(x.reshape(FMAX, own_pixels, C), "head", 0, 1, tiled=True)
        return x.reshape(tokens, C)

    frame_of = jnp.arange(tokens) // PIX
    spatial_bias = jnp.where(frame_of[:, None] == frame_of[None, :], 0.0, MASK_FILL).astype(F32)
    column = jnp.arange(columns)
    same_pixel = (column % own_pixels)[:, None] == (column % own_pixels)[None, :]
    key_there = (column // own_pixels)[None, :] < frames[0]
    temporal_bias = jnp.where(same_pixel & key_there, 0.0, MASK_FILL).astype(F32)
    text_len = text.shape[1]
    text_rows = 128
    cross_bias = jnp.broadcast_to(
        jnp.where(jnp.arange(text_rows)[None, :] < text_len, 0.0, MASK_FILL), (tokens, text_rows)
    ).astype(F32)
    own_frame = head_index * own_frames + jnp.arange(own_frames)
    frame_mask = (own_frame < frames[0]).astype(F32)[:, None, None]

    x0 = latents[0].astype(F32)
    grad_out = frame_mask * cotangent[0].astype(F32)
    arrays = frozen_arrays(conv_weight, time_weight, spatial_square, cross_kv, spatial_ffn)
    time_in = jax.nn.silu(time_table(timesteps)).astype(BF)
    text_pad = jnp.pad(text[0], ((0, text_rows - text_len), (0, 0)))
    if sizes == (8, 4):
        lat = latents.reshape(tokens, C)
        g_frames = flat(grad_out.astype(BF))
        frozen, trained, saved, motion, g_out, vector_f = forward_fused(
            arrays,
            projections,
            feedforward,
            vectors,
            up_bias,
            lat,
            g_frames,
            Q,
            time_in,
            text_pad,
            geglu_bias,
            temporal_bias,
        )
        alive = jnp.pad(frame_mask[:, :, 0], ((0, 8 - own_frames), (0, 127)))
        output, input_gradient, own_square, own_wide, small = backward_fused(
            frozen, trained, saved, motion, lat, g_out, g_frames, Q, vector_f, temporal_bias, alive
        )
        output, input_gradient = framed(output)[None], framed(input_gradient)[None]
    else:
        small = pack_small(vectors, up_bias)
        frozen, trained, small = gather_plain(arrays, small, projections, feedforward)
        vector_f, bias_f = unpack_small(sizes, small, vectors, up_bias)
        saved = forward_plain(
            frozen, x0, Q, time_in, text_pad, geglu_bias, spatial_bias, cross_bias
        )
        second = framed(saved[5])
        codes = jnp.repeat(frame_table(), own_pixels, axis=0)
        motion = motion_plain(
            trained, second, vector_f, bias_f, codes, temporal_bias, to_pixels
        )
        g_out = to_pixels(grad_out.astype(BF))
        moved = to_frames(through(motion[10], trained[0][2]).astype(BF)).astype(F32)
        output = (frame_mask * (second + framed(moved) + vector_f[12])).astype(BF)[None]
        parts, wide_parts, small, grad_second = motion_back_plain(
            trained, motion, g_out, grad_out, second, vector_f, temporal_bias, to_frames
        )
        own_square, own_wide, small = sum_plain(parts, wide_parts, small)
        input_gradient = backward_plain(
            frozen, saved, x0, Q, grad_second, spatial_bias, cross_bias
        )[None]
    k = vectors.shape[1]
    own_vector = lax.dynamic_slice_in_dim(small[:13], clip_index * k, k, 1)
    own_bias = lax.dynamic_slice(
        small[13:17].reshape(-1, 128),
        (head_index * up_bias.shape[0], clip_index * up_bias.shape[1]),
        up_bias.shape,
    )

    square_parts = update_turned(
        projections, projections_moment, projections_average, own_square, RATE_MATRIX
    )
    ffn_parts = update_turned(
        feedforward, feedforward_moment, feedforward_average, own_wide, RATE_MATRIX)
    bias_parts = update(up_bias, up_bias_moment, up_bias_average, own_bias, RATE_VECTOR)
    vector_parts = update(vectors, vectors_moment, vectors_average, own_vector, RATE_VECTOR)
    return (output, input_gradient) + square_parts + ffn_parts + bias_parts + vector_parts


def solution(mesh):
    sizes = (mesh.shape["clip"], mesh.shape["head"])
    return jax.shard_map(
        functools.partial(per_device, sizes),
        mesh=mesh,
        in_specs=(
            P("clip", "head", None, None),
            P("clip", "head", None, None),
            P("clip"),
            P("clip"),
            P("clip", None, None),
            P(None, None, "head", None),
            P("head", None),
            P(),
            P(None, "head", None),
            P(None, "head", None),
            P(None, "head", None),
            P(None, "head"),
            P(None, "head", "clip"),
            P(None, "head", "clip"),
            P("head", "clip"),
            P(None, "clip"),
            P(None, "head", "clip"),
            P(None, "head", "clip"),
            P("head", "clip"),
            P(None, "clip"),
            P(None, "head", "clip"),
            P(None, "head", "clip"),
            P("head", "clip"),
            P(None, "clip"),
        ),
        out_specs=(
            P("clip", "head", None, None),
            P("clip", "head", None, None),
            P(None, "head", "clip"),
            P(None, "head", "clip"),
            P(None, "head", "clip"),
            P(None, "head", "clip"),
            P(None, "head", "clip"),
            P(None, "head", "clip"),
            P("head", "clip"),
            P("head", "clip"),
            P("head", "clip"),
            P(None, "clip"),
            P(None, "clip"),
            P(None, "clip"),
        ),
        check_vma=False,
    )
```
